128 devices in a mesh: section: 2 (over core), edata: 4 (over y), expert: 16 (over x, z).
Axes of the slice: x: 4, y: 4, z: 4, core: 2. Of those that a mesh axis runs over, the one named last changes fastest.
Arguments:
- hidden_in: bfloat16 [2, 8192, 2048], P('section', ('edata', 'expert')), may hold values from -6 to 6
- out_grad: bfloat16 [2, 8192, 2048], P('section', ('edata', 'expert')), may hold values from -16 to 16
- routes: int32 [2, 8192, 8], P('section', ('edata', 'expert')), may hold values from 0 to 15, all different within a row; in each aligned block of 128 rows (0 to 127, 128 to 255, ..., all dimensions but the last counted through in order) at most 72 rows name the same one
- gates: float32 [2, 8192, 8], P('section', ('edata', 'expert')), may hold values from 0.05 to 0.5
- w_gate_up: bfloat16 [2, 16, 2048, 1536], P('section', 'expert'), may hold values from -0.125 to 0.125
- w_down: bfloat16 [2, 16, 768, 2048], P('section', 'expert'), may hold values from -0.21875 to 0.21875
Outputs:
- upstream_grad: bfloat16 [2, 8192, 2048], P('section', ('edata', 'expert'))
- gate_up_grad: bfloat16 [2, 16, 2048, 1536], P('section', 'expert', 'edata')
- down_grad: bfloat16 [2, 16, 768, 2048], P('section', 'expert', None, 'edata')
The draws below stay inside these ranges and needn't reach their ends.
Inputs may be any that keep to these rules, and one draw needn't show every extreme that they name: `routes`: the 8 experts of a token are distinct. In the 128 tokens of one device no expert is chosen more than 72 times, a bound that some block reaches.
All inputs are finite; a program needn't handle non-finite values.
Results may differ from the reference program's by a relative error of at most 0.0058.
Values may be sent and summed in bfloat16 or wider, within the bound.
No kernel may reach another device: no remote copies, remote signals or barrier semaphores. Data moves between devices by JAX's collectives and lax.ppermute only.
A program may use at most 192 MiB of HBM per device.

```python
import math
import jax
import jax.numpy as jnp
import numpy as np
from jax import lax

D = 2048
FF = 768
TOK_DEV = 128
SECTIONS = 2
EXPERTS = 16
TOPK = 8
CAP = 72
TOKENS = 8192
N_EDATA = 4
N_EXPERT = 16


def with_spikes(result, rng, source, target, shards_of, factor):
    owner, partner = [(jnp.arange(result.shape[dim]) // (result.shape[dim] // shards_of)).reshape([-1 if axis == dim else 1 for axis in range(result.ndim)]) for dim in (source, target)]
    chosen = jax.random.permutation(rng, shards_of)[partner]
    strong = (owner == chosen) | (owner == (partner + shards_of // 2) % shards_of)
    return jnp.where(strong, factor * result, result)


def block_scale(key, dims, cuts, least, top_value):
    gain = 1.0
    for axis_at, blocks in cuts:
        draws = jax.random.uniform(jax.random.fold_in(jax.random.fold_in(key, 6), axis_at), (blocks,), jnp.float32, least / len(cuts), top_value / len(cuts))
        gain = gain * jnp.repeat(jnp.exp(draws), dims[axis_at] // blocks).reshape((-1,) + (1,) * (len(dims) - 1 - axis_at))
    return gain


def routed_block(own_key, own, number, rows, number_of, top, bound, slope):
    order = jax.random.permutation(own_key, number_of)
    crowded, common = portions_of(number_of, rows * top, bound, slope, True), portions_of(number_of, rows * top, bound, slope, False)
    places = jnp.arange(number_of)

    def named(tallies, rotation):
        used = int((tallies > 0).sum())
        fixed = max(1, used // 4)
        shifted = fixed + (places - fixed + rotation * (used - fixed)) % max(1, number_of - fixed)
        return jnp.zeros((number_of,), jnp.int32).at[order[jnp.where(places < fixed, places, shifted)]].set(jnp.asarray(tallies, jnp.int32))

    tallies = jnp.where(number % 4 == 0, named(crowded, number // 4), named(common, number - number // 4 - 1))
    mixed = jax.random.permutation(jax.random.fold_in(own, 3), number_of)
    donor, sink = mixed[0:number_of // 2 * 2:2], mixed[1:number_of // 2 * 2:2]
    margin = jnp.minimum(tallies[donor] - 1, bound - tallies[sink]) // 2
    margin = jnp.where((donor == order[0]) | (sink == order[0]) | (tallies[sink] == 0), 0, jnp.maximum(margin, 0))
    shifted = jax.random.randint(jax.random.fold_in(own, 4), (number_of // 2,), 0, 1 << 20) % (margin + 1)
    tallies = tallies.at[donor].add(-shifted).at[sink].add(shifted)
    labels = jnp.searchsorted(jnp.cumsum(tallies), jnp.arange(rows * top), side="right").astype(jnp.int32)
    listing = labels.reshape(top, rows).T
    listing = listing[jax.random.permutation(jax.random.fold_in(own, 1), rows)]
    rotation = jax.random.randint(jax.random.fold_in(own, 2), (rows, 1), 0, top)
    return jnp.take_along_axis(listing, (jnp.arange(top)[None, :] + rotation) % top, axis=1)


def portions_of(number_of, total, bound, slope, full):
    portions = [(1 << 20) // math.isqrt(rank ** slope) + 1 for rank in range(1, number_of + 1)]
    largest = bound if full else min(bound, max(-(-total // number_of), total * portions[0] // sum(portions)))
    least = 1 if total - largest >= number_of - 1 else 0
    counts, spare = [largest] + [least] * (number_of - 1), total - largest - least * (number_of - 1)
    while spare > 0:
        candidates = [i for i in range(1, number_of) if counts[i] < largest] or [i for i in range(1, number_of) if counts[i] < bound]
        whole, remaining = sum([portions[i] for i in candidates]), spare
        for i in candidates:
            more = min(bound - counts[i], max(1, remaining * portions[i] // whole), spare)
            counts[i] = counts[i] + more
            spare = spare - more
    return np.array(counts)


def normal_values(rng, dims, deviation, bound, cuts=(), kind=jnp.bfloat16):
    values = deviation * jax.random.normal(rng, dims, jnp.float32)
    if cuts:
        values = values * block_scale(rng, dims, cuts, -0.22, 0.18)
    return jnp.clip(values, -bound, bound).astype(kind)


def bell_draw_with(own_key, extent, width, limit, cuts, heavy, kind=jnp.bfloat16):
    drawn = width * jax.random.normal(own_key, extent, jnp.float32)
    if cuts:
        drawn = drawn * block_scale(own_key, extent, cuts, -0.22, 0.18)
    return jnp.clip(with_spikes(drawn, jax.random.fold_in(own_key, 3), *heavy), -limit, limit).astype(kind)


def setup_inputs(seed: int = 0) -> dict:
    seeds = jax.random.split(jax.random.key(seed), 7)
    hidden_in = normal_values(seeds[0], (SECTIONS, TOKENS, D), 1.0, 6.0, ((0, 2), (1, 64)))
    out_grad = bell_draw_with(seeds[1], (SECTIONS, TOKENS, D), 1.0, 16.0, ((0, 2), (1, 64)), (1, 2, 64, 4.0))
    routes_keys = jax.random.split(jax.random.fold_in(seeds[2], 1), SECTIONS * TOKENS // TOK_DEV)
    routes_turns = jax.random.permutation(jax.random.fold_in(seeds[2], 3), SECTIONS * TOKENS // TOK_DEV)
    routes = jax.vmap(lambda own, number: routed_block(jax.random.fold_in(seeds[2], 2), own, number, TOK_DEV, EXPERTS, TOPK, CAP, 2))(routes_keys, routes_turns).reshape((SECTIONS, TOKENS, TOPK))
    gates = jnp.clip(jnp.exp(math.log(0.5) - 2.3025851 * jax.random.uniform(seeds[3], (SECTIONS, TOKENS, TOPK), jnp.float32) ** block_scale(seeds[3], (SECTIONS, TOKENS, TOPK), ((0, 2), (1, 64)), -0.2, 0.2)), 0.05, 0.5)
    w_gate_up = normal_values(seeds[4], (SECTIONS, EXPERTS, D, 2 * FF), D ** -0.5, 0.125, ((0, 2), (1, 16)))
    w_down = normal_values(seeds[5], (SECTIONS, EXPERTS, FF, D), FF ** -0.5, 0.21875, ((0, 2), (1, 16)))
    return {"hidden_in": hidden_in, "out_grad": out_grad, "routes": routes, "gates": gates, "w_gate_up": w_gate_up, "w_down": w_down}


def expert_pass(xrows, srows, wgu, wdown):
    ab = jnp.dot(xrows, wgu, preferred_element_type=jnp.float32)
    first = ab[:, :FF]
    second = ab[:, FF:]
    sig = jax.nn.sigmoid(first)
    hrows = (first * sig * second).astype(jnp.bfloat16)
    dh = jnp.dot(srows, wdown.T, preferred_element_type=jnp.float32)
    dfirst = dh * second * sig * (1.0 + first * (1.0 - sig))
    dsecond = dh * first * sig
    dab = jnp.concatenate([dfirst, dsecond], axis=1).astype(jnp.bfloat16)
    slot_grad = jnp.dot(dab, wgu.T, preferred_element_type=jnp.float32).astype(jnp.bfloat16)
    term_gu = jnp.dot(xrows.T, dab, preferred_element_type=jnp.float32)
    term_down = jnp.dot(hrows.T, srows, preferred_element_type=jnp.float32)
    return slot_grad, term_gu, term_down


def reference(hidden_in, out_grad, routes, gates, w_gate_up, w_down):
    group = TOK_DEV * N_EXPERT
    block = TOK_DEV * TOPK
    slots = group * TOPK
    layer_grads = []
    gu_grads = []
    down_grads = []
    for section_id in range(SECTIONS):
        gu_total = jnp.zeros((EXPERTS, D, 2 * FF), jnp.float32)
        down_total = jnp.zeros((EXPERTS, FF, D), jnp.float32)
        pieces = []
        for group_id in range(N_EDATA):
            first_tok = group_id * group
            xtok = hidden_in[section_id, first_tok:first_tok + group]
            gtok = out_grad[section_id, first_tok:first_tok + group]
            chosen = routes[section_id, first_tok:first_tok + group].reshape(N_EXPERT, block).astype(jnp.int32)
            onehot = (chosen[:, :, None] == jnp.arange(EXPERTS, dtype=jnp.int32)[None, None, :]).astype(jnp.int32)
            before = jnp.cumsum(onehot, axis=1).astype(jnp.int32) - onehot
            place = jnp.sum(before * onehot, axis=2).astype(jnp.int32)
            source = jnp.arange(N_EXPERT, dtype=jnp.int32)[:, None]
            dest = (chosen * (N_EXPERT * CAP) + source * CAP + place).reshape(-1).astype(jnp.int32)
            table = jnp.full((EXPERTS * N_EXPERT * CAP,), slots, jnp.int32)
            table = table.at[dest].set(jnp.arange(slots, dtype=jnp.int32)).reshape(EXPERTS, N_EXPERT * CAP)
            scaled = (gates[section_id, first_tok:first_tok + group][:, :, None] * gtok[:, None, :].astype(jnp.float32)).astype(jnp.bfloat16)
            scaled_pad = jnp.concatenate([scaled.reshape(slots, D), jnp.zeros((1, D), jnp.bfloat16)], axis=0)
            x_pad = jnp.concatenate([xtok, jnp.zeros((1, D), jnp.bfloat16)], axis=0)

            def per_expert(packed):
                wgu, wdown, index = packed
                xrows = x_pad[index // TOPK]
                srows = scaled_pad[index]
                return expert_pass(xrows, srows, wgu, wdown)

            slot_rows, term_gu, term_down = lax.map(per_expert, (w_gate_up[section_id], w_down[section_id], table))
            gu_total = gu_total + term_gu
            down_total = down_total + term_down
            values = jnp.zeros((slots + 1, D), jnp.bfloat16).at[table.reshape(-1)].set(slot_rows.reshape(-1, D))
            summed = jnp.sum(values[:slots].reshape(group, TOPK, D).astype(jnp.float32), axis=1)
            pieces.append((gtok.astype(jnp.float32) + summed).astype(jnp.bfloat16))
        layer_grads.append(jnp.concatenate(pieces, axis=0))
        gu_grads.append(gu_total.astype(jnp.bfloat16))
        down_grads.append(down_total.astype(jnp.bfloat16))
    layer_grad = jnp.stack(layer_grads, axis=0)
    upstream_grad = jnp.roll(layer_grad, -1, axis=0)
    return upstream_grad, jnp.stack(gu_grads, axis=0), jnp.stack(down_grads, axis=0)
```

```python
import functools

import jax
import jax.numpy as jnp
from jax import lax
from jax.experimental import pallas as pl
from jax.experimental.pallas import tpu as pltpu
from jax.sharding import PartitionSpec as P

BF16 = jnp.bfloat16
F32 = jnp.float32
OFF = (0, 1, 3, 2)
SIDE = 4
LANES = 128
VMEM_LIMIT = 56 * 1024 * 1024


def params(steps):
    return pltpu.CompilerParams(
        vmem_limit_bytes=VMEM_LIMIT, dimension_semantics=("arbitrary",) * steps
    )


def cost(flops, moved):
    return pl.CostEstimate(flops=int(flops), bytes_accessed=int(moved), transcendentals=0)


def moved_along(block, axis, distance):
    if axis == "edata" or axis == "section":
        size = lax.axis_size(axis)
        return lax.ppermute(block, axis, [(i, (i + distance) % size) for i in range(size)])
    pairs = []
    for a in range(SIDE):
        for b in range(SIDE):
            if axis == "x":
                pairs.append((a * SIDE + b, (a + distance) % SIDE * SIDE + b))
            else:
                pairs.append((a * SIDE + b, a * SIDE + (b + distance) % SIDE))
    return lax.ppermute(block, "expert", pairs)


def iota(shape, dim):
    return lax.broadcasted_iota(jnp.int32, shape, dim)


def dot(a, b, da=1, db=0):
    return lax.dot_general(a, b, (((da,), (db,)), ((), ())), preferred_element_type=F32)


def prep_kernel(experts, routes_ref, gates_ref, x_ref, g_ref, xe_ref, ge_ref):
    tok, width = x_ref.shape
    topk = routes_ref.shape[1]
    lane = iota((tok, LANES), 1)
    expert = lax.rem(lane, experts)
    full = jnp.zeros((tok, LANES), F32)
    for k in range(topk):
        full += jnp.where(routes_ref[:, k : k + 1] == expert, gates_ref[:, k : k + 1], 0.0)
    high = full.astype(BF16).astype(F32)
    rest = full - high
    middle = rest.astype(BF16).astype(F32)
    low = rest - middle
    piece = jnp.where(lane < 2 * experts, middle, jnp.where(lane < 3 * experts, low, 0.0))
    piece = jnp.where(lane < experts, high, piece).astype(BF16)
    for src, dst in ((x_ref, xe_ref), (g_ref, ge_ref)):
        dst[:, :width] = src[...]
        dst[:, width:] = piece


def prep(routes, gates, x, g, experts):
    tok, width = x.shape
    shape = jax.ShapeDtypeStruct((tok, width + LANES), BF16)
    return pl.pallas_call(
        functools.partial(prep_kernel, experts),
        out_shape=(shape, shape),
        compiler_params=params(0),
        name="prep",
    )(routes, gates, x, g)


def pair_table(eids_ref, piece, experts, cap, lanes):
    rows = piece.shape[0]
    tok = rows // 2
    r, c = iota((rows, rows), 0), iota((rows, rows), 1)
    lower = jnp.where((c < r) & ((c >= tok) == (r >= tok)), 1.0, 0.0).astype(BF16)
    lane = iota((rows, LANES), 1)
    mask = jnp.where((lane < experts) & (piece.astype(F32) > 0.0), 1.0, 0.0)
    before = dot(lower, mask.astype(BF16))
    slot = iota((rows, lanes), 1)
    second = jnp.where(iota((rows, 1), 0) >= tok, cap, 0)
    table = jnp.zeros((rows, lanes), F32)
    for j in range(SIDE):
        here = lane == eids_ref[j]
        named = jnp.sum(jnp.where(here, mask, 0.0), axis=1, keepdims=True)
        place = jnp.sum(jnp.where(here, before, 0.0), axis=1, keepdims=True)
        target = jnp.where(named > 0.0, place.astype(jnp.int32) + second + 2 * cap * j, -1)
        table += jnp.where(slot == target, 1.0, 0.0)
    return table


def pack_kernel(scale, experts, cap, eids_ref, *refs):
    blocks, tails, outs = refs[:4], refs[4:8], refs[8:12]
    table_ref, gate_ref = refs[12:]
    pair = 2 * cap
    total = SIDE * pair
    lanes = -(-total // LANES) * LANES

    @pl.when(pl.program_id(0) == 0)
    def _():
        for p in range(2):
            piece = jnp.concatenate([tails[2 * p][...], tails[2 * p + 1][...]], axis=0)
            table = pair_table(eids_ref, piece, experts, cap, lanes).T[:total].astype(BF16)
            table_ref[p] = table
            if scale:
                packed = dot(table, piece)
                row = iota((total, LANES), 0)
                lane = iota((total, LANES), 1)
                want = jnp.full((total, LANES), eids_ref[0], jnp.int32)
                for j in range(1, SIDE):
                    want = jnp.where(row >= j * pair, eids_ref[j], want)
                mine = (lax.rem(lane, experts) == want) & (lane < 3 * experts)
                gate_ref[p] = jnp.sum(jnp.where(mine, packed, 0.0), axis=1, keepdims=True)

    for p in range(2):
        rows = jnp.concatenate([blocks[2 * p][...], blocks[2 * p + 1][...]], axis=0)
        packed = dot(table_ref[p], rows)
        if scale:
            packed = packed * gate_ref[p]
        packed = packed.astype(BF16)
        for j in range(SIDE):
            outs[j][p * pair : (p + 1) * pair, :] = packed[j * pair : (j + 1) * pair]


def pack(eids, blocks, width, experts, cap, scale):
    tok = blocks[0].shape[0]
    step = 512
    pair = 2 * cap
    last = width // LANES
    out = jax.ShapeDtypeStruct((2 * pair, width), BF16)
    return pl.pallas_call(
        functools.partial(pack_kernel, scale, experts, cap),
        grid=(width // step,),
        in_specs=[pl.BlockSpec(memory_space=pltpu.SMEM)]
        + [pl.BlockSpec((tok, step), lambda i: (0, i))] * 4
        + [pl.BlockSpec((tok, LANES), lambda i: (0, last))] * 4,
        out_specs=[pl.BlockSpec((2 * pair, step), lambda i: (0, i))] * 4,
        out_shape=[out] * 4,
        scratch_shapes=[
            pltpu.VMEM((2, SIDE * pair, 2 * tok), BF16),
            pltpu.VMEM((2, SIDE * pair, 1), F32),
        ],
        compiler_params=params(1),
        cost_estimate=cost(4 * SIDE * pair * 2 * tok * width, 8 * pair * width * 4),
        name="pack_scaled" if scale else "pack_rows",
    )(eids, *blocks, *blocks)


def unpack_kernel(experts, cap, eids_ref, *refs):
    tails, rets, outs = refs[:4], refs[4:8], refs[8:12]
    table_ref = refs[12]
    tok = tails[0].shape[0]
    pair = 2 * cap
    lanes = table_ref.shape[2]
    fill = lanes - SIDE * pair

    @pl.when(pl.program_id(0) == 0)
    def _():
        for p in range(2):
            piece = jnp.concatenate([tails[2 * p][...], tails[2 * p + 1][...]], axis=0)
            table_ref[p] = pair_table(eids_ref, piece, experts, cap, lanes).astype(BF16)

    for p in range(2):
        parts = [rets[j][p * pair : (p + 1) * pair, :] for j in range(SIDE)]
        parts.append(jnp.zeros((fill, rets[0].shape[1]), BF16))
        dense = dot(table_ref[p], jnp.concatenate(parts, axis=0))
        for s in range(2):
            outs[2 * p + s][...] = dense[s * tok : (s + 1) * tok].astype(outs[2 * p + s].dtype)


def unpack(eids, blocks, rets, width, experts, cap):
    tok = blocks[0].shape[0]
    pair = 2 * cap
    lanes = -(-SIDE * pair // LANES) * LANES
    cols = rets[0].shape[1]
    step = 512
    last = width // LANES
    return pl.pallas_call(
        functools.partial(unpack_kernel, experts, cap),
        grid=(cols // step,),
        in_specs=[pl.BlockSpec(memory_space=pltpu.SMEM)]
        + [pl.BlockSpec((tok, LANES), lambda i: (0, last))] * 4
        + [pl.BlockSpec((2 * pair, step), lambda i: (0, i))] * 4,
        out_specs=[pl.BlockSpec((tok, step), lambda i: (0, i))] * 4,
        out_shape=[jax.ShapeDtypeStruct((tok, cols), F32)]
        + [jax.ShapeDtypeStruct((tok, cols), BF16)] * 3,
        scratch_shapes=[pltpu.VMEM((2, 2 * tok, lanes), BF16)],
        compiler_params=params(1),
        cost_estimate=cost(4 * SIDE * pair * 2 * tok * cols, 8 * pair * cols * 2),
        name="unpack",
    )(eids, *blocks, *rets)


def up_kernel(count, *refs):
    xs, (wa, wb), outs = refs[:count], refs[count : count + 2], refs[count + 2 :]
    for i in range(count):
        rows = xs[i][...]
        a = dot(rows, wa[...])
        b = dot(rows, wb[...])
        sig = jax.nn.sigmoid(a)
        outs[3 * i][...] = a * sig * b
        outs[3 * i + 1][...] = b * sig * (1.0 + a * (1.0 - sig))
        outs[3 * i + 2][...] = a * sig


def up(xs, wgu):
    count = len(xs)
    rows, width = xs[0].shape
    hidden = wgu.shape[1] // 2
    step = 256
    steps = hidden // step
    out = jax.ShapeDtypeStruct((rows, hidden), F32)
    flat = pl.pallas_call(
        functools.partial(up_kernel, count),
        grid=(steps,),
        in_specs=[pl.BlockSpec((rows, width), lambda i: (0, 0))] * count
        + [
            pl.BlockSpec((width, step), lambda i: (0, i)),
            pl.BlockSpec((width, step), lambda i: (0, i + steps)),
        ],
        out_specs=[pl.BlockSpec((rows, step), lambda i: (0, i))] * (3 * count),
        out_shape=[out] * (3 * count),
        compiler_params=params(1),
        cost_estimate=cost(
            4 * count * rows * width * hidden,
            2 * count * rows * width + 4 * width * hidden + 12 * count * rows * hidden,
        ),
        name="up",
    )(*xs, wgu, wgu)
    return [flat[3 * i : 3 * i + 3] for i in range(count)]


def dh_kernel(count, *refs):
    ss, wd, outs = refs[:count], refs[count], refs[count + 1 :]
    for i in range(count):
        outs[i][...] = dot(ss[i][...], wd[...], 1, 1)


def dh_of(ss, wdown):
    count = len(ss)
    rows, width = ss[0].shape
    hidden = wdown.shape[0]
    step = 256
    return pl.pallas_call(
        functools.partial(dh_kernel, count),
        grid=(hidden // step,),
        in_specs=[pl.BlockSpec((rows, width), lambda i: (0, 0))] * count
        + [pl.BlockSpec((step, width), lambda i: (i, 0))],
        out_specs=[pl.BlockSpec((rows, step), lambda i: (0, i))] * count,
        out_shape=[jax.ShapeDtypeStruct((rows, hidden), F32)] * count,
        compiler_params=params(1),
        cost_estimate=cost(
            2 * count * rows * width * hidden,
            2 * count * rows * width + 2 * width * hidden + 4 * count * rows * hidden,
        ),
        name="dh",
    )(*ss, wdown)


def crossed(refs, j, cap):
    return jnp.concatenate([ref[j * cap : (j + 1) * cap, :] for ref in refs], axis=0)


def keep_quarter(step, part, own, first_up, first_down, wait_up, wait_down):
    half = part.shape[0] // 2

    @pl.when(step == 0)
    def _():
        first_up[:half, :] = part[:half].astype(BF16)
        first_down[half:, :] = part[half:].astype(BF16)

    @pl.when(step == 1)
    def _():
        wait_up[...] = part[:half]
        first_up[half:, :] = part[half:].astype(BF16)

    @pl.when(step == 2)
    def _():
        first_down[:half, :] = part[:half].astype(BF16)
        wait_down[...] = part[half:]

    @pl.when(step == 3)
    def _():
        own[...] = part


STEPS = (2, 1, 3, 0)


def quarter_of(step, place_ref):
    ahead = jnp.where(step == 0, 2, jnp.where(step == 1, 1, jnp.where(step == 2, 3, 0)))
    return lax.rem(place_ref[0] + ahead, SIDE)


def quarter_outs(shape):
    rows, cols = shape
    shapes = [
        ((rows, cols), F32),
        ((rows, cols), BF16),
        ((rows, cols), BF16),
        ((rows // 2, cols), F32),
        ((rows // 2, cols), F32),
    ]
    return (
        [jax.ShapeDtypeStruct(s, t) for s, t in shapes],
        [pl.BlockSpec(s, lambda i, place: (0, 0)) for s, t in shapes],
    )


def down_kernel(cap, place_ref, *refs):
    hs, ss, outs, turned = refs[:4], refs[4:8], refs[8:13], refs[13]
    step = pl.program_id(0)

    @pl.when(step == 0)
    def _():
        rows = jnp.concatenate([crossed(hs, j, cap) for j in range(SIDE)], axis=0)
        turned[...] = rows.T.astype(BF16)

    rows = jnp.concatenate([s[...] for s in ss], axis=0)
    keep_quarter(step, dot(turned[...], rows), *outs)


def down_parts(place, hs, ss, cap):
    rows, hidden = hs[0].shape
    width = ss[0].shape[1]
    quarter = width // SIDE
    shapes, specs = quarter_outs((hidden, quarter))
    return pl.pallas_call(
        functools.partial(down_kernel, cap),
        grid_spec=pltpu.PrefetchScalarGridSpec(
            num_scalar_prefetch=1,
            grid=(SIDE,),
            in_specs=[pl.BlockSpec((rows, hidden), lambda i, place: (0, 0))] * 4
            + [pl.BlockSpec((rows, quarter), lambda i, place: (0, quarter_of(i, place)))] * 4,
            out_specs=specs,
            scratch_shapes=[pltpu.VMEM((hidden, SIDE * rows), BF16)],
        ),
        out_shape=shapes,
        compiler_params=params(1),
        cost_estimate=cost(8 * rows * width * hidden, 16 * rows * hidden + 8 * rows * width),
        name="down_parts",
    )(place, *hs, *ss)


def dab_kernel(cap, *refs):
    cas, cbs, dhs, outs = refs[:4], refs[4:8], refs[8:12], refs[12:]
    for i in range(SIDE):
        hidden = dhs[0].shape[1]
        dh = crossed(dhs, i, cap)
        outs[i][:, :hidden] = (dh * cas[i][...]).astype(BF16)
        outs[i][:, hidden:] = (dh * cbs[i][...]).astype(BF16)


def dab_of(cas, cbs, dhs, cap):
    rows, hidden = dhs[0].shape
    return pl.pallas_call(
        functools.partial(dab_kernel, cap),
        out_shape=[jax.ShapeDtypeStruct((rows, 2 * hidden), BF16)] * 4,
        compiler_params=params(0),
        cost_estimate=cost(8 * rows * hidden, 16 * rows * hidden * 4),
        name="dab",
    )(*cas, *cbs, *dhs)


def gate_up_kernel(place_ref, *refs):
    xs, ds, outs = refs[:4], refs[4:8], refs[8:13]
    total = dot(xs[0][...], ds[0][...], 0, 0)
    for i in range(1, SIDE):
        total += dot(xs[i][...], ds[i][...], 0, 0)
    keep_quarter(pl.program_id(0), total, *outs)


def gate_up_parts(place, xs, ds):
    rows, width = xs[0].shape
    both = ds[0].shape[1]
    quarter = width // SIDE
    shapes, specs = quarter_outs((quarter, both))
    return pl.pallas_call(
        gate_up_kernel,
        grid_spec=pltpu.PrefetchScalarGridSpec(
            num_scalar_prefetch=1,
            grid=(SIDE,),
            in_specs=[pl.BlockSpec((rows, quarter), lambda i, place: (0, quarter_of(i, place)))] * 4
            + [pl.BlockSpec((rows, both), lambda i, place: (0, 0))] * 4,
            out_specs=specs,
        ),
        out_shape=shapes,
        compiler_params=params(1),
        cost_estimate=cost(8 * rows * width * both, 8 * rows * (width + both)),
        name="gate_up_parts",
    )(place, *xs, *ds)


def slot_body(cap, cross, *refs):
    ds, w, outs = refs[:4], refs[4], refs[5:9]
    if not cross:
        for i in range(SIDE):
            outs[i][...] = dot(ds[i][...], w[...], 1, 1).astype(BF16)
        return
    parts = [dot(ds[i][...], w[...], 1, 1) for i in range(SIDE)]
    for j in range(SIDE):
        rows = [part[j * cap : (j + 1) * cap] for part in parts]
        outs[j][...] = jnp.concatenate(rows, axis=0).astype(BF16)


def slot_rows(ds, wgu, first, cols, cap, cross):
    rows, both = ds[0].shape
    step = 512
    base = first // step
    return pl.pallas_call(
        functools.partial(slot_body, cap, cross),
        grid=(cols // step,),
        in_specs=[pl.BlockSpec((rows, both), lambda i: (0, 0))] * 4
        + [pl.BlockSpec((step, both), lambda i: (base + i, 0))],
        out_specs=[pl.BlockSpec((rows, step), lambda i: (0, i))] * 4,
        out_shape=[jax.ShapeDtypeStruct((rows, cols), BF16)] * 4,
        compiler_params=params(1),
        cost_estimate=cost(8 * rows * both * cols, 8 * rows * (both + cols) + 2 * both * cols),
        name="slot_rows",
    )(*ds, wgu)


def around(first, axis):
    return [first] + [moved_along(first, axis, OFF[b]) for b in range(1, SIDE)]


def spread(outs, axis):
    near = [moved_along(outs[j], axis, OFF[j]) for j in (1, 2)]
    far, n0, n1 = lax.optimization_barrier((outs[3], near[0], near[1]))
    return [outs[0], n0, n1, moved_along(far, axis, OFF[3])]


def ring_sum(own, first_up, first_down, wait_up, wait_down):
    half = wait_up.shape[0]
    up1 = moved_along(first_up, "edata", 1)
    down1 = moved_along(first_down, "edata", -1)
    second_up = (wait_up + up1[:half].astype(F32)).astype(BF16)
    second_down = (wait_down + down1[half:].astype(F32)).astype(BF16)
    up2 = moved_along(second_up, "edata", 1)
    down2 = moved_along(second_down, "edata", -1)
    upper = own[:half] + down1[:half].astype(F32) + up2.astype(F32)
    lower = own[half:] + up1[half:].astype(F32) + down2.astype(F32)
    return jnp.concatenate([upper, lower], axis=0).astype(BF16)


def body(hidden_in, out_grad, routes, gates, w_gate_up, w_down):
    tok = hidden_in.shape[1]
    width = hidden_in.shape[2]
    topk = routes.shape[2]
    experts = lax.axis_size("expert")
    cap = min(tok, tok * topk * 9 // (8 * experts))
    half = width // 2
    wgu, wdown = w_gate_up[0, 0], w_down[0, 0]
    me = lax.axis_index("expert")
    mx, mz = me // SIDE, me % SIDE
    off = jnp.array(OFF, jnp.int32)
    eids_x = (mx * SIDE + (mz + off) % SIDE).astype(jnp.int32)
    eids_g = ((mx + off) % SIDE * SIDE + mz).astype(jnp.int32)
    place = lax.axis_index("edata").astype(jnp.int32).reshape(1)

    xe, ge = prep(routes[0], gates[0], hidden_in[0], out_grad[0], experts)
    xblocks = around(xe, "x")
    gblocks = around(ge, "z")
    xs = spread(pack(eids_x, xblocks, width, experts, cap, False), "z")
    ss = spread(pack(eids_g, gblocks, width, experts, cap, True), "x")

    ups = up(xs[:3], wgu) + up(xs[3:], wgu)
    dhs = dh_of(ss[:3], wdown) + dh_of(ss[3:], wdown)
    hs, cas, cbs = ([u[k] for u in ups] for k in range(3))
    down = down_parts(place, hs, ss, cap)
    ds = dab_of(cas, cbs, dhs, cap)
    gate_up = gate_up_parts(place, xs, ds)

    left = slot_rows(ds, wgu, 0, half, cap, False)
    right = slot_rows(ds, wgu, half, half, cap, True)
    back_l = [left[0]] + [moved_along(left[j], "z", -OFF[j]) for j in range(1, SIDE)]
    back_r = [right[0]] + [moved_along(right[j], "x", -OFF[j]) for j in range(1, SIDE)]
    home_l = unpack(eids_x, xblocks, back_l, width, experts, cap)
    home_r = unpack(eids_g, gblocks, back_r, width, experts, cap)
    sums = []
    for parts, axis in ((home_l, "x"), (home_r, "z")):
        total = parts[0]
        for b in range(1, SIDE):
            total = total + moved_along(parts[b], axis, -OFF[b]).astype(F32)
        sums.append(total)
    layer = (out_grad[0].astype(F32) + jnp.concatenate(sums, axis=1)).astype(BF16)
    upstream = moved_along(layer, "section", -1)

    down_grad = ring_sum(*down)
    gate_up_grad = ring_sum(*gate_up)
    return (upstream[None], gate_up_grad[None, None], down_grad[None, None])


def solution(mesh):
    return jax.shard_map(
        body,
        mesh=mesh,
        in_specs=(
            P("section", ("edata", "expert"), None),
            P("section", ("edata", "expert"), None),
            P("section", ("edata", "expert"), None),
            P("section", ("edata", "expert"), None),
            P("section", "expert", None, None),
            P("section", "expert", None, None),
        ),
        out_specs=(
            P("section", ("edata", "expert"), None),
            P("section", "expert", "edata", None),
            P("section", "expert", None, "edata"),
        ),
        check_vma=False,
    )
```

```python
import functools

import jax
import jax.numpy as jnp
from jax import lax
from jax.experimental import pallas as pl
from jax.experimental.pallas import tpu as pltpu
from jax.sharding import PartitionSpec as P

BF16 = jnp.bfloat16
F32 = jnp.float32
OFF = (0, 1, 3, 2)
SIDE = 4
LANES = 128
MIB = 1024 * 1024


def params(steps, limit):
    return pltpu.CompilerParams(
        vmem_limit_bytes=limit * MIB, dimension_semantics=("arbitrary",) * steps
    )


def held(shape, index):
    return pl.BlockSpec(shape, index, pipeline_mode=pl.Buffered(1))


def cost(flops, moved):
    return pl.CostEstimate(flops=int(flops), bytes_accessed=int(moved), transcendentals=0)


def moved_along(block, axis, distance):
    if axis == "edata" or axis == "section":
        size = lax.axis_size(axis)
        return lax.ppermute(block, axis, [(i, (i + distance) % size) for i in range(size)])
    pairs = []
    for a in range(SIDE):
        for b in range(SIDE):
            if axis == "x":
                pairs.append((a * SIDE + b, (a + distance) % SIDE * SIDE + b))
            else:
                pairs.append((a * SIDE + b, a * SIDE + (b + distance) % SIDE))
    return lax.ppermute(block, "expert", pairs)


def iota(shape, dim):
    return lax.broadcasted_iota(jnp.int32, shape, dim)


def dot(a, b, da=1, db=0):
    return lax.dot_general(a, b, (((da,), (db,)), ((), ())), preferred_element_type=F32)


def prep_kernel(experts, routes_ref, gates_ref, x_ref, g_ref, xe_ref, ge_ref):
    tok, width = x_ref.shape
    topk = routes_ref.shape[0]
    expert = lax.rem(iota((LANES, tok), 0), experts)
    full = jnp.zeros((LANES, tok), F32)
    for k in range(topk):
        full += jnp.where(routes_ref[k : k + 1, :] == expert, gates_ref[k : k + 1, :], 0.0)
    full = full.T
    lane = iota((tok, LANES), 1)
    high = full.astype(BF16).astype(F32)
    rest = full - high
    middle = rest.astype(BF16).astype(F32)
    low = rest - middle
    piece = jnp.where(lane < 2 * experts, middle, jnp.where(lane < 3 * experts, low, 0.0))
    piece = jnp.where(lane < experts, high, piece).astype(BF16)
    for src, dst in ((x_ref, xe_ref), (g_ref, ge_ref)):
        dst[:, :width] = src[...]
        dst[:, width:] = piece


def prep(routes, gates, x, g, experts):
    tok, width = x.shape
    shape = jax.ShapeDtypeStruct((tok, width + LANES), BF16)
    return pl.pallas_call(
        functools.partial(prep_kernel, experts),
        out_shape=(shape, shape),
        compiler_params=params(0, 8),
        name="prep",
    )(routes, gates, x, g)


def places(piece, experts, blocks):
    rows = piece.shape[0]
    tok = rows // blocks
    r, c = iota((rows, rows), 0), iota((rows, rows), 1)
    upto = jnp.where((c <= r) & (lax.div(c, tok) == lax.div(r, tok)), 1.0, 0.0).astype(BF16)
    lane = iota((rows, LANES), 1)
    mask = jnp.where((lane < experts) & (piece.astype(F32) > 0.0), 1.0, 0.0)
    return (dot(upto, mask.astype(BF16)) * mask).astype(BF16)


def pack_kernel(scale, experts, cap, eids_ref, *refs):
    blocks, tails, outs = refs[:4], refs[4:8], refs[8:12]
    table_ref, gate_ref = refs[12:]
    pair = 2 * cap
    total = SIDE * pair
    tok = tails[0].shape[0]

    @pl.when(pl.program_id(0) == 0)
    def _():
        row = iota((total, LANES), 0)
        lane = iota((total, LANES), 1)
        want = jnp.full((total, LANES), eids_ref[0], jnp.int32)
        for j in range(1, SIDE):
            want = jnp.where(row >= j * pair, eids_ref[j], want)
        choose = jnp.where(lane == want, 1.0, 0.0).astype(BF16)
        mine = (lax.rem(lane, experts) == want) & (lane < 3 * experts)
        slot = lax.rem(iota((total, 2 * tok), 0), pair)
        place = slot + 1 - jnp.where(iota((total, 2 * tok), 1) >= tok, cap, 0)
        place = jnp.where(place > 0, place, -1).astype(F32)
        for p in range(2):
            piece = jnp.concatenate([tails[2 * p][...], tails[2 * p + 1][...]], axis=0)
            found = dot(choose, places(piece, experts, 2), 1, 1)
            table = jnp.where(found == place, 1.0, 0.0).astype(BF16)
            table_ref[p] = table
            if scale:
                packed = dot(table, piece)
                gate_ref[p] = jnp.sum(jnp.where(mine, packed, 0.0), axis=1, keepdims=True)

    for p in range(2):
        rows = jnp.concatenate([blocks[2 * p][...], blocks[2 * p + 1][...]], axis=0)
        packed = dot(table_ref[p], rows)
        if scale:
            packed = packed * gate_ref[p]
        packed = packed.astype(BF16)
        for j in range(SIDE):
            outs[j][p * pair : (p + 1) * pair, :] = packed[j * pair : (j + 1) * pair]


def pack(eids, blocks, width, experts, cap, scale):
    tok = blocks[0].shape[0]
    step = 512
    pair = 2 * cap
    last = width // LANES
    out = jax.ShapeDtypeStruct((2 * pair, width), BF16)
    return pl.pallas_call(
        functools.partial(pack_kernel, scale, experts, cap),
        grid=(width // step,),
        in_specs=[pl.BlockSpec(memory_space=pltpu.SMEM)]
        + [pl.BlockSpec((tok, step), lambda i: (0, i))] * 4
        + [held((tok, LANES), lambda i: (0, last))] * 4,
        out_specs=[pl.BlockSpec((2 * pair, step), lambda i: (0, i))] * 4,
        out_shape=[out] * 4,
        scratch_shapes=[
            pltpu.VMEM((2, SIDE * pair, 2 * tok), BF16),
            pltpu.VMEM((2, SIDE * pair, 1), F32),
        ],
        compiler_params=params(1, 20),
        cost_estimate=cost(4 * SIDE * pair * 2 * tok * width, 8 * pair * width * 4),
        name="pack_scaled" if scale else "pack_rows",
    )(eids, *blocks, *blocks)


def home_kernel(experts, cap, tail_ref, rows_ref, grad_ref, out_ref, table_ref):
    tok = tail_ref.shape[0]
    total = experts * cap

    @pl.when(pl.program_id(0) == 0)
    def _():
        choose = jnp.where(iota((LANES, total), 0) == lax.div(iota((LANES, total), 1), cap), 1.0, 0.0)
        found = dot(places(tail_ref[...], experts, 1), choose.astype(BF16))
        place = lax.rem(iota((tok, total), 1), cap) + 1
        table_ref[...] = jnp.where(found == place.astype(F32), 1.0, 0.0).astype(BF16)

    total_grad = dot(table_ref[...], rows_ref[...]) + grad_ref[...].astype(F32)
    out_ref[...] = total_grad.astype(BF16)


def home(ge, rows, grad, experts, cap):
    tok, width = grad.shape
    step = 512
    last = width // LANES
    total = experts * cap
    return pl.pallas_call(
        functools.partial(home_kernel, experts, cap),
        grid=(width // step,),
        in_specs=[
            held((tok, LANES), lambda i: (0, last)),
            pl.BlockSpec((total, step), lambda i: (0, i)),
            pl.BlockSpec((tok, step), lambda i: (0, i)),
        ],
        out_specs=pl.BlockSpec((tok, step), lambda i: (0, i)),
        out_shape=jax.ShapeDtypeStruct((tok, width), BF16),
        scratch_shapes=[pltpu.VMEM((tok, total), BF16)],
        compiler_params=params(1, 16),
        cost_estimate=cost(2 * tok * total * width, 2 * total * width + 4 * tok * width),
        name="home",
    )(ge, rows, grad)


def up_kernel(count, *refs):
    xs, (wa, wb), outs = refs[:count], refs[count : count + 2], refs[count + 2 :]
    for i in range(count):
        rows = xs[i][...]
        a = dot(rows, wa[...])
        b = dot(rows, wb[...])
        sig = jax.nn.sigmoid(a)
        outs[3 * i][...] = a * sig * b
        outs[3 * i + 1][...] = b * sig * (1.0 + a * (1.0 - sig))
        outs[3 * i + 2][...] = a * sig


def up(xs, wgu):
    count = len(xs)
    rows, width = xs[0].shape
    hidden = wgu.shape[1] // 2
    step = 256
    steps = hidden // step
    out = jax.ShapeDtypeStruct((rows, hidden), F32)
    flat = pl.pallas_call(
        functools.partial(up_kernel, count),
        grid=(steps,),
        in_specs=[held((rows, width), lambda i: (0, 0))] * count
        + [
            pl.BlockSpec((width, step), lambda i: (0, i)),
            pl.BlockSpec((width, step), lambda i: (0, i + steps)),
        ],
        out_specs=[pl.BlockSpec((rows, step), lambda i: (0, i))] * (3 * count),
        out_shape=[out] * (3 * count),
        compiler_params=params(1, 22),
        cost_estimate=cost(
            4 * count * rows * width * hidden,
            2 * count * rows * width + 4 * width * hidden + 12 * count * rows * hidden,
        ),
        name="up",
    )(*xs, wgu, wgu)
    return [flat[3 * i : 3 * i + 3] for i in range(count)]


def dh_kernel(count, *refs):
    ss, wd, outs = refs[:count], refs[count], refs[count + 1 :]
    for i in range(count):
        outs[i][...] = dot(ss[i][...], wd[...], 1, 1)


def dh_of(ss, wdown):
    count = len(ss)
    rows, width = ss[0].shape
    hidden = wdown.shape[0]
    step = 256
    return pl.pallas_call(
        functools.partial(dh_kernel, count),
        grid=(hidden // step,),
        in_specs=[held((rows, width), lambda i: (0, 0))] * count
        + [pl.BlockSpec((step, width), lambda i: (i, 0))],
        out_specs=[pl.BlockSpec((rows, step), lambda i: (0, i))] * count,
        out_shape=[jax.ShapeDtypeStruct((rows, hidden), F32)] * count,
        compiler_params=params(1, 16),
        cost_estimate=cost(
            2 * count * rows * width * hidden,
            2 * count * rows * width + 2 * width * hidden + 4 * count * rows * hidden,
        ),
        name="dh",
    )(*ss, wdown)


def crossed(parts, j, cap):
    return jnp.concatenate([part[j * cap : (j + 1) * cap, :] for part in parts], axis=0)


def turn_kernel(cap, *refs):
    hs, out = refs[:4], refs[4]
    rows = jnp.concatenate([crossed(hs, j, cap) for j in range(SIDE)], axis=0)
    out[...] = rows.T.astype(BF16)


def turned(hs, cap):
    rows, hidden = hs[0].shape
    step = 256
    return pl.pallas_call(
        functools.partial(turn_kernel, cap),
        grid=(hidden // step,),
        in_specs=[pl.BlockSpec((rows, step), lambda i: (0, i))] * 4,
        out_specs=pl.BlockSpec((step, SIDE * rows), lambda i: (i, 0)),
        out_shape=jax.ShapeDtypeStruct((hidden, SIDE * rows), BF16),
        compiler_params=params(1, 16),
        cost_estimate=cost(8 * rows * hidden, 24 * rows * hidden),
        name="turned",
    )(*hs)


def dab_kernel(cap, *refs):
    s, wd, dhs, cas, cbs = refs[0], refs[1], refs[2:5], refs[5:9], refs[9:13]
    da, db = refs[13:]
    rows = s.shape[0]
    parts = [d[...] for d in dhs] + [dot(s[...], wd[...], 1, 1)]
    for i in range(SIDE):
        dh = crossed(parts, i, cap)
        da[i * rows : (i + 1) * rows, :] = (dh * cas[i][...]).astype(BF16)
        db[i * rows : (i + 1) * rows, :] = (dh * cbs[i][...]).astype(BF16)


def dab_of(s, wdown, dhs, cas, cbs, cap):
    rows, width = s.shape
    hidden = wdown.shape[0]
    step = 256
    out = jax.ShapeDtypeStruct((SIDE * rows, hidden), BF16)
    return pl.pallas_call(
        functools.partial(dab_kernel, cap),
        grid=(hidden // step,),
        in_specs=[
            held((rows, width), lambda i: (0, 0)),
            pl.BlockSpec((step, width), lambda i: (i, 0)),
        ]
        + [pl.BlockSpec((rows, step), lambda i: (0, i))] * 11,
        out_specs=[pl.BlockSpec((SIDE * rows, step), lambda i: (0, i))] * 2,
        out_shape=[out] * 2,
        compiler_params=params(1, 24),
        cost_estimate=cost(2 * rows * width * hidden, 64 * rows * hidden),
        name="dab",
    )(s, wdown, *dhs, *cas, *cbs)


def keep_quarter(step, part, first_up, first_down, wait_up, wait_down):
    half = part.shape[0] // 2

    @pl.when(step == 0)
    def _():
        first_up[:half, :] = part[:half].astype(BF16)
        first_down[half:, :] = part[half:].astype(BF16)

    @pl.when(step == 1)
    def _():
        wait_up[...] = part[:half]
        first_up[half:, :] = part[half:].astype(BF16)

    @pl.when(step == 2)
    def _():
        first_down[:half, :] = part[:half].astype(BF16)
        wait_down[...] = part[half:]


def quarter_of(own, step, place_ref):
    if own:
        return place_ref[0]
    ahead = jnp.where(step == 0, 2, jnp.where(step == 1, 1, 3))
    return lax.rem(place_ref[0] + ahead, SIDE)


def quarter_outs(own, shape):
    rows, cols = shape
    shapes = [
        ((rows, cols), BF16),
        ((rows, cols), BF16),
        ((rows // 2, cols), F32),
        ((rows // 2, cols), F32),
    ]
    if own:
        shapes = [((rows, cols), F32)]
    return (
        [jax.ShapeDtypeStruct(s, t) for s, t in shapes],
        [pl.BlockSpec(s, lambda i, place: (0, 0)) for s, t in shapes],
    )


def down_kernel(own, place_ref, *refs):
    turned_ref, ss, outs = refs[0], refs[1:5], refs[5:]
    rows = jnp.concatenate([s[...] for s in ss], axis=0)
    part = dot(turned_ref[...], rows)
    if own:
        outs[0][...] = part
    else:
        keep_quarter(pl.program_id(0), part, *outs)


def down_parts(place, turned_h, ss, own):
    hidden, total = turned_h.shape
    rows, width = ss[0].shape
    quarter = width // SIDE
    steps = 1 if own else SIDE - 1
    shapes, specs = quarter_outs(own, (hidden, quarter))
    column = functools.partial(quarter_of, own)
    return pl.pallas_call(
        functools.partial(down_kernel, own),
        grid_spec=pltpu.PrefetchScalarGridSpec(
            num_scalar_prefetch=1,
            grid=(steps,),
            in_specs=[held((hidden, total), lambda i, place: (0, 0))]
            + [pl.BlockSpec((rows, quarter), lambda i, place: (0, column(i, place)))] * 4,
            out_specs=specs,
        ),
        out_shape=shapes,
        compiler_params=params(1, 20),
        cost_estimate=cost(2 * total * steps * quarter * hidden, 4 * total * width),
        name="down_own" if own else "down_parts",
    )(place, turned_h, *ss)


def gate_up_kernel(own, place_ref, *refs):
    xs, ds, outs = refs[:4], refs[4:6], refs[6:]
    rows = jnp.concatenate([x[...] for x in xs], axis=0).T
    part = jnp.concatenate([dot(rows, d[...]) for d in ds], axis=1)
    if own:
        outs[0][...] = part
    else:
        keep_quarter(pl.program_id(0), part, *outs)


def gate_up_parts(place, xs, ds, own):
    rows, width = xs[0].shape
    total, hidden = ds[0].shape
    quarter = width // SIDE
    steps = 1 if own else SIDE - 1
    shapes, specs = quarter_outs(own, (quarter, 2 * hidden))
    column = functools.partial(quarter_of, own)
    return pl.pallas_call(
        functools.partial(gate_up_kernel, own),
        grid_spec=pltpu.PrefetchScalarGridSpec(
            num_scalar_prefetch=1,
            grid=(steps,),
            in_specs=[pl.BlockSpec((rows, quarter), lambda i, place: (0, column(i, place)))] * 4
            + [held((total, hidden), lambda i, place: (0, 0))] * 2,
            out_specs=specs,
        ),
        out_shape=shapes,
        compiler_params=params(1, 32),
        cost_estimate=cost(4 * total * steps * quarter * hidden, 4 * total * width),
        name="gate_up_own" if own else "gate_up_parts",
    )(place, *xs, *ds)


def slot_kernel(cap, to_ref, *refs):
    da, db, w, out = refs
    hidden = da.shape[1]
    part = dot(da[...], w[:, :hidden], 1, 1) + dot(db[...], w[:, hidden:], 1, 1)
    for b in range(SIDE * SIDE):
        out[to_ref[b]] = part[b * cap : (b + 1) * cap].astype(BF16)


def slot_rows(to, ds, wgu, cap):
    total, hidden = ds[0].shape
    width = wgu.shape[0]
    step = 512
    blocks = total // cap
    return pl.pallas_call(
        functools.partial(slot_kernel, cap),
        grid=(width // step,),
        in_specs=[pl.BlockSpec(memory_space=pltpu.SMEM)]
        + [held((total, hidden), lambda i: (0, 0))] * 2
        + [pl.BlockSpec((step, 2 * hidden), lambda i: (i, 0))],
        out_specs=pl.BlockSpec((blocks, cap, step), lambda i: (0, 0, i)),
        out_shape=jax.ShapeDtypeStruct((blocks, cap, width), BF16),
        compiler_params=params(1, 24),
        cost_estimate=cost(4 * total * hidden * width, 4 * total * hidden + 4 * hidden * width),
        name="slot_rows",
    )(to, *ds, wgu)


def around(first, axis):
    return [first] + [moved_along(first, axis, OFF[b]) for b in range(1, SIDE)]


def spread(outs, axis):
    near = [moved_along(outs[j], axis, OFF[j]) for j in (1, 2)]
    far, n0, n1 = lax.optimization_barrier((outs[3], near[0], near[1]))
    return [outs[0], n0, n1, moved_along(far, axis, OFF[3])]


def ring_sum(own, first_up, first_down, wait_up, wait_down):
    half = wait_up.shape[0]
    up1 = moved_along(first_up, "edata", 1)
    down1 = moved_along(first_down, "edata", -1)
    second_up = (wait_up + up1[:half].astype(F32)).astype(BF16)
    second_down = (wait_down + down1[half:].astype(F32)).astype(BF16)
    up2 = moved_along(second_up, "edata", 1)
    down2 = moved_along(second_down, "edata", -1)
    upper = own[:half] + down1[:half].astype(F32) + up2.astype(F32)
    lower = own[half:] + up1[half:].astype(F32) + down2.astype(F32)
    return jnp.concatenate([upper, lower], axis=0).astype(BF16)


def body(hidden_in, out_grad, routes, gates, w_gate_up, w_down):
    tok = hidden_in.shape[1]
    width = hidden_in.shape[2]
    topk = routes.shape[2]
    experts = lax.axis_size("expert")
    cap = min(tok, tok * topk * 9 // (8 * experts))
    wgu, wdown = w_gate_up[0, 0], w_down[0, 0]
    me = lax.axis_index("expert")
    mx, mz = me // SIDE, me % SIDE
    off = jnp.array(OFF, jnp.int32)
    eids_x = (mx * SIDE + (mz + off) % SIDE).astype(jnp.int32)
    eids_g = ((mx + off) % SIDE * SIDE + mz).astype(jnp.int32)
    to = ((mx - off)[None, :] % SIDE * SIDE + (mz - off)[:, None] % SIDE).reshape(-1)
    place = lax.axis_index("edata").astype(jnp.int32).reshape(1)

    xe, ge = prep(routes[0].T, gates[0].T, hidden_in[0], out_grad[0], experts)
    xblocks = around(xe, "x")
    gblocks = around(ge, "z")
    xs = spread(pack(eids_x, xblocks, width, experts, cap, False), "z")
    ss = spread(pack(eids_g, gblocks, width, experts, cap, True), "x")

    ups = up(xs[:3], wgu) + up(xs[3:], wgu)
    hs, cas, cbs = ([u[k] for u in ups] for k in range(3))
    dhs = dh_of(ss[:3], wdown)
    turned_h = turned(hs, cap)
    down = down_parts(place, turned_h, ss, False)
    last, *down = lax.optimization_barrier((ss[3], *down))
    ds = dab_of(last, wdown, dhs, cas, cbs, cap)
    rows = slot_rows(to.astype(jnp.int32), ds, wgu, cap)
    rows, *ds = lax.optimization_barrier((rows, *ds))
    returned = lax.all_to_all(rows, "expert", split_axis=0, concat_axis=0, tiled=True)
    gate_up = gate_up_parts(place, xs, ds, False)
    own_down = down_parts(place, turned_h, ss, True)
    own_gate_up = gate_up_parts(place, xs, ds, True)
    down_grad = ring_sum(*own_down, *down)
    gate_up_grad = ring_sum(*own_gate_up, *gate_up)

    layer = home(ge, returned.reshape(experts * cap, width), out_grad[0], experts, cap)
    upstream = moved_along(layer, "section", -1)
    return (upstream[None], gate_up_grad[None, None], down_grad[None, None])


def solution(mesh):
    return jax.shard_map(
        body,
        mesh=mesh,
        in_specs=(
            P("section", ("edata", "expert"), None),
            P("section", ("edata", "expert"), None),
            P("section", ("edata", "expert"), None),
            P("section", ("edata", "expert"), None),
            P("section", "expert", None, None),
            P("section", "expert", None, None),
        ),
        out_specs=(
            P("section", ("edata", "expert"), None),
            P("section", "expert", "edata", None),
            P("section", "expert", None, "edata"),
        ),
        check_vma=False,
    )
```

```python
import functools

import jax
import jax.numpy as jnp
from jax import lax
from jax.experimental import pallas as pl
from jax.experimental.pallas import tpu as pltpu
from jax.sharding import PartitionSpec as P

BF16 = jnp.bfloat16
F32 = jnp.float32
OFF = (0, 1, 3, 2)
SIDE = 4
LANES = 128
MIB = 1024 * 1024


def params(steps):
    return pltpu.CompilerParams(
        vmem_limit_bytes=58 * MIB, dimension_semantics=("arbitrary",) * steps
    )


SCALARS = pl.BlockSpec(memory_space=pltpu.SMEM)
FAR = pl.BlockSpec(memory_space=pl.ANY)


def begun(src, dst, sem):
    copy = pltpu.make_async_copy(src, dst, sem)
    copy.start()
    return copy


def held(shape, index):
    return pl.BlockSpec(shape, index, pipeline_mode=pl.Buffered(1))


def cost(flops, moved):
    return pl.CostEstimate(flops=int(flops), bytes_accessed=int(moved), transcendentals=0)


def moved_along(block, axis, distance):
    if axis == "edata" or axis == "section":
        size = lax.axis_size(axis)
        return lax.ppermute(block, axis, [(i, (i + distance) % size) for i in range(size)])
    pairs = []
    for a in range(SIDE):
        for b in range(SIDE):
            if axis == "x":
                pairs.append((a * SIDE + b, (a + distance) % SIDE * SIDE + b))
            else:
                pairs.append((a * SIDE + b, a * SIDE + (b + distance) % SIDE))
    return lax.ppermute(block, "expert", pairs)


def iota(shape, dim):
    return lax.broadcasted_iota(jnp.int32, shape, dim)


def dot(a, b, da=1, db=0):
    return lax.dot_general(a, b, (((da,), (db,)), ((), ())), preferred_element_type=F32)


def prep_kernel(experts, routes_ref, gates_ref, x_ref, g_ref, xe_ref, ge_ref, tail_ref):
    tok, width = x_ref.shape
    topk = routes_ref.shape[0]
    expert = lax.rem(iota((LANES, tok), 0), experts)
    full = jnp.zeros((LANES, tok), F32)
    for k in range(topk):
        full += jnp.where(routes_ref[k : k + 1, :] == expert, gates_ref[k : k + 1, :], 0.0)
    full = full.T
    lane = iota((tok, LANES), 1)
    high = full.astype(BF16).astype(F32)
    rest = full - high
    middle = rest.astype(BF16).astype(F32)
    low = rest - middle
    piece = jnp.where(lane < 2 * experts, middle, jnp.where(lane < 3 * experts, low, 0.0))
    piece = jnp.where(lane < experts, high, piece).astype(BF16)
    for src, dst in ((x_ref, xe_ref), (g_ref, ge_ref)):
        dst[:, :width] = src[...]
        dst[:, width:] = piece
    tail_ref[...] = piece


def prep(routes, gates, x, g, experts):
    tok, width = x.shape
    shape = jax.ShapeDtypeStruct((tok, width + LANES), BF16)
    return pl.pallas_call(
        functools.partial(prep_kernel, experts),
        out_shape=(shape, shape, jax.ShapeDtypeStruct((tok, LANES), BF16)),
        compiler_params=params(0),
        name="prep",
    )(routes, gates, x, g)


def places(piece, experts, blocks):
    rows = piece.shape[0]
    tok = rows // blocks
    r, c = iota((rows, rows), 0), iota((rows, rows), 1)
    upto = jnp.where((c <= r) & (lax.div(c, tok) == lax.div(r, tok)), 1.0, 0.0).astype(BF16)
    lane = iota((rows, LANES), 1)
    mask = jnp.where((lane < experts) & (piece.astype(F32) > 0.0), 1.0, 0.0)
    return (dot(upto, mask.astype(BF16)) * mask).astype(BF16)


def pack_kernel(scale, experts, cap, eids_ref, *refs):
    blocks, outs = refs[:4], refs[4:8]
    rows_v, packed_v, table_v, in_sems, out_sems = refs[8:]
    pair = 2 * cap
    tok, width = blocks[0].shape[0], outs[0].shape[1]
    steps, step = packed_v.shape[0], packed_v.shape[3]
    pieces = [slice(width, width + LANES)] + [slice(t * step, (t + 1) * step) for t in range(steps)]
    loads = []
    for n, cols in enumerate(pieces):
        for b in range(4):
            part = rows_v.at[b // 2, pl.ds(b % 2 * tok, tok), cols]
            loads.append(begun(blocks[b].at[:, cols], part, in_sems.at[n, b]))
    for load in loads[:4]:
        load.wait()
    lane = iota((pair, LANES), 1)
    second = jnp.where(iota((pair, 2 * tok), 1) >= tok, cap, 0)
    place = iota((pair, 2 * tok), 0) + 1 - second
    place = jnp.where(place > 0, place, -1).astype(F32)
    factors = []
    for p in range(2):
        piece = rows_v[p, :, width:]
        known = places(piece, experts, 2)
        for j in range(SIDE):
            choose = jnp.where(lane == eids_ref[j], 1.0, 0.0).astype(BF16)
            found = dot(choose, known, 1, 1)
            table = jnp.where(found == place, 1.0, 0.0).astype(BF16)
            table_v[p, j * pair : (j + 1) * pair, :] = table
            if scale:
                mine = (lax.rem(lane, experts) == eids_ref[j]) & (lane < 3 * experts)
                gate = jnp.where(mine, dot(table, piece), 0.0)
                factors.append(jnp.sum(gate, axis=1, keepdims=True))
    stores = []
    for t in range(steps):
        for load in loads[4 * t + 4 : 4 * t + 8]:
            load.wait()
        for p in range(2):
            packed = dot(table_v[p], rows_v[p, :, pieces[t + 1]])
            for j in range(SIDE):
                part = packed[j * pair : (j + 1) * pair]
                if scale:
                    part = part * factors[p * SIDE + j]
                packed_v[t, j, p * pair : (p + 1) * pair, :] = part.astype(BF16)
        for j in range(SIDE):
            target = outs[j].at[:, pieces[t + 1]]
            stores.append(begun(packed_v.at[t, j], target, out_sems.at[t, j]))
    for store in stores:
        store.wait()


def pack(eids, blocks, width, experts, cap, scale):
    tok = blocks[0].shape[0]
    step = 512
    steps = width // step
    pair = 2 * cap
    out = jax.ShapeDtypeStruct((2 * pair, width), BF16)
    return pl.pallas_call(
        functools.partial(pack_kernel, scale, experts, cap),
        in_specs=[SCALARS] + [FAR] * 4,
        out_specs=[FAR] * 4,
        out_shape=[out] * 4,
        scratch_shapes=[
            pltpu.VMEM((2, 2 * tok, width + LANES), BF16),
            pltpu.VMEM((steps, SIDE, 2 * pair, step), BF16),
            pltpu.VMEM((2, SIDE * pair, 2 * tok), BF16),
            pltpu.SemaphoreType.DMA((steps + 1, 4)),
            pltpu.SemaphoreType.DMA((steps, SIDE)),
        ],
        compiler_params=params(0),
        cost_estimate=cost(3e9, 10e6),
        name="pack_scaled" if scale else "pack_rows",
    )(eids, *blocks)


def home_kernel(experts, cap, tail_ref, rows_ref, grad_ref, out_ref, table_ref):
    tok = tail_ref.shape[0]
    total = experts * cap

    @pl.when(pl.program_id(0) == 0)
    def _():
        choose = jnp.where(iota((LANES, total), 0) == lax.div(iota((LANES, total), 1), cap), 1.0, 0.0)
        found = dot(places(tail_ref[...], experts, 1), choose.astype(BF16))
        place = lax.rem(iota((tok, total), 1), cap) + 1
        table_ref[...] = jnp.where(found == place.astype(F32), 1.0, 0.0).astype(BF16)

    total_grad = dot(table_ref[...], rows_ref[...]) + grad_ref[...].astype(F32)
    out_ref[...] = total_grad.astype(BF16)


def home(tail, rows, grad, experts, cap):
    tok, width = grad.shape
    step = 512
    total = experts * cap
    return pl.pallas_call(
        functools.partial(home_kernel, experts, cap),
        grid=(width // step,),
        in_specs=[
            held((tok, LANES), lambda i: (0, 0)),
            pl.BlockSpec((total, step), lambda i: (0, i)),
            pl.BlockSpec((tok, step), lambda i: (0, i)),
        ],
        out_specs=pl.BlockSpec((tok, step), lambda i: (0, i)),
        out_shape=jax.ShapeDtypeStruct((tok, width), BF16),
        scratch_shapes=[pltpu.VMEM((tok, total), BF16)],
        compiler_params=params(1),
        cost_estimate=cost(3e9, 10e6),
        name="home",
    )(tail, rows, grad)


def up_kernel(count, *refs):
    xs, (wa, wb), outs = refs[:count], refs[count : count + 2], refs[count + 2 :]
    for i in range(count):
        rows = xs[i][...]
        a = dot(rows, wa[...])
        b = dot(rows, wb[...])
        sig = jax.nn.sigmoid(a)
        outs[3 * i][...] = a * sig * b
        outs[3 * i + 1][...] = (b * sig * (1.0 + a * (1.0 - sig))).astype(BF16)
        outs[3 * i + 2][...] = (a * sig).astype(BF16)


def up(xs, wgu):
    count = len(xs)
    rows, width = xs[0].shape
    hidden = wgu.shape[1] // 2
    step = 256
    steps = hidden // step
    kinds = (F32, BF16, BF16) * count
    flat = pl.pallas_call(
        functools.partial(up_kernel, count),
        grid=(steps,),
        in_specs=[held((rows, width), lambda i: (0, 0))] * count
        + [
            pl.BlockSpec((width, step), lambda i: (0, i)),
            pl.BlockSpec((width, step), lambda i: (0, i + steps)),
        ],
        out_specs=[pl.BlockSpec((rows, step), lambda i: (0, i))] * (3 * count),
        out_shape=[jax.ShapeDtypeStruct((rows, hidden), kind) for kind in kinds],
        compiler_params=params(1),
        cost_estimate=cost(3e9, 10e6),
        name="up",
    )(*xs, wgu, wgu)
    return [flat[3 * i : 3 * i + 3] for i in range(count)]


def dh_kernel(count, *refs):
    ss, wd, outs = refs[:count], refs[count], refs[count + 1 :]
    for i in range(count):
        outs[i][...] = dot(ss[i][...], wd[...], 1, 1)


def dh_of(ss, wdown):
    count = len(ss)
    rows, width = ss[0].shape
    hidden = wdown.shape[0]
    step = 256
    return pl.pallas_call(
        functools.partial(dh_kernel, count),
        grid=(hidden // step,),
        in_specs=[held((rows, width), lambda i: (0, 0))] * count
        + [pl.BlockSpec((step, width), lambda i: (i, 0))],
        out_specs=[pl.BlockSpec((rows, step), lambda i: (0, i))] * count,
        out_shape=[jax.ShapeDtypeStruct((rows, hidden), F32)] * count,
        compiler_params=params(1),
        cost_estimate=cost(3e9, 10e6),
        name="dh",
    )(*ss, wdown)


def crossed(parts, j, cap):
    return jnp.concatenate([part[j * cap : (j + 1) * cap, :] for part in parts], axis=0)


AHEAD = (2, 1, 3)
SPOTS = (((0, 0), (1, 1)), ((2, 0), (0, 1)), ((1, 0), (2, 1)))


def put_halves(k, part, sent_v, wait_v, outs, sems):
    half = part.shape[0] // 2
    copies = []
    for side in range(2):
        out, row = SPOTS[k][side]
        piece = part[side * half : (side + 1) * half]
        if out == 2:
            staged = wait_v.at[row]
            staged[...] = piece
        else:
            staged = sent_v.at[out, row]
            staged[...] = piece.astype(BF16)
        target = outs[out].at[row * half : (row + 1) * half, :]
        copies.append(begun(staged, target, sems.at[k, side]))
    return copies


def ahead_of(place_ref, ahead, size):
    start = lax.rem(place_ref[0] + ahead, SIDE) * size
    return pl.ds(pl.multiple_of(start, size), size)


def message_outs(rows, cols):
    return [jax.ShapeDtypeStruct((rows, cols), kind) for kind in (BF16, BF16, F32)]


def message_scratch(rows, cols):
    return [
        pltpu.VMEM((2, 2, rows // 2, cols), BF16),
        pltpu.VMEM((2, rows // 2, cols), F32),
        pltpu.SemaphoreType.DMA((3, 2)),
    ]


def down_kernel(cap, place_ref, *refs):
    hs, ss, outs, turned_out = refs[:4], refs[4:8], refs[8:11], refs[11]
    h_v, s_v, turned_v, sent_v, wait_v, out_sems, h_sems, s_sems, turned_sem = refs[12:]
    rows, width = ss[0].shape
    size = width // SIDE
    h_loads = [begun(hs[i], h_v.at[i], h_sems.at[i]) for i in range(SIDE)]
    s_loads = []
    for k, ahead in enumerate(AHEAD):
        cols = ahead_of(place_ref, ahead, size)
        for j in range(SIDE):
            part = s_v.at[k, pl.ds(j * rows, rows), :]
            s_loads.append(begun(ss[j].at[:, cols], part, s_sems.at[k, j]))
    for load in h_loads:
        load.wait()
    step = 256
    for t in range(turned_v.shape[0] // step):
        cols = slice(t * step, (t + 1) * step)
        parts = [h_v[i, :, cols] for i in range(SIDE)]
        whole = jnp.concatenate([crossed(parts, j, cap) for j in range(SIDE)], axis=0)
        turned_v[cols, :] = whole.T.astype(BF16)
    copies = [begun(turned_v, turned_out, turned_sem)]
    for k in range(3):
        for load in s_loads[4 * k : 4 * k + 4]:
            load.wait()
        copies += put_halves(k, dot(turned_v[...], s_v[k]), sent_v, wait_v, outs, out_sems)
    for copy in copies:
        copy.wait()


def down_parts(place, hs, ss, cap):
    rows, hidden = hs[0].shape
    quarter = ss[0].shape[1] // SIDE
    total = SIDE * rows
    *messages, turned_h = pl.pallas_call(
        functools.partial(down_kernel, cap),
        in_specs=[SCALARS] + [FAR] * 8,
        out_specs=[FAR] * 4,
        out_shape=message_outs(hidden, quarter) + [jax.ShapeDtypeStruct((hidden, total), BF16)],
        scratch_shapes=[
            pltpu.VMEM((SIDE, rows, hidden), F32),
            pltpu.VMEM((3, total, quarter), BF16),
            pltpu.VMEM((hidden, total), BF16),
        ]
        + message_scratch(hidden, quarter)
        + [
            pltpu.SemaphoreType.DMA((SIDE,)),
            pltpu.SemaphoreType.DMA((3, SIDE)),
            pltpu.SemaphoreType.DMA,
        ],
        compiler_params=params(0),
        cost_estimate=cost(1, 1),
        name="down_parts",
    )(place, *hs, *ss)
    return messages, turned_h


def down_own_kernel(place_ref, *refs):
    turned_ref, ss, out = refs[0], refs[1:5], refs[5]
    out[...] = dot(turned_ref[...], jnp.concatenate([s[...] for s in ss], axis=0))


def down_own(place, turned_h, ss):
    hidden, total = turned_h.shape
    rows, width = ss[0].shape
    quarter = width // SIDE
    return pl.pallas_call(
        down_own_kernel,
        grid_spec=pltpu.PrefetchScalarGridSpec(
            num_scalar_prefetch=1,
            grid=(2,),
            in_specs=[pl.BlockSpec((hidden // 2, total), lambda i, place: (i, 0))]
            + [held((rows, quarter), lambda i, place: (0, place[0]))] * 4,
            out_specs=pl.BlockSpec((hidden // 2, quarter), lambda i, place: (i, 0)),
        ),
        out_shape=jax.ShapeDtypeStruct((hidden, quarter), F32),
        compiler_params=params(1),
        cost_estimate=cost(1, 1),
        name="down_own",
    )(place, turned_h, *ss)


EARLY = tuple((i, j) for i in range(3) for j in range(3))
LATE = tuple((3, j) for j in range(3)) + tuple((i, 3) for i in range(4))


def early_kernel(cap, to_ref, *refs):
    dhs, cas, cbs, w, out, ds = refs[:3], refs[3:6], refs[6:9], refs[9], refs[10], refs[11:13]
    dh_v, f_v, d_v, e_v, w_v, rows_v, dh_sems, f_sems, w_sems, d_sems, out_sems = refs[13:]
    rows, hidden = dhs[0].shape
    loads = []
    for i in range(3):
        loads.append(begun(dhs[i], dh_v.at[i], dh_sems.at[i]))
        loads.append(begun(cas[i], f_v.at[0, i], f_sems.at[0, i]))
        loads.append(begun(cbs[i], f_v.at[1, i], f_sems.at[1, i]))
    steps, step = w_v.shape[0], w_v.shape[1]
    cols = [pl.ds(t * step, step) for t in range(steps)]
    w_loads = [begun(w.at[cols[t], :], w_v.at[t], w_sems.at[t]) for t in range(steps)]
    for load in loads:
        load.wait()
    copies = []
    for k in range(2):
        for t in range(hidden // 256):
            part = slice(t * 256, (t + 1) * 256)
            chunks = [dh_v[j, :, part] for j in range(3)]
            kept = []
            for i in range(3):
                factor = f_v[k, i, :, part].astype(F32)[: 3 * cap]
                product = crossed(chunks, i, cap) * factor
                kept.append(product)
                whole = jnp.concatenate([product, jnp.zeros((cap, 256), F32)], axis=0)
                d_v[k, i * rows : (i + 1) * rows, part] = whole.astype(BF16)
            e_v[k, :, part] = jnp.concatenate(kept, axis=0).astype(BF16)
        target = ds[k].at[pl.ds(0, 3 * rows), :]
        copies.append(begun(d_v.at[k], target, d_sems.at[k]))
    for t in range(steps):
        w_loads[t].wait()
        part = dot(e_v[0], w_v[t, :, :hidden], 1, 1) + dot(e_v[1], w_v[t, :, hidden:], 1, 1)
        for n, (i, j) in enumerate(EARLY):
            block = part[n * cap : (n + 1) * cap].astype(BF16)
            rows_v[t, n] = block
            target = out.at[to_ref[i * SIDE + j], :, cols[t]]
            copies.append(begun(rows_v.at[t, n], target, out_sems.at[t, n]))
    for copy in copies:
        copy.wait()


def early_rows(to, dhs, cas, cbs, wgu, cap):
    rows, hidden = dhs[0].shape
    width = wgu.shape[0]
    step = 512
    steps = width // step
    early = len(EARLY)
    out = jax.ShapeDtypeStruct((SIDE * rows, hidden), BF16)
    slots, da, db = pl.pallas_call(
        functools.partial(early_kernel, cap),
        in_specs=[SCALARS] + [FAR] * 10,
        out_specs=[FAR] * 3,
        out_shape=[jax.ShapeDtypeStruct((SIDE * SIDE, cap, width), BF16), out, out],
        scratch_shapes=[
            pltpu.VMEM((3, rows, hidden), F32),
            pltpu.VMEM((2, 3, rows, hidden), BF16),
            pltpu.VMEM((2, 3 * rows, hidden), BF16),
            pltpu.VMEM((2, early * cap, hidden), BF16),
            pltpu.VMEM((steps, step, 2 * hidden), BF16),
            pltpu.VMEM((steps, early, cap, step), BF16),
            pltpu.SemaphoreType.DMA((3,)),
            pltpu.SemaphoreType.DMA((2, 3)),
            pltpu.SemaphoreType.DMA((steps,)),
            pltpu.SemaphoreType.DMA((2,)),
            pltpu.SemaphoreType.DMA((steps, early)),
        ],
        compiler_params=params(0),
        cost_estimate=cost(3e9, 10e6),
        name="early_rows",
    )(to, *dhs, *cas, *cbs, wgu)
    return slots, [da, db]


def late_kernel(cap, to_ref, s, wd, *refs):
    dhs, cas, cbs, w, _, out, ds = refs[:3], refs[3:7], refs[7:11], refs[11], refs[12], refs[13], refs[14:16]
    s_v, wd_v, dh_v, f_v, d_v, w_v, rows_v = refs[16:23]
    s_sem, wd_sems, dh_sems, f_sems, w_sems, d_sems, out_sems = refs[23:]
    rows = s.shape[0]
    hidden = wd.shape[0]
    step = 256
    s_load = begun(s, s_v, s_sem)
    wd_loads, f_loads = [], []
    for t in range(hidden // step):
        cols = pl.ds(t * step, step)
        wd_loads.append(begun(wd.at[cols, :], wd_v.at[cols, :], wd_sems.at[t]))
    for j in range(3):
        f_loads.append(begun(dhs[j], dh_v.at[j], dh_sems.at[j]))
    for i in range(SIDE):
        f_loads.append(begun(cas[i], f_v.at[0, i], f_sems.at[0, i]))
        f_loads.append(begun(cbs[i], f_v.at[1, i], f_sems.at[1, i]))
    steps, part_width = w_v.shape[0], w_v.shape[1]
    parts = [pl.ds(t * part_width, part_width) for t in range(steps)]
    w_loads = [begun(w.at[parts[t], :], w_v.at[t], w_sems.at[t]) for t in range(steps)]
    s_load.wait()
    for t in range(hidden // step):
        cols = slice(t * step, (t + 1) * step)
        wd_loads[t].wait()
        last = dot(s_v[...], wd_v[cols, :], 1, 1)
        if t == 0:
            for load in f_loads:
                load.wait()
        chunks = [dh_v[j, 3 * cap :, cols] for j in range(3)] + [last]
        dh = jnp.concatenate(chunks, axis=0)
        for k in range(2):
            factors = [f_v[k, 3, :, cols].astype(F32)[: 3 * cap]]
            factors += [f_v[k, i, :, cols].astype(F32)[3 * cap :] for i in range(SIDE)]
            d_v[k, :, cols] = (dh * jnp.concatenate(factors, axis=0)).astype(BF16)
    copies = [begun(d_v.at[k], ds[k], d_sems.at[k]) for k in range(2)]
    for t in range(steps):
        w_loads[t].wait()
        part = dot(d_v[0], w_v[t, :, :hidden], 1, 1) + dot(d_v[1], w_v[t, :, hidden:], 1, 1)
        for n, (i, j) in enumerate(LATE):
            rows_v[t, n] = part[n * cap : (n + 1) * cap].astype(BF16)
            target = out.at[to_ref[i * SIDE + j], :, parts[t]]
            copies.append(begun(rows_v.at[t, n], target, out_sems.at[t, n]))
    for copy in copies:
        copy.wait()


def late_rows(to, s, wdown, dhs, cas, cbs, wgu, slots, cap):
    rows, width = s.shape
    hidden = wdown.shape[0]
    step = 512
    steps = width // step
    late = len(LATE)
    out = jax.ShapeDtypeStruct((late * cap, hidden), BF16)
    slots, da, db = pl.pallas_call(
        functools.partial(late_kernel, cap),
        in_specs=[SCALARS] + [FAR] * 15,
        out_specs=[FAR] * 3,
        out_shape=[jax.ShapeDtypeStruct(slots.shape, BF16), out, out],
        input_output_aliases={15: 0},
        scratch_shapes=[
            pltpu.VMEM((rows, width), BF16),
            pltpu.VMEM((hidden, width), BF16),
            pltpu.VMEM((3, rows, hidden), F32),
            pltpu.VMEM((2, SIDE, rows, hidden), BF16),
            pltpu.VMEM((2, late * cap, hidden), BF16),
            pltpu.VMEM((steps, step, 2 * hidden), BF16),
            pltpu.VMEM((steps, late, cap, step), BF16),
            pltpu.SemaphoreType.DMA,
            pltpu.SemaphoreType.DMA((hidden // 256,)),
            pltpu.SemaphoreType.DMA((3,)),
            pltpu.SemaphoreType.DMA((2, SIDE)),
            pltpu.SemaphoreType.DMA((steps,)),
            pltpu.SemaphoreType.DMA((2,)),
            pltpu.SemaphoreType.DMA((steps, late)),
        ],
        compiler_params=params(0),
        cost_estimate=cost(1, 1),
        name="late_rows",
    )(to, s, wdown, *dhs, *cas, *cbs, wgu, slots)
    return slots, [da, db]


def gate_up_kernel(cap, place_ref, *refs):
    early, late, xs, outs, ds = refs[:2], refs[2:4], refs[4:8], refs[8:11], refs[11:13]
    d_v, late_v, x_v, sent_v, wait_v, out_sems, d_sems, x_sems = refs[13:]
    rows, width = xs[0].shape
    size = width // SIDE
    loads = []
    for k in range(2):
        part = pl.ds(0, 3 * rows)
        loads.append(begun(early[k].at[part, :], d_v.at[k, part, :], d_sems.at[0, k]))
        loads.append(begun(late[k], late_v.at[k], d_sems.at[1, k]))
    for k, ahead in enumerate(AHEAD):
        cols = ahead_of(place_ref, ahead, size)
        for i in range(SIDE):
            part = x_v.at[k, pl.ds(i * rows, rows), :]
            loads.append(begun(xs[i].at[:, cols], part, x_sems.at[k, i]))
    for load in loads[:4]:
        load.wait()
    edge = 3 * cap - 8
    copies = []
    for k in range(2):
        fresh = late_v[k].astype(F32)
        for i in range(3):
            at = slice(i * rows + edge, (i + 1) * rows)
            old = d_v[k, at, :].astype(F32)[:8]
            new = fresh[(3 + i) * cap : (4 + i) * cap]
            d_v[k, at, :] = jnp.concatenate([old, new], axis=0).astype(BF16)
        new = jnp.concatenate([fresh[: 3 * cap], fresh[6 * cap :]], axis=0)
        d_v[k, 3 * rows :, :] = new.astype(BF16)
        copies.append(begun(d_v.at[k], ds[k], d_sems.at[2, k]))
    for k in range(3):
        for load in loads[4 * k + 4 : 4 * k + 8]:
            load.wait()
        turned_x = x_v[k].T
        part = jnp.concatenate([dot(turned_x, d_v[0]), dot(turned_x, d_v[1])], axis=1)
        copies += put_halves(k, part, sent_v, wait_v, outs, out_sems)
    for copy in copies:
        copy.wait()


def gate_up_parts(place, early, late, xs, cap):
    rows, width = xs[0].shape
    total, hidden = early[0].shape
    quarter = width // SIDE
    out = jax.ShapeDtypeStruct((total, hidden), BF16)
    *messages, da, db = pl.pallas_call(
        functools.partial(gate_up_kernel, cap),
        in_specs=[SCALARS] + [FAR] * 8,
        out_specs=[FAR] * 5,
        out_shape=message_outs(quarter, 2 * hidden) + [out, out],
        scratch_shapes=[
            pltpu.VMEM((2, total, hidden), BF16),
            pltpu.VMEM((2, *late[0].shape), BF16),
            pltpu.VMEM((3, total, quarter), BF16),
        ]
        + message_scratch(quarter, 2 * hidden)
        + [pltpu.SemaphoreType.DMA((3, 2)), pltpu.SemaphoreType.DMA((3, SIDE))],
        compiler_params=params(0),
        cost_estimate=cost(1, 1),
        name="gate_up_parts",
    )(place, *early, *late, *xs)
    return messages, [da, db]


def gate_up_own_kernel(place_ref, *refs):
    xs, ds, out = refs[:4], refs[4:6], refs[6]
    rows = jnp.concatenate([x[...] for x in xs], axis=0).T
    out[...] = jnp.concatenate([dot(rows, d[...]) for d in ds], axis=1)


def gate_up_own(place, xs, ds):
    rows, width = xs[0].shape
    total, hidden = ds[0].shape
    half = width // SIDE // 2
    return pl.pallas_call(
        gate_up_own_kernel,
        grid_spec=pltpu.PrefetchScalarGridSpec(
            num_scalar_prefetch=1,
            grid=(2,),
            in_specs=[pl.BlockSpec((rows, half), lambda i, place: (0, 2 * place[0] + i))] * 4
            + [held((total, hidden), lambda i, place: (0, 0))] * 2,
            out_specs=pl.BlockSpec((half, 2 * hidden), lambda i, place: (i, 0)),
        ),
        out_shape=jax.ShapeDtypeStruct((2 * half, 2 * hidden), F32),
        compiler_params=params(1),
        cost_estimate=cost(200e9, 10e6),
        name="gate_up_own",
    )(place, *xs, *ds)


def around(first, axis):
    return [first] + [moved_along(first, axis, OFF[b]) for b in range(1, SIDE)]


def spread(outs, axis, work):
    near = [moved_along(outs[j], axis, OFF[j]) for j in (1, 2)]
    done = work(outs[0])
    far, near[0], near[1], *done = lax.optimization_barrier((outs[3], *near, *done))
    return [outs[0], *near, moved_along(far, axis, OFF[3])], done


def ring_first(first_up, first_down, wait):
    return moved_along(first_up, "edata", 1), moved_along(first_down, "edata", -1)


def ring_second(up1, down1, first_up, first_down, wait):
    half = wait.shape[0] // 2
    second_up = (wait[:half] + up1[:half].astype(F32)).astype(BF16)
    second_down = (wait[half:] + down1[half:].astype(F32)).astype(BF16)
    return moved_along(second_up, "edata", 1), moved_along(second_down, "edata", -1)


def ring_last(own, up1, down1, up2, down2):
    half = own.shape[0] // 2
    upper = own[:half] + down1[:half].astype(F32) + up2.astype(F32)
    lower = own[half:] + up1[half:].astype(F32) + down2.astype(F32)
    return jnp.concatenate([upper, lower], axis=0).astype(BF16)


def body(hidden_in, out_grad, routes, gates, w_gate_up, w_down):
    tok = hidden_in.shape[1]
    width = hidden_in.shape[2]
    topk = routes.shape[2]
    experts = lax.axis_size("expert")
    cap = min(tok, tok * topk * 9 // (8 * experts))
    wgu, wdown = w_gate_up[0, 0], w_down[0, 0]
    me = lax.axis_index("expert")
    mx, mz = me // SIDE, me % SIDE
    off = jnp.array(OFF, jnp.int32)
    eids_x = (mx * SIDE + (mz + off) % SIDE).astype(jnp.int32)
    eids_g = ((mx + off) % SIDE * SIDE + mz).astype(jnp.int32)
    to = ((mx - off)[None, :] % SIDE * SIDE + (mz - off)[:, None] % SIDE).reshape(-1)
    place = lax.axis_index("edata").astype(jnp.int32).reshape(1)

    xe, ge, tail = prep(routes[0].T, gates[0].T, hidden_in[0], out_grad[0], experts)
    xblocks = around(xe, "x")
    gblocks = around(ge, "z")
    xpacked = list(pack(eids_x, xblocks, width, experts, cap, False))
    xpacked[0], gblocks[0] = lax.optimization_barrier((xpacked[0], gblocks[0]))
    gpacked = pack(eids_g, gblocks, width, experts, cap, True)
    xs, first_up = spread(xpacked, "z", lambda rows: up([rows], wgu)[0])
    ss, first_dh = spread(gpacked, "x", lambda rows: dh_of([rows], wdown))
    to = to.astype(jnp.int32)
    ups = [first_up] + up(xs[1:3], wgu)
    dhs = [*first_dh, *dh_of(ss[1:3], wdown)]
    cas, cbs = ([u[k] for u in ups] for k in (1, 2))
    slots, early = early_rows(to, dhs, cas, cbs, wgu, cap)
    ups += up(xs[3:], wgu)
    hs, cas, cbs = ([u[k] for u in ups] for k in range(3))
    last, slots, hs[3], *dhs = lax.optimization_barrier((ss[3], slots, hs[3], *dhs))
    ss = ss[:3] + [last]
    down, turned_h = down_parts(place, hs, ss, cap)
    last, *down = lax.optimization_barrier((last, *down))
    down_first = ring_first(*down)
    rows, late = late_rows(to, last, wdown, dhs, cas, cbs, wgu, slots, cap)
    returned = lax.all_to_all(rows, "expert", split_axis=0, concat_axis=0, tiled=True)
    rows, *later = lax.optimization_barrier((rows, *late, *down_first))
    late, down_first = later[:2], later[2:]
    gate_up, ds = gate_up_parts(place, early, late, xs, cap)
    gate_up_first = ring_first(*gate_up)
    wait, da, db, turned_h = lax.optimization_barrier((gate_up[2], *ds, turned_h))
    gate_up = [*gate_up[:2], wait]
    own_down = down_own(place, turned_h, ss)
    own_gate_up = gate_up_own(place, xs, [da, db])
    own_down, own_gate_up, *gate_up_first = lax.optimization_barrier(
        (own_down, own_gate_up, *gate_up_first)
    )
    down_second = ring_second(*down_first, *down)
    gate_up_second = ring_second(*gate_up_first, *gate_up)
    down_grad = ring_last(own_down, *down_first, *down_second)
    gate_up_grad = ring_last(own_gate_up, *gate_up_first, *gate_up_second)

    layer = home(tail, returned.reshape(experts * cap, width), out_grad[0], experts, cap)
    upstream = moved_along(layer, "section", -1)
    return (upstream[None], gate_up_grad[None, None], down_grad[None, None])


def solution(mesh):
    return jax.shard_map(
        body,
        mesh=mesh,
        in_specs=(
            P("section", ("edata", "expert"), None),
            P("section", ("edata", "expert"), None),
            P("section", ("edata", "expert"), None),
            P("section", ("edata", "expert"), None),
            P("section", "expert", None, None),
            P("section", "expert", None, None),
        ),
        out_specs=(
            P("section", ("edata", "expert"), None),
            P("section", "expert", "edata", None),
            P("section", "expert", None, "edata"),
        ),
        check_vma=False,
    )
```

```python
import functools

import jax
import jax.numpy as jnp
from jax import lax
from jax.experimental import pallas as pl
from jax.experimental.pallas import tpu as pltpu
from jax.sharding import PartitionSpec as P

BF16 = jnp.bfloat16
F32 = jnp.float32
OFF = (0, 1, 3, 2)
SIDE = 4
LANES = 128
MIB = 1024 * 1024


def params(steps):
    return pltpu.CompilerParams(
        vmem_limit_bytes=58 * MIB, dimension_semantics=("arbitrary",) * steps
    )


SCALARS = pl.BlockSpec(memory_space=pltpu.SMEM)
FAR = pl.BlockSpec(memory_space=pl.ANY)


def begun(src, dst, sem):
    copy = pltpu.make_async_copy(src, dst, sem)
    copy.start()
    return copy


def held(shape, index):
    return pl.BlockSpec(shape, index, pipeline_mode=pl.Buffered(1))


def cost(flops, moved):
    return pl.CostEstimate(flops=int(flops), bytes_accessed=int(moved), transcendentals=0)


def moved_along(block, axis, distance):
    if axis == "edata" or axis == "section":
        size = lax.axis_size(axis)
        return lax.ppermute(block, axis, [(i, (i + distance) % size) for i in range(size)])
    pairs = []
    for a in range(SIDE):
        for b in range(SIDE):
            if axis == "x":
                pairs.append((a * SIDE + b, (a + distance) % SIDE * SIDE + b))
            else:
                pairs.append((a * SIDE + b, a * SIDE + (b + distance) % SIDE))
    return lax.ppermute(block, "expert", pairs)


def iota(shape, dim):
    return lax.broadcasted_iota(jnp.int32, shape, dim)


def dot(a, b, da=1, db=0):
    return lax.dot_general(a, b, (((da,), (db,)), ((), ())), preferred_element_type=F32)


def prep_kernel(experts, routes_ref, gates_ref, x_ref, g_ref, xe_ref, ge_ref, tail_ref):
    tok, width = x_ref.shape
    topk = routes_ref.shape[0]
    expert = lax.rem(iota((LANES, tok), 0), experts)
    full = jnp.zeros((LANES, tok), F32)
    for k in range(topk):
        full += jnp.where(routes_ref[k : k + 1, :] == expert, gates_ref[k : k + 1, :], 0.0)
    full = full.T
    lane = iota((tok, LANES), 1)
    high = full.astype(BF16).astype(F32)
    rest = full - high
    middle = rest.astype(BF16).astype(F32)
    low = rest - middle
    piece = jnp.where(lane < 2 * experts, middle, jnp.where(lane < 3 * experts, low, 0.0))
    piece = jnp.where(lane < experts, high, piece).astype(BF16)
    for src, dst in ((x_ref, xe_ref), (g_ref, ge_ref)):
        dst[:, :width] = src[...]
        dst[:, width:] = piece
    tail_ref[...] = piece


def prep(routes, gates, x, g, experts):
    tok, width = x.shape
    shape = jax.ShapeDtypeStruct((tok, width + LANES), BF16)
    return pl.pallas_call(
        functools.partial(prep_kernel, experts),
        out_shape=(shape, shape, jax.ShapeDtypeStruct((tok, LANES), BF16)),
        compiler_params=params(0),
        name="prep",
    )(routes, gates, x, g)


def places(piece, experts, blocks):
    rows = piece.shape[0]
    tok = rows // blocks
    r, c = iota((rows, rows), 0), iota((rows, rows), 1)
    upto = jnp.where((c <= r) & (lax.div(c, tok) == lax.div(r, tok)), 1.0, 0.0).astype(BF16)
    lane = iota((rows, LANES), 1)
    mask = jnp.where((lane < experts) & (piece.astype(F32) > 0.0), 1.0, 0.0)
    return (dot(upto, mask.astype(BF16)) * mask).astype(BF16)


def pack_kernel(scale, experts, cap, eids_ref, *refs):
    blocks, outs = refs[:4], refs[4:-5]
    rows_v, packed_v, table_v, in_sems, out_sems = refs[-5:]
    count = len(outs)
    pair = 2 * cap
    tok, width = blocks[0].shape[0], outs[0].shape[1]
    steps, step = packed_v.shape[0], packed_v.shape[3]
    pieces = [slice(width, width + LANES)] + [slice(t * step, (t + 1) * step) for t in range(steps)]
    loads = []
    for n, cols in enumerate(pieces):
        for b in range(4):
            part = rows_v.at[b // 2, pl.ds(b % 2 * tok, tok), cols]
            loads.append(begun(blocks[b].at[:, cols], part, in_sems.at[n, b]))
    for load in loads[:4]:
        load.wait()
    lane = iota((pair, LANES), 1)
    second = jnp.where(iota((pair, 2 * tok), 1) >= tok, cap, 0)
    place = iota((pair, 2 * tok), 0) + 1 - second
    place = jnp.where(place > 0, place, -1).astype(F32)
    factors = []
    for p in range(2):
        piece = rows_v[p, :, width:]
        known = places(piece, experts, 2)
        for j in range(count):
            choose = jnp.where(lane == eids_ref[j], 1.0, 0.0).astype(BF16)
            found = dot(choose, known, 1, 1)
            table = jnp.where(found == place, 1.0, 0.0).astype(BF16)
            table_v[p, j * pair : (j + 1) * pair, :] = table
            if scale:
                mine = (lax.rem(lane, experts) == eids_ref[j]) & (lane < 3 * experts)
                gate = jnp.where(mine, dot(table, piece), 0.0)
                factors.append(jnp.sum(gate, axis=1, keepdims=True))
    stores = []
    for t in range(steps):
        for load in loads[4 * t + 4 : 4 * t + 8]:
            load.wait()
        for p in range(2):
            packed = dot(table_v[p], rows_v[p, :, pieces[t + 1]])
            for j in range(count):
                part = packed[j * pair : (j + 1) * pair]
                if scale:
                    part = part * factors[p * count + j]
                packed_v[t, j, p * pair : (p + 1) * pair, :] = part.astype(BF16)
        for j in range(count):
            target = outs[j].at[:, pieces[t + 1]]
            stores.append(begun(packed_v.at[t, j], target, out_sems.at[t, j]))
    for store in stores:
        store.wait()


def pack(eids, blocks, width, experts, cap, scale, name):
    count = eids.shape[0]
    tok = blocks[0].shape[0]
    step = 512
    steps = width // step
    pair = 2 * cap
    out = jax.ShapeDtypeStruct((2 * pair, width), BF16)
    return pl.pallas_call(
        functools.partial(pack_kernel, scale, experts, cap),
        in_specs=[SCALARS] + [FAR] * 4,
        out_specs=[FAR] * count,
        out_shape=[out] * count,
        scratch_shapes=[
            pltpu.VMEM((2, 2 * tok, width + LANES), BF16),
            pltpu.VMEM((steps, count, 2 * pair, step), BF16),
            pltpu.VMEM((2, count * pair, 2 * tok), BF16),
            pltpu.SemaphoreType.DMA((steps + 1, 4)),
            pltpu.SemaphoreType.DMA((steps, count)),
        ],
        compiler_params=params(0),
        cost_estimate=cost(3e9, 10e6),
        name=name,
    )(eids, *blocks)


def home_kernel(experts, cap, tail_ref, rows_ref, grad_ref, out_ref, table_ref):
    tok = tail_ref.shape[0]
    total = experts * cap

    @pl.when(pl.program_id(0) == 0)
    def _():
        choose = jnp.where(iota((LANES, total), 0) == lax.div(iota((LANES, total), 1), cap), 1.0, 0.0)
        found = dot(places(tail_ref[...], experts, 1), choose.astype(BF16))
        place = lax.rem(iota((tok, total), 1), cap) + 1
        table_ref[...] = jnp.where(found == place.astype(F32), 1.0, 0.0).astype(BF16)

    total_grad = dot(table_ref[...], rows_ref[...]) + grad_ref[...].astype(F32)
    out_ref[...] = total_grad.astype(BF16)


def home(tail, rows, grad, experts, cap):
    tok, width = grad.shape
    step = 512
    total = experts * cap
    return pl.pallas_call(
        functools.partial(home_kernel, experts, cap),
        grid=(width // step,),
        in_specs=[
            held((tok, LANES), lambda i: (0, 0)),
            pl.BlockSpec((total, step), lambda i: (0, i)),
            pl.BlockSpec((tok, step), lambda i: (0, i)),
        ],
        out_specs=pl.BlockSpec((tok, step), lambda i: (0, i)),
        out_shape=jax.ShapeDtypeStruct((tok, width), BF16),
        scratch_shapes=[pltpu.VMEM((tok, total), BF16)],
        compiler_params=params(1),
        cost_estimate=cost(3e9, 10e6),
        name="home",
    )(tail, rows, grad)


def up_kernel(count, *refs):
    xs, (wa, wb), outs = refs[:count], refs[count : count + 2], refs[count + 2 :]
    for i in range(count):
        rows = xs[i][...]
        a = dot(rows, wa[...])
        b = dot(rows, wb[...])
        sig = jax.nn.sigmoid(a)
        outs[3 * i][...] = a * sig * b
        outs[3 * i + 1][...] = (b * sig * (1.0 + a * (1.0 - sig))).astype(BF16)
        outs[3 * i + 2][...] = (a * sig).astype(BF16)


def up(xs, wgu):
    count = len(xs)
    rows, width = xs[0].shape
    hidden = wgu.shape[1] // 2
    step = 256
    steps = hidden // step
    kinds = (F32, BF16, BF16) * count
    flat = pl.pallas_call(
        functools.partial(up_kernel, count),
        grid=(steps,),
        in_specs=[held((rows, width), lambda i: (0, 0))] * count
        + [
            pl.BlockSpec((width, step), lambda i: (0, i)),
            pl.BlockSpec((width, step), lambda i: (0, i + steps)),
        ],
        out_specs=[pl.BlockSpec((rows, step), lambda i: (0, i))] * (3 * count),
        out_shape=[jax.ShapeDtypeStruct((rows, hidden), kind) for kind in kinds],
        compiler_params=params(1),
        cost_estimate=cost(3e9, 10e6),
        name="up",
    )(*xs, wgu, wgu)
    return [flat[3 * i : 3 * i + 3] for i in range(count)]


def dh_kernel(count, *refs):
    ss, wd, outs = refs[:count], refs[count], refs[count + 1 :]
    for i in range(count):
        outs[i][...] = dot(ss[i][...], wd[...], 1, 1)


def dh_of(ss, wdown):
    count = len(ss)
    rows, width = ss[0].shape
    hidden = wdown.shape[0]
    step = 256
    return pl.pallas_call(
        functools.partial(dh_kernel, count),
        grid=(hidden // step,),
        in_specs=[held((rows, width), lambda i: (0, 0))] * count
        + [pl.BlockSpec((step, width), lambda i: (i, 0))],
        out_specs=[pl.BlockSpec((rows, step), lambda i: (0, i))] * count,
        out_shape=[jax.ShapeDtypeStruct((rows, hidden), F32)] * count,
        compiler_params=params(1),
        cost_estimate=cost(3e9, 10e6),
        name="dh",
    )(*ss, wdown)


def crossed(parts, j, cap):
    return jnp.concatenate([part[j * cap : (j + 1) * cap, :] for part in parts], axis=0)


def activations(rows, w, cols, hidden):
    a = dot(rows, w[:, cols])
    b = dot(rows, w[:, slice(hidden + cols.start, hidden + cols.stop)])
    sig = jax.nn.sigmoid(a)
    return a * sig * b, (b * sig * (1.0 + a * (1.0 - sig)), a * sig)


def tiles(total, step):
    return [slice(t * step, (t + 1) * step) for t in range(total // step)]


def gate_up_loads(w, w_v, sems, hidden):
    loads = []
    for t, cols in enumerate(tiles(hidden, 256)):
        for k in range(2):
            part = pl.ds(k * hidden + cols.start, 256)
            loads.append(begun(w.at[:, part], w_v.at[:, part], sems.at[t, k]))
    return loads


def send_rows(d_v, w_v, blocks, cap, to_ref, rows_v, out, sems):
    hidden = w_v.shape[1] // 2
    copies = []
    for t, cols in enumerate(tiles(w_v.shape[0], 512)):
        part = dot(d_v[0], w_v[cols, :hidden], 1, 1) + dot(d_v[1], w_v[cols, hidden:], 1, 1)
        for n, (i, j) in enumerate(blocks):
            rows_v[t, n] = part[n * cap : (n + 1) * cap].astype(BF16)
            target = out.at[to_ref[i * SIDE + j], :, cols]
            copies.append(begun(rows_v.at[t, n], target, sems.at[t, n]))
    return copies


def middle_kernel(cap, to_ref, *refs):
    w, wd, xs, ss, fs, dh0 = refs[0], refs[1], refs[2:4], refs[4:6], refs[6:8], refs[8]
    h_out, tail_out, dh_out, out, ds = refs[9:11], refs[11], refs[12], refs[13], refs[14:16]
    w_v, wd_v, x_v, s_v, h_v, f_v, dh_v, tail_v, dh_tail_v, d_v, e_v, rows_v = refs[16:28]
    w_sems, wd_sems, in_sems, out_sems, row_sems = refs[28:]
    rows = xs[0].shape[0]
    hidden = wd.shape[0]
    edge = 3 * cap - 8
    x_loads = [begun(xs[n], x_v.at[n], in_sems.at[n]) for n in range(2)]
    w_loads = gate_up_loads(w, w_v, w_sems, hidden)
    s_loads = [begun(ss[n], s_v.at[n], in_sems.at[2 + n]) for n in range(2)]
    wd_loads = [begun(wd.at[c, :], wd_v.at[c, :], wd_sems.at[t]) for t, c in enumerate(tiles(hidden, 256))]
    f_loads = [begun(fs[k], f_v.at[k, 0], in_sems.at[4 + k]) for k in range(2)]
    f_loads.append(begun(dh0, dh_v.at[0], in_sems.at[6]))
    for load in x_loads:
        load.wait()
    for t, cols in enumerate(tiles(hidden, 256)):
        for load in w_loads[2 * t : 2 * t + 2]:
            load.wait()
        for n in range(2):
            h, factors = activations(x_v[n], w_v, cols, hidden)
            h_v[n, :, cols] = h
            for k in range(2):
                f_v[k, n + 1, :, cols] = factors[k].astype(BF16)
    copies = [begun(h_v.at[n], h_out[n], out_sems.at[n]) for n in range(2)]
    for load in s_loads:
        load.wait()
    for t, cols in enumerate(tiles(hidden, 256)):
        wd_loads[t].wait()
        for n in range(2):
            dh_v[n + 1, :, cols] = dot(s_v[n], wd_v[cols, :], 1, 1)
    for load in f_loads:
        load.wait()
    for j in range(3):
        dh_tail_v[j * cap : (j + 1) * cap, :] = dh_v[j, 3 * cap :, :]
        for k in range(2):
            tail_v[k, j] = f_v[k, j, edge:, :]
    copies.append(begun(dh_tail_v, dh_out, out_sems.at[2]))
    copies.append(begun(tail_v, tail_out, out_sems.at[3]))
    for k in range(2):
        for cols in tiles(hidden, 256):
            chunks = [dh_v[j, :, cols] for j in range(3)]
            kept = []
            for i in range(3):
                factor = f_v[k, i, :, cols].astype(F32)[: 3 * cap]
                product = crossed(chunks, i, cap) * factor
                kept.append(product)
                whole = jnp.concatenate([product, jnp.zeros((cap, 256), F32)], axis=0)
                d_v[k, i * rows : (i + 1) * rows, cols] = whole.astype(BF16)
            e_v[k, :, cols] = jnp.concatenate(kept, axis=0).astype(BF16)
        copies.append(begun(d_v.at[k], ds[k].at[pl.ds(0, 3 * rows), :], out_sems.at[4 + k]))
    blocks = [(i, j) for i in range(3) for j in range(3)]
    copies += send_rows(e_v, w_v, blocks, cap, to_ref, rows_v, out, row_sems)
    for copy in copies:
        copy.wait()


def middle(to, wgu, wdown, xs, ss, factors, dh0, cap):
    rows, width = xs[0].shape
    hidden = wdown.shape[0]
    steps = width // 512
    h = jax.ShapeDtypeStruct((rows, hidden), F32)
    tail = jax.ShapeDtypeStruct((2, 3, cap + 8, hidden), BF16)
    dab = jax.ShapeDtypeStruct((SIDE * rows, hidden), BF16)
    slots = jax.ShapeDtypeStruct((SIDE * SIDE, cap, width), BF16)
    h1, h2, tails, dh_tail, slots, da, db = pl.pallas_call(
        functools.partial(middle_kernel, cap),
        in_specs=[SCALARS] + [FAR] * 9,
        out_specs=[FAR] * 7,
        out_shape=[h, h, tail, jax.ShapeDtypeStruct((3 * cap, hidden), F32), slots, dab, dab],
        scratch_shapes=[
            pltpu.VMEM((width, 2 * hidden), BF16),
            pltpu.VMEM((hidden, width), BF16),
            pltpu.VMEM((2, rows, width), BF16),
            pltpu.VMEM((2, rows, width), BF16),
            pltpu.VMEM((2, rows, hidden), F32),
            pltpu.VMEM((2, 3, rows, hidden), BF16),
            pltpu.VMEM((3, rows, hidden), F32),
            pltpu.VMEM((2, 3, cap + 8, hidden), BF16),
            pltpu.VMEM((3 * cap, hidden), F32),
            pltpu.VMEM((2, 3 * rows, hidden), BF16),
            pltpu.VMEM((2, 9 * cap, hidden), BF16),
            pltpu.VMEM((steps, 9, cap, 512), BF16),
            pltpu.SemaphoreType.DMA((hidden // 256, 2)),
            pltpu.SemaphoreType.DMA((hidden // 256,)),
            pltpu.SemaphoreType.DMA((7,)),
            pltpu.SemaphoreType.DMA((6,)),
            pltpu.SemaphoreType.DMA((steps, 9)),
        ],
        compiler_params=params(0),
        cost_estimate=cost(3e9, 10e6),
        name="middle",
    )(to, wgu, wdown, *xs, *ss, *factors, dh0)
    return [h1, h2], tails, dh_tail, slots, [da, db]


def last_x_kernel(cap, to_ref, *refs):
    w, x, hs, dh_tail = refs[0], refs[1], refs[2:5], refs[5]
    turned_out, tail_out, out, ds = refs[9], refs[10], refs[11], refs[12:14]
    w_v, x_v, h_v, f_v, dh_v, turned_v, d_v, e_v, rows_v = refs[14:23]
    w_sems, in_sems, out_sems, row_sems = refs[23:]
    rows = x.shape[0]
    hidden = w.shape[1] // 2
    edge = 3 * cap - 8
    x_load = begun(x, x_v, in_sems.at[0])
    w_loads = gate_up_loads(w, w_v, w_sems, hidden)
    loads = [begun(hs[n], h_v.at[n], in_sems.at[1 + n]) for n in range(3)]
    loads.append(begun(dh_tail, dh_v, in_sems.at[4]))
    x_load.wait()
    for t, cols in enumerate(tiles(hidden, 256)):
        for load in w_loads[2 * t : 2 * t + 2]:
            load.wait()
        h, factors = activations(x_v[...], w_v, cols, hidden)
        h_v[3, :, cols] = h
        for k in range(2):
            f_v[k, :, cols] = factors[k].astype(BF16)
    for load in loads:
        load.wait()
    copies = [begun(f_v.at[:, pl.ds(edge, cap + 8), :], tail_out, out_sems.at[0])]
    for cols in tiles(hidden, 256):
        parts = [h_v[n, :, cols] for n in range(SIDE)]
        whole = jnp.concatenate([crossed(parts, j, cap) for j in range(SIDE)], axis=0)
        turned_v[cols, :] = whole.T.astype(BF16)
        for k in range(2):
            product = dh_v[:, cols] * f_v[k, :, cols].astype(F32)[: 3 * cap]
            e_v[k, :, cols] = product.astype(BF16)
            whole = jnp.concatenate([product, jnp.zeros((cap, 256), F32)], axis=0)
            d_v[k, :, cols] = whole.astype(BF16)
    copies.append(begun(turned_v, turned_out, out_sems.at[1]))
    for k in range(2):
        copies.append(begun(d_v.at[k], ds[k].at[pl.ds(3 * rows, rows), :], out_sems.at[2 + k]))
    blocks = [(3, j) for j in range(3)]
    copies += send_rows(e_v, w_v, blocks, cap, to_ref, rows_v, out, row_sems)
    for copy in copies:
        copy.wait()


def last_x(to, wgu, x, hs, dh_tail, slots, ds, cap):
    rows, width = x.shape
    hidden = wgu.shape[1] // 2
    steps = width // 512
    turned_h, tail, slots, da, db = pl.pallas_call(
        functools.partial(last_x_kernel, cap),
        in_specs=[SCALARS] + [FAR] * 9,
        out_specs=[FAR] * 5,
        out_shape=[
            jax.ShapeDtypeStruct((hidden, SIDE * rows), BF16),
            jax.ShapeDtypeStruct((2, cap + 8, hidden), BF16),
        ]
        + [jax.ShapeDtypeStruct(a.shape, BF16) for a in (slots, *ds)],
        input_output_aliases={7: 2, 8: 3, 9: 4},
        scratch_shapes=[
            pltpu.VMEM((width, 2 * hidden), BF16),
            pltpu.VMEM((rows, width), BF16),
            pltpu.VMEM((SIDE, rows, hidden), F32),
            pltpu.VMEM((2, rows, hidden), BF16),
            pltpu.VMEM((3 * cap, hidden), F32),
            pltpu.VMEM((hidden, SIDE * rows), BF16),
            pltpu.VMEM((2, rows, hidden), BF16),
            pltpu.VMEM((2, 3 * cap, hidden), BF16),
            pltpu.VMEM((steps, 3, cap, 512), BF16),
            pltpu.SemaphoreType.DMA((hidden // 256, 2)),
            pltpu.SemaphoreType.DMA((5,)),
            pltpu.SemaphoreType.DMA((4,)),
            pltpu.SemaphoreType.DMA((steps, 3)),
        ],
        compiler_params=params(0),
        cost_estimate=cost(3e9, 10e6),
        name="last_x",
    )(to, wgu, x, *hs, dh_tail, slots, *ds)
    return turned_h, tail, slots, [da, db]


def last_s_kernel(cap, to_ref, *refs):
    s, wd, tails, tail, w = refs[:5]
    out, ds = refs[6], refs[7:9]
    s_v, wd_v, f_v, d_v, w_v, rows_v = refs[9:15]
    in_sems, wd_sems, w_sems, out_sems, row_sems = refs[15:]
    hidden = wd.shape[0]
    s_load = begun(s, s_v, in_sems.at[0])
    wd_loads = [begun(wd.at[c, :], wd_v.at[c, :], wd_sems.at[t]) for t, c in enumerate(tiles(hidden, 256))]
    loads = [begun(tails, f_v.at[:, pl.ds(0, 3)], in_sems.at[1])]
    loads.append(begun(tail, f_v.at[:, 3], in_sems.at[2]))
    parts = tiles(w.shape[0], 512)
    w_loads = [begun(w.at[c, :], w_v.at[c, :], w_sems.at[t]) for t, c in enumerate(parts)]
    s_load.wait()
    for t, cols in enumerate(tiles(hidden, 256)):
        wd_loads[t].wait()
        dh = dot(s_v[...], wd_v[cols, :], 1, 1)
        if t == 0:
            for load in loads:
                load.wait()
        for k in range(2):
            factors = [f_v[k, i, :, cols].astype(F32)[8:] for i in range(SIDE)]
            d_v[k, :, cols] = (dh * jnp.concatenate(factors, axis=0)).astype(BF16)
    copies = [begun(d_v.at[k], ds[k], out_sems.at[k]) for k in range(2)]
    for t, cols in enumerate(parts):
        w_loads[t].wait()
        part = dot(d_v[0], w_v[cols, :hidden], 1, 1) + dot(d_v[1], w_v[cols, hidden:], 1, 1)
        for i in range(SIDE):
            rows_v[t, i] = part[i * cap : (i + 1) * cap].astype(BF16)
            target = out.at[to_ref[i * SIDE + 3], :, cols]
            copies.append(begun(rows_v.at[t, i], target, row_sems.at[t, i]))
    for copy in copies:
        copy.wait()


def last_s(to, s, wdown, tails, tail, wgu, slots, cap):
    rows, width = s.shape
    hidden = wdown.shape[0]
    steps = width // 512
    dab = jax.ShapeDtypeStruct((rows, hidden), BF16)
    slots, da, db = pl.pallas_call(
        functools.partial(last_s_kernel, cap),
        in_specs=[SCALARS] + [FAR] * 6,
        out_specs=[FAR] * 3,
        out_shape=[jax.ShapeDtypeStruct(slots.shape, BF16), dab, dab],
        input_output_aliases={6: 0},
        scratch_shapes=[
            pltpu.VMEM((rows, width), BF16),
            pltpu.VMEM((hidden, width), BF16),
            pltpu.VMEM((2, SIDE, cap + 8, hidden), BF16),
            pltpu.VMEM((2, rows, hidden), BF16),
            pltpu.VMEM((width, 2 * hidden), BF16),
            pltpu.VMEM((steps, SIDE, cap, 512), BF16),
            pltpu.SemaphoreType.DMA((3,)),
            pltpu.SemaphoreType.DMA((hidden // 256,)),
            pltpu.SemaphoreType.DMA((steps,)),
            pltpu.SemaphoreType.DMA((2,)),
            pltpu.SemaphoreType.DMA((steps, SIDE)),
        ],
        compiler_params=params(0),
        cost_estimate=cost(1, 1),
        name="last_s",
    )(to, s, wdown, tails, tail, wgu, slots)
    return slots, [da, db]


AHEAD = (2, 1, 3)
SPOTS = (((0, 0), (1, 1)), ((2, 0), (0, 1)), ((1, 0), (2, 1)))


def put_halves(k, part, sent_v, wait_v, outs, sems):
    half = part.shape[0] // 2
    copies = []
    for side in range(2):
        out, row = SPOTS[k][side]
        piece = part[side * half : (side + 1) * half]
        if out == 2:
            staged = wait_v.at[row]
            staged[...] = piece
        else:
            staged = sent_v.at[out, row]
            staged[...] = piece.astype(BF16)
        target = outs[out].at[row * half : (row + 1) * half, :]
        copies.append(begun(staged, target, sems.at[k, side]))
    return copies


def ahead_of(place_ref, ahead, size):
    start = lax.rem(place_ref[0] + ahead, SIDE) * size
    return pl.ds(pl.multiple_of(start, size), size)


def message_outs(rows, cols):
    return [jax.ShapeDtypeStruct((rows, cols), kind) for kind in (BF16, BF16, F32)]


def message_scratch(rows, cols):
    return [
        pltpu.VMEM((2, 2, rows // 2, cols), BF16),
        pltpu.VMEM((2, rows // 2, cols), F32),
        pltpu.SemaphoreType.DMA((3, 2)),
    ]


def down_kernel(place_ref, *refs):
    turned, ss, outs = refs[0], refs[1:5], refs[5:8]
    s_v, turned_v, sent_v, wait_v, out_sems, s_sems, turned_sem = refs[8:]
    rows, width = ss[0].shape
    size = width // SIDE
    turned_load = begun(turned, turned_v, turned_sem)
    loads = []
    for k, ahead in enumerate(AHEAD):
        cols = ahead_of(place_ref, ahead, size)
        for j in range(SIDE):
            part = s_v.at[k, pl.ds(j * rows, rows), :]
            loads.append(begun(ss[j].at[:, cols], part, s_sems.at[k, j]))
    turned_load.wait()
    copies = []
    for k in range(3):
        for load in loads[4 * k : 4 * k + 4]:
            load.wait()
        copies += put_halves(k, dot(turned_v[...], s_v[k]), sent_v, wait_v, outs, out_sems)
    for copy in copies:
        copy.wait()


def down_parts(place, turned_h, ss):
    hidden, total = turned_h.shape
    rows, width = ss[0].shape
    quarter = width // SIDE
    return pl.pallas_call(
        down_kernel,
        in_specs=[SCALARS] + [FAR] * 5,
        out_specs=[FAR] * 3,
        out_shape=message_outs(hidden, quarter),
        scratch_shapes=[
            pltpu.VMEM((3, total, quarter), BF16),
            pltpu.VMEM((hidden, total), BF16),
        ]
        + message_scratch(hidden, quarter)
        + [pltpu.SemaphoreType.DMA((3, SIDE)), pltpu.SemaphoreType.DMA],
        compiler_params=params(0),
        cost_estimate=cost(1, 1),
        name="down_parts",
    )(place, turned_h, *ss)


def down_own_kernel(place_ref, *refs):
    turned_ref, ss, out = refs[0], refs[1:5], refs[5]
    out[...] = dot(turned_ref[...], jnp.concatenate([s[...] for s in ss], axis=0))


def down_own(place, turned_h, ss):
    hidden, total = turned_h.shape
    rows, width = ss[0].shape
    quarter = width // SIDE
    return pl.pallas_call(
        down_own_kernel,
        grid_spec=pltpu.PrefetchScalarGridSpec(
            num_scalar_prefetch=1,
            grid=(2,),
            in_specs=[pl.BlockSpec((hidden // 2, total), lambda i, place: (i, 0))]
            + [held((rows, quarter), lambda i, place: (0, place[0]))] * 4,
            out_specs=pl.BlockSpec((hidden // 2, quarter), lambda i, place: (i, 0)),
        ),
        out_shape=jax.ShapeDtypeStruct((hidden, quarter), F32),
        compiler_params=params(1),
        cost_estimate=cost(1, 1),
        name="down_own",
    )(place, turned_h, *ss)


def gate_up_kernel(cap, place_ref, *refs):
    early, late, xs, outs, ds = refs[:2], refs[2:4], refs[4:8], refs[8:11], refs[11:13]
    d_v, late_v, x_v, sent_v, wait_v, out_sems, d_sems, x_sems = refs[13:]
    rows, width = xs[0].shape
    size = width // SIDE
    loads = []
    for k in range(2):
        loads.append(begun(early[k], d_v.at[k], d_sems.at[0, k]))
        loads.append(begun(late[k], late_v.at[k], d_sems.at[1, k]))
    for k, ahead in enumerate(AHEAD):
        cols = ahead_of(place_ref, ahead, size)
        for i in range(SIDE):
            part = x_v.at[k, pl.ds(i * rows, rows), :]
            loads.append(begun(xs[i].at[:, cols], part, x_sems.at[k, i]))
    for load in loads[:4]:
        load.wait()
    edge = 3 * cap - 8
    copies = []
    for k in range(2):
        fresh = late_v[k].astype(F32)
        for i in range(SIDE):
            at = slice(i * rows + edge, (i + 1) * rows)
            old = d_v[k, at, :].astype(F32)[:8]
            new = fresh[i * cap : (i + 1) * cap]
            d_v[k, at, :] = jnp.concatenate([old, new], axis=0).astype(BF16)
        copies.append(begun(d_v.at[k], ds[k], d_sems.at[2, k]))
    for k in range(3):
        for load in loads[4 * k + 4 : 4 * k + 8]:
            load.wait()
        turned_x = x_v[k].T
        part = jnp.concatenate([dot(turned_x, d_v[0]), dot(turned_x, d_v[1])], axis=1)
        copies += put_halves(k, part, sent_v, wait_v, outs, out_sems)
    for copy in copies:
        copy.wait()


def gate_up_parts(place, early, late, xs, cap):
    rows, width = xs[0].shape
    total, hidden = early[0].shape
    quarter = width // SIDE
    out = jax.ShapeDtypeStruct((total, hidden), BF16)
    *messages, da, db = pl.pallas_call(
        functools.partial(gate_up_kernel, cap),
        in_specs=[SCALARS] + [FAR] * 8,
        out_specs=[FAR] * 5,
        out_shape=message_outs(quarter, 2 * hidden) + [out, out],
        scratch_shapes=[
            pltpu.VMEM((2, total, hidden), BF16),
            pltpu.VMEM((2, *late[0].shape), BF16),
            pltpu.VMEM((3, total, quarter), BF16),
        ]
        + message_scratch(quarter, 2 * hidden)
        + [pltpu.SemaphoreType.DMA((3, 2)), pltpu.SemaphoreType.DMA((3, SIDE))],
        compiler_params=params(0),
        cost_estimate=cost(1, 1),
        name="gate_up_parts",
    )(place, *early, *late, *xs)
    return messages, [da, db]


def gate_up_own_kernel(place_ref, *refs):
    xs, ds, out = refs[:4], refs[4:6], refs[6]
    rows = jnp.concatenate([x[...] for x in xs], axis=0).T
    out[...] = jnp.concatenate([dot(rows, d[...]) for d in ds], axis=1)


def gate_up_own(place, xs, ds):
    rows, width = xs[0].shape
    total, hidden = ds[0].shape
    half = width // SIDE // 2
    return pl.pallas_call(
        gate_up_own_kernel,
        grid_spec=pltpu.PrefetchScalarGridSpec(
            num_scalar_prefetch=1,
            grid=(2,),
            in_specs=[pl.BlockSpec((rows, half), lambda i, place: (0, 2 * place[0] + i))] * 4
            + [held((total, hidden), lambda i, place: (0, 0))] * 2,
            out_specs=pl.BlockSpec((half, 2 * hidden), lambda i, place: (i, 0)),
        ),
        out_shape=jax.ShapeDtypeStruct((2 * half, 2 * hidden), F32),
        compiler_params=params(1),
        cost_estimate=cost(200e9, 10e6),
        name="gate_up_own",
    )(place, *xs, *ds)


def around(first, axis):
    return [first] + [moved_along(first, axis, OFF[b]) for b in range(1, SIDE)]


def spread(outs, axis, work):
    near = [moved_along(outs[j], axis, OFF[j]) for j in (1, 2)]
    done = work(outs[0])
    far, near[0], near[1], *done = lax.optimization_barrier((outs[3], *near, *done))
    return [outs[0], *near, moved_along(far, axis, OFF[3])], done


def ring_first(first_up, first_down, wait):
    return moved_along(first_up, "edata", 1), moved_along(first_down, "edata", -1)


def ring_second(up1, down1, first_up, first_down, wait):
    half = wait.shape[0] // 2
    second_up = (wait[:half] + up1[:half].astype(F32)).astype(BF16)
    second_down = (wait[half:] + down1[half:].astype(F32)).astype(BF16)
    return moved_along(second_up, "edata", 1), moved_along(second_down, "edata", -1)


def ring_last(own, up1, down1, up2, down2):
    half = own.shape[0] // 2
    upper = own[:half] + down1[:half].astype(F32) + up2.astype(F32)
    lower = own[half:] + up1[half:].astype(F32) + down2.astype(F32)
    return jnp.concatenate([upper, lower], axis=0).astype(BF16)


def body(hidden_in, out_grad, routes, gates, w_gate_up, w_down):
    tok = hidden_in.shape[1]
    width = hidden_in.shape[2]
    topk = routes.shape[2]
    experts = lax.axis_size("expert")
    cap = min(tok, tok * topk * 9 // (8 * experts))
    wgu, wdown = w_gate_up[0, 0], w_down[0, 0]
    me = lax.axis_index("expert")
    mx, mz = me // SIDE, me % SIDE
    off = jnp.array(OFF, jnp.int32)
    eids_x = (mx * SIDE + (mz + off) % SIDE).astype(jnp.int32)
    eids_g = ((mx + off) % SIDE * SIDE + mz).astype(jnp.int32)
    to = ((mx - off)[None, :] % SIDE * SIDE + (mz - off)[:, None] % SIDE).reshape(-1)
    place = lax.axis_index("edata").astype(jnp.int32).reshape(1)

    xe, ge, tail = prep(routes[0].T, gates[0].T, hidden_in[0], out_grad[0], experts)
    xblocks = around(xe, "x")
    gblocks = around(ge, "z")
    def packed(eids, blocks, scale, name, which):
        picked = jnp.stack([eids[j] for j in which])
        return list(pack(picked, blocks, width, experts, cap, scale, name))

    xnear = packed(eids_x, xblocks, False, "pack_rows", (1, 2))
    xnear[0], gblocks[0] = lax.optimization_barrier((xnear[0], gblocks[0]))
    gnear = packed(eids_g, gblocks, True, "pack_scaled", (1, 2))
    xblocks[0], gnear[0] = lax.optimization_barrier((xblocks[0], gnear[0]))
    x0, xfar = packed(eids_x, xblocks, False, "pack_rows_rest", (0, 3))
    s0, sfar = packed(eids_g, gblocks, True, "pack_scaled_rest", (0, 3))
    xs, (h0, *factors) = spread([x0, *xnear, xfar], "z", lambda rows: up([rows], wgu)[0])
    ss, (dh0,) = spread([s0, *gnear, sfar], "x", lambda rows: dh_of([rows], wdown))
    to = to.astype(jnp.int32)
    hs, tails, dh_tail, slots, early = middle(
        to, wgu, wdown, xs[1:3], ss[1:3], factors, dh0, cap
    )
    turned_h, last_tail, slots, early = last_x(to, wgu, xs[3], [h0, *hs], dh_tail, slots, early, cap)
    last, slots, turned_h = lax.optimization_barrier((ss[3], slots, turned_h))
    ss = ss[:3] + [last]
    down = down_parts(place, turned_h, ss)
    last, *down = lax.optimization_barrier((last, *down))
    down_first = ring_first(*down)
    rows, late = last_s(to, last, wdown, tails, last_tail, wgu, slots, cap)
    returned = lax.all_to_all(rows, "expert", split_axis=0, concat_axis=0, tiled=True)
    rows, *later = lax.optimization_barrier((rows, *late, *down_first))
    late, down_first = later[:2], later[2:]
    gate_up, ds = gate_up_parts(place, early, late, xs, cap)
    gate_up_first = ring_first(*gate_up)
    wait, da, db, turned_h = lax.optimization_barrier((gate_up[2], *ds, turned_h))
    gate_up = [*gate_up[:2], wait]
    own_down = down_own(place, turned_h, ss)
    own_gate_up = gate_up_own(place, xs, [da, db])
    own_down, own_gate_up, *gate_up_first = lax.optimization_barrier(
        (own_down, own_gate_up, *gate_up_first)
    )
    down_second = ring_second(*down_first, *down)
    gate_up_second = ring_second(*gate_up_first, *gate_up)
    down_grad = ring_last(own_down, *down_first, *down_second)
    gate_up_grad = ring_last(own_gate_up, *gate_up_first, *gate_up_second)

    layer = home(tail, returned.reshape(experts * cap, width), out_grad[0], experts, cap)
    upstream = moved_along(layer, "section", -1)
    return (upstream[None], gate_up_grad[None, None], down_grad[None, None])


def solution(mesh):
    return jax.shard_map(
        body,
        mesh=mesh,
        in_specs=(
            P("section", ("edata", "expert"), None),
            P("section", ("edata", "expert"), None),
            P("section", ("edata", "expert"), None),
            P("section", ("edata", "expert"), None),
            P("section", "expert", None, None),
            P("section", "expert", None, None),
        ),
        out_specs=(
            P("section", ("edata", "expert"), None),
            P("section", "expert", "edata", None),
            P("section", "expert", None, "edata"),
        ),
        check_vma=False,
    )
```

```python
import functools

import jax
import jax.numpy as jnp
from jax import lax
from jax.experimental import pallas as pl
from jax.experimental.pallas import tpu as pltpu
from jax.sharding import PartitionSpec as P

BF16 = jnp.bfloat16
F32 = jnp.float32
OFF = (0, 1, 3, 2)
SIDE = 4
LANES = 128
MIB = 1024 * 1024


def params(steps):
    return pltpu.CompilerParams(
        vmem_limit_bytes=58 * MIB, dimension_semantics=("arbitrary",) * steps
    )


SCALARS = pl.BlockSpec(memory_space=pltpu.SMEM)
FAR = pl.BlockSpec(memory_space=pl.ANY)


def begun(src, dst, sem):
    copy = pltpu.make_async_copy(src, dst, sem)
    copy.start()
    return copy


def expert_at(me_ref, dx, dz):
    x, z = lax.div(me_ref[0], SIDE), lax.rem(me_ref[0], SIDE)
    return lax.rem(x + dx, SIDE) * SIDE + lax.rem(z + dz, SIDE)


def home_of(me_ref, i, j):
    return expert_at(me_ref, SIDE - OFF[j], SIDE - OFF[i])


def held(shape, index):
    return pl.BlockSpec(shape, index, pipeline_mode=pl.Buffered(1))


def cost(flops, moved):
    return pl.CostEstimate(flops=int(flops), bytes_accessed=int(moved), transcendentals=0)


def moved_along(block, axis, distance):
    if axis == "edata" or axis == "section":
        size = lax.axis_size(axis)
        return lax.ppermute(block, axis, [(i, (i + distance) % size) for i in range(size)])
    pairs = []
    for a in range(SIDE):
        for b in range(SIDE):
            if axis == "x":
                pairs.append((a * SIDE + b, (a + distance) % SIDE * SIDE + b))
            else:
                pairs.append((a * SIDE + b, a * SIDE + (b + distance) % SIDE))
    return lax.ppermute(block, "expert", pairs)


def iota(shape, dim):
    return lax.broadcasted_iota(jnp.int32, shape, dim)


def dot(a, b, da=1, db=0):
    return lax.dot_general(a, b, (((da,), (db,)), ((), ())), preferred_element_type=F32)


def prep_kernel(experts, routes_ref, gates_ref, x_ref, g_ref, xe_ref, ge_ref, tail_ref):
    tok, width = x_ref.shape
    topk = routes_ref.shape[0]
    expert = lax.rem(iota((LANES, tok), 0), experts)
    full = jnp.zeros((LANES, tok), F32)
    for k in range(topk):
        full += jnp.where(routes_ref[k : k + 1, :] == expert, gates_ref[k : k + 1, :], 0.0)
    full = full.T
    lane = iota((tok, LANES), 1)
    high = full.astype(BF16).astype(F32)
    rest = full - high
    middle = rest.astype(BF16).astype(F32)
    low = rest - middle
    piece = jnp.where(lane < 2 * experts, middle, jnp.where(lane < 3 * experts, low, 0.0))
    piece = jnp.where(lane < experts, high, piece).astype(BF16)
    for src, dst in ((x_ref, xe_ref), (g_ref, ge_ref)):
        dst[:, :width] = src[...]
        dst[:, width:] = piece
    tail_ref[...] = piece


def prep(routes, gates, x, g, experts):
    tok, width = x.shape
    shape = jax.ShapeDtypeStruct((tok, width + LANES), BF16)
    return pl.pallas_call(
        functools.partial(prep_kernel, experts),
        out_shape=(shape, shape, jax.ShapeDtypeStruct((tok, LANES), BF16)),
        compiler_params=params(0),
        name="prep",
    )(routes, gates, x, g)


def places(piece, experts, blocks):
    rows = piece.shape[0]
    tok = rows // blocks
    r, c = iota((rows, rows), 0), iota((rows, rows), 1)
    upto = jnp.where((c <= r) & (lax.div(c, tok) == lax.div(r, tok)), 1.0, 0.0).astype(BF16)
    lane = iota((rows, LANES), 1)
    mask = jnp.where((lane < experts) & (piece.astype(F32) > 0.0), 1.0, 0.0)
    return (dot(upto, mask.astype(BF16)) * mask).astype(BF16)


def pack_kernel(scale, experts, cap, steps_to, me_ref, *refs):
    blocks, outs = refs[:4], refs[4:-5]
    rows_v, packed_v, table_v, in_sems, out_sems = refs[-5:]
    count = len(outs)
    eids = [expert_at(me_ref, dx, dz) for dx, dz in steps_to]
    pair = 2 * cap
    tok, width = blocks[0].shape[0], outs[0].shape[1]
    steps, step = packed_v.shape[0], packed_v.shape[3]
    pieces = [slice(width, width + LANES)] + [slice(t * step, (t + 1) * step) for t in range(steps)]
    loads = []
    for n, cols in enumerate(pieces):
        for b in range(4):
            part = rows_v.at[b // 2, pl.ds(b % 2 * tok, tok), cols]
            loads.append(begun(blocks[b].at[:, cols], part, in_sems.at[n, b]))
    for load in loads[:4]:
        load.wait()
    lane = iota((pair, LANES), 1)
    second = jnp.where(iota((pair, 2 * tok), 1) >= tok, cap, 0)
    place = iota((pair, 2 * tok), 0) + 1 - second
    place = jnp.where(place > 0, place, -1).astype(F32)
    factors = []
    for p in range(2):
        piece = rows_v[p, :, width:]
        known = places(piece, experts, 2)
        for j in range(count):
            choose = jnp.where(lane == eids[j], 1.0, 0.0).astype(BF16)
            found = dot(choose, known, 1, 1)
            table = jnp.where(found == place, 1.0, 0.0).astype(BF16)
            table_v[p, j * pair : (j + 1) * pair, :] = table
            if scale:
                mine = (lax.rem(lane, experts) == eids[j]) & (lane < 3 * experts)
                gate = jnp.where(mine, dot(table, piece), 0.0)
                factors.append(jnp.sum(gate, axis=1, keepdims=True))
    stores = []
    for t in range(steps):
        for load in loads[4 * t + 4 : 4 * t + 8]:
            load.wait()
        for p in range(2):
            packed = dot(table_v[p], rows_v[p, :, pieces[t + 1]])
            for j in range(count):
                part = packed[j * pair : (j + 1) * pair]
                if scale:
                    part = part * factors[p * count + j]
                packed_v[t, j, p * pair : (p + 1) * pair, :] = part.astype(BF16)
        for j in range(count):
            target = outs[j].at[:, pieces[t + 1]]
            stores.append(begun(packed_v.at[t, j], target, out_sems.at[t, j]))
    for store in stores:
        store.wait()


def pack(me, blocks, width, experts, cap, steps_to, scale, name):
    count = len(steps_to)
    tok = blocks[0].shape[0]
    step = 512
    steps = width // step
    pair = 2 * cap
    out = jax.ShapeDtypeStruct((2 * pair, width), BF16)
    return pl.pallas_call(
        functools.partial(pack_kernel, scale, experts, cap, steps_to),
        in_specs=[SCALARS] + [FAR] * 4,
        out_specs=[FAR] * count,
        out_shape=[out] * count,
        scratch_shapes=[
            pltpu.VMEM((2, 2 * tok, width + LANES), BF16),
            pltpu.VMEM((steps, count, 2 * pair, step), BF16),
            pltpu.VMEM((2, count * pair, 2 * tok), BF16),
            pltpu.SemaphoreType.DMA((steps + 1, 4)),
            pltpu.SemaphoreType.DMA((steps, count)),
        ],
        compiler_params=params(0),
        cost_estimate=cost(3e9, 10e6),
        name=name,
    )(me, *blocks)


def home_kernel(experts, cap, tail_ref, rows_ref, grad_ref, out_ref, table_ref):
    tok = tail_ref.shape[0]
    total = experts * cap

    @pl.when(pl.program_id(0) == 0)
    def _():
        choose = jnp.where(iota((LANES, total), 0) == lax.div(iota((LANES, total), 1), cap), 1.0, 0.0)
        found = dot(places(tail_ref[...], experts, 1), choose.astype(BF16))
        place = lax.rem(iota((tok, total), 1), cap) + 1
        table_ref[...] = jnp.where(found == place.astype(F32), 1.0, 0.0).astype(BF16)

    total_grad = dot(table_ref[...], rows_ref[...]) + grad_ref[...].astype(F32)
    out_ref[...] = total_grad.astype(BF16)


def home(tail, rows, grad, experts, cap):
    tok, width = grad.shape
    step = 512
    total = experts * cap
    return pl.pallas_call(
        functools.partial(home_kernel, experts, cap),
        grid=(width // step,),
        in_specs=[
            held((tok, LANES), lambda i: (0, 0)),
            pl.BlockSpec((total, step), lambda i: (0, i)),
            pl.BlockSpec((tok, step), lambda i: (0, i)),
        ],
        out_specs=pl.BlockSpec((tok, step), lambda i: (0, i)),
        out_shape=jax.ShapeDtypeStruct((tok, width), BF16),
        scratch_shapes=[pltpu.VMEM((tok, total), BF16)],
        compiler_params=params(1),
        cost_estimate=cost(3e9, 10e6),
        name="home",
    )(tail, rows, grad)


def up_kernel(count, *refs):
    xs, (wa, wb), outs = refs[:count], refs[count : count + 2], refs[count + 2 :]
    for i in range(count):
        rows = xs[i][...]
        a = dot(rows, wa[...])
        b = dot(rows, wb[...])
        sig = jax.nn.sigmoid(a)
        outs[3 * i][...] = a * sig * b
        outs[3 * i + 1][...] = (b * sig * (1.0 + a * (1.0 - sig))).astype(BF16)
        outs[3 * i + 2][...] = (a * sig).astype(BF16)


def up(xs, wgu):
    count = len(xs)
    rows, width = xs[0].shape
    hidden = wgu.shape[1] // 2
    step = 256
    steps = hidden // step
    kinds = (F32, BF16, BF16) * count
    flat = pl.pallas_call(
        functools.partial(up_kernel, count),
        grid=(steps,),
        in_specs=[held((rows, width), lambda i: (0, 0))] * count
        + [
            pl.BlockSpec((width, step), lambda i: (0, i)),
            pl.BlockSpec((width, step), lambda i: (0, i + steps)),
        ],
        out_specs=[pl.BlockSpec((rows, step), lambda i: (0, i))] * (3 * count),
        out_shape=[jax.ShapeDtypeStruct((rows, hidden), kind) for kind in kinds],
        compiler_params=params(1),
        cost_estimate=cost(3e9, 10e6),
        name="up",
    )(*xs, wgu, wgu)
    return [flat[3 * i : 3 * i + 3] for i in range(count)]


def dh_kernel(count, *refs):
    ss, wd, outs = refs[:count], refs[count], refs[count + 1 :]
    for i in range(count):
        outs[i][...] = dot(ss[i][...], wd[...], 1, 1)


def dh_of(ss, wdown):
    count = len(ss)
    rows, width = ss[0].shape
    hidden = wdown.shape[0]
    step = 256
    return pl.pallas_call(
        functools.partial(dh_kernel, count),
        grid=(hidden // step,),
        in_specs=[held((rows, width), lambda i: (0, 0))] * count
        + [pl.BlockSpec((step, width), lambda i: (i, 0))],
        out_specs=[pl.BlockSpec((rows, step), lambda i: (0, i))] * count,
        out_shape=[jax.ShapeDtypeStruct((rows, hidden), F32)] * count,
        compiler_params=params(1),
        cost_estimate=cost(3e9, 10e6),
        name="dh",
    )(*ss, wdown)


def crossed(parts, j, cap):
    return jnp.concatenate([part[j * cap : (j + 1) * cap, :] for part in parts], axis=0)


def activations(rows, w, cols, hidden):
    a = dot(rows, w[:, cols])
    b = dot(rows, w[:, slice(hidden + cols.start, hidden + cols.stop)])
    sig = jax.nn.sigmoid(a)
    return a * sig * b, (b * sig * (1.0 + a * (1.0 - sig)), a * sig)


def tiles(total, step):
    return [slice(t * step, (t + 1) * step) for t in range(total // step)]


def gate_up_loads(w, w_v, sems, hidden):
    loads = []
    for t, cols in enumerate(tiles(hidden, 256)):
        for k in range(2):
            part = pl.ds(k * hidden + cols.start, 256)
            loads.append(begun(w.at[:, part], w_v.at[:, part], sems.at[t, k]))
    return loads


def send_rows(d_v, w_v, blocks, cap, me_ref, rows_v, out, sems):
    hidden = w_v.shape[1] // 2
    copies = []
    for t, cols in enumerate(tiles(w_v.shape[0], 512)):
        part = dot(d_v[0], w_v[cols, :hidden], 1, 1) + dot(d_v[1], w_v[cols, hidden:], 1, 1)
        for n, (i, j) in enumerate(blocks):
            rows_v[t, n] = part[n * cap : (n + 1) * cap].astype(BF16)
            target = out.at[home_of(me_ref, i, j), :, cols]
            copies.append(begun(rows_v.at[t, n], target, sems.at[t, n]))
    return copies


def middle_kernel(cap, me_ref, *refs):
    w, wd, xs, ss, fs, dh0 = refs[0], refs[1], refs[2:4], refs[4:6], refs[6:8], refs[8]
    h_out, tail_out, dh_out, out, ds = refs[9:11], refs[11], refs[12], refs[13], refs[14:16]
    w_v, wd_v, x_v, s_v, h_v, f_v, dh_v, tail_v, dh_tail_v, d_v, e_v, rows_v = refs[16:28]
    w_sems, wd_sems, in_sems, out_sems, row_sems = refs[28:]
    rows = xs[0].shape[0]
    hidden = wd.shape[0]
    edge = 3 * cap - 8
    x_loads = [begun(xs[n], x_v.at[n], in_sems.at[n]) for n in range(2)]
    w_loads = gate_up_loads(w, w_v, w_sems, hidden)
    s_loads = [begun(ss[n], s_v.at[n], in_sems.at[2 + n]) for n in range(2)]
    wd_loads = [begun(wd.at[c, :], wd_v.at[c, :], wd_sems.at[t]) for t, c in enumerate(tiles(hidden, 256))]
    f_loads = [begun(fs[k], f_v.at[k, 0], in_sems.at[4 + k]) for k in range(2)]
    f_loads.append(begun(dh0, dh_v.at[0], in_sems.at[6]))
    for load in x_loads:
        load.wait()
    for t, cols in enumerate(tiles(hidden, 256)):
        for load in w_loads[2 * t : 2 * t + 2]:
            load.wait()
        for n in range(2):
            h, factors = activations(x_v[n], w_v, cols, hidden)
            h_v[n, :, cols] = h
            for k in range(2):
                f_v[k, n + 1, :, cols] = factors[k].astype(BF16)
    copies = [begun(h_v.at[n], h_out[n], out_sems.at[n]) for n in range(2)]
    for load in s_loads:
        load.wait()
    for t, cols in enumerate(tiles(hidden, 256)):
        wd_loads[t].wait()
        for n in range(2):
            dh_v[n + 1, :, cols] = dot(s_v[n], wd_v[cols, :], 1, 1)
    for load in f_loads:
        load.wait()
    for j in range(3):
        dh_tail_v[j * cap : (j + 1) * cap, :] = dh_v[j, 3 * cap :, :]
        for k in range(2):
            tail_v[k, j] = f_v[k, j, edge:, :]
    copies.append(begun(dh_tail_v, dh_out, out_sems.at[2]))
    copies.append(begun(tail_v, tail_out, out_sems.at[3]))
    for k in range(2):
        for cols in tiles(hidden, 256):
            chunks = [dh_v[j, :, cols] for j in range(3)]
            kept = []
            for i in range(3):
                factor = f_v[k, i, :, cols].astype(F32)[: 3 * cap]
                product = crossed(chunks, i, cap) * factor
                kept.append(product)
                whole = jnp.concatenate([product, jnp.zeros((cap, 256), F32)], axis=0)
                d_v[k, i * rows : (i + 1) * rows, cols] = whole.astype(BF16)
            e_v[k, :, cols] = jnp.concatenate(kept, axis=0).astype(BF16)
        copies.append(begun(d_v.at[k], ds[k].at[pl.ds(0, 3 * rows), :], out_sems.at[4 + k]))
    blocks = [(i, j) for i in range(3) for j in range(3)]
    copies += send_rows(e_v, w_v, blocks, cap, me_ref, rows_v, out, row_sems)
    for copy in copies:
        copy.wait()


def middle(me, wgu, wdown, xs, ss, factors, dh0, cap):
    rows, width = xs[0].shape
    hidden = wdown.shape[0]
    steps = width // 512
    h = jax.ShapeDtypeStruct((rows, hidden), F32)
    tail = jax.ShapeDtypeStruct((2, 3, cap + 8, hidden), BF16)
    dab = jax.ShapeDtypeStruct((SIDE * rows, hidden), BF16)
    slots = jax.ShapeDtypeStruct((SIDE * SIDE, cap, width), BF16)
    h1, h2, tails, dh_tail, slots, da, db = pl.pallas_call(
        functools.partial(middle_kernel, cap),
        in_specs=[SCALARS] + [FAR] * 9,
        out_specs=[FAR] * 7,
        out_shape=[h, h, tail, jax.ShapeDtypeStruct((3 * cap, hidden), F32), slots, dab, dab],
        scratch_shapes=[
            pltpu.VMEM((width, 2 * hidden), BF16),
            pltpu.VMEM((hidden, width), BF16),
            pltpu.VMEM((2, rows, width), BF16),
            pltpu.VMEM((2, rows, width), BF16),
            pltpu.VMEM((2, rows, hidden), F32),
            pltpu.VMEM((2, 3, rows, hidden), BF16),
            pltpu.VMEM((3, rows, hidden), F32),
            pltpu.VMEM((2, 3, cap + 8, hidden), BF16),
            pltpu.VMEM((3 * cap, hidden), F32),
            pltpu.VMEM((2, 3 * rows, hidden), BF16),
            pltpu.VMEM((2, 9 * cap, hidden), BF16),
            pltpu.VMEM((steps, 9, cap, 512), BF16),
            pltpu.SemaphoreType.DMA((hidden // 256, 2)),
            pltpu.SemaphoreType.DMA((hidden // 256,)),
            pltpu.SemaphoreType.DMA((7,)),
            pltpu.SemaphoreType.DMA((6,)),
            pltpu.SemaphoreType.DMA((steps, 9)),
        ],
        compiler_params=params(0),
        cost_estimate=cost(3e9, 10e6),
        name="middle",
    )(me, wgu, wdown, *xs, *ss, *factors, dh0)
    return [h1, h2], tails, dh_tail, slots, [da, db]


def last_x_kernel(cap, me_ref, *refs):
    w, x, hs, dh_tail = refs[0], refs[1], refs[2:5], refs[5]
    turned_out, tail_out, out, ds = refs[9], refs[10], refs[11], refs[12:14]
    w_v, x_v, h_v, f_v, dh_v, turned_v, d_v, e_v, rows_v = refs[14:23]
    w_sems, in_sems, out_sems, row_sems = refs[23:]
    rows = x.shape[0]
    hidden = w.shape[1] // 2
    edge = 3 * cap - 8
    x_load = begun(x, x_v, in_sems.at[0])
    w_loads = gate_up_loads(w, w_v, w_sems, hidden)
    loads = [begun(hs[n], h_v.at[n], in_sems.at[1 + n]) for n in range(3)]
    loads.append(begun(dh_tail, dh_v, in_sems.at[4]))
    x_load.wait()
    for t, cols in enumerate(tiles(hidden, 256)):
        for load in w_loads[2 * t : 2 * t + 2]:
            load.wait()
        h, factors = activations(x_v[...], w_v, cols, hidden)
        h_v[3, :, cols] = h
        for k in range(2):
            f_v[k, :, cols] = factors[k].astype(BF16)
    for load in loads:
        load.wait()
    copies = [begun(f_v.at[:, pl.ds(edge, cap + 8), :], tail_out, out_sems.at[0])]
    for cols in tiles(hidden, 256):
        parts = [h_v[n, :, cols] for n in range(SIDE)]
        whole = jnp.concatenate([crossed(parts, j, cap) for j in range(SIDE)], axis=0)
        turned_v[cols, :] = whole.T.astype(BF16)
        for k in range(2):
            product = dh_v[:, cols] * f_v[k, :, cols].astype(F32)[: 3 * cap]
            e_v[k, :, cols] = product.astype(BF16)
            whole = jnp.concatenate([product, jnp.zeros((cap, 256), F32)], axis=0)
            d_v[k, :, cols] = whole.astype(BF16)
    copies.append(begun(turned_v, turned_out, out_sems.at[1]))
    for k in range(2):
        copies.append(begun(d_v.at[k], ds[k].at[pl.ds(3 * rows, rows), :], out_sems.at[2 + k]))
    blocks = [(3, j) for j in range(3)]
    copies += send_rows(e_v, w_v, blocks, cap, me_ref, rows_v, out, row_sems)
    for copy in copies:
        copy.wait()


def last_x(me, wgu, x, hs, dh_tail, slots, ds, cap):
    rows, width = x.shape
    hidden = wgu.shape[1] // 2
    steps = width // 512
    turned_h, tail, slots, da, db = pl.pallas_call(
        functools.partial(last_x_kernel, cap),
        in_specs=[SCALARS] + [FAR] * 9,
        out_specs=[FAR] * 5,
        out_shape=[
            jax.ShapeDtypeStruct((hidden, SIDE * rows), BF16),
            jax.ShapeDtypeStruct((2, cap + 8, hidden), BF16),
        ]
        + [jax.ShapeDtypeStruct(a.shape, BF16) for a in (slots, *ds)],
        input_output_aliases={7: 2, 8: 3, 9: 4},
        scratch_shapes=[
            pltpu.VMEM((width, 2 * hidden), BF16),
            pltpu.VMEM((rows, width), BF16),
            pltpu.VMEM((SIDE, rows, hidden), F32),
            pltpu.VMEM((2, rows, hidden), BF16),
            pltpu.VMEM((3 * cap, hidden), F32),
            pltpu.VMEM((hidden, SIDE * rows), BF16),
            pltpu.VMEM((2, rows, hidden), BF16),
            pltpu.VMEM((2, 3 * cap, hidden), BF16),
            pltpu.VMEM((steps, 3, cap, 512), BF16),
            pltpu.SemaphoreType.DMA((hidden // 256, 2)),
            pltpu.SemaphoreType.DMA((5,)),
            pltpu.SemaphoreType.DMA((4,)),
            pltpu.SemaphoreType.DMA((steps, 3)),
        ],
        compiler_params=params(0),
        cost_estimate=cost(3e9, 10e6),
        name="last_x",
    )(me, wgu, x, *hs, dh_tail, slots, *ds)
    return turned_h, tail, slots, [da, db]


AHEAD = (2, 1, 3)
SPOTS = (((0, 0), (1, 1)), ((2, 0), (0, 1)), ((1, 0), (2, 1)))


def put_halves(k, part, sent_v, wait_v, outs, sems):
    half = part.shape[0] // 2
    copies = []
    for side in range(2):
        out, row = SPOTS[k][side]
        piece = part[side * half : (side + 1) * half]
        if out == 2:
            staged = wait_v.at[row]
            staged[...] = piece
        else:
            staged = sent_v.at[out, row]
            staged[...] = piece.astype(BF16)
        target = outs[out].at[row * half : (row + 1) * half, :]
        copies.append(begun(staged, target, sems.at[k, side]))
    return copies


def ahead_of(place_ref, ahead, size):
    start = lax.rem(place_ref[0] + ahead, SIDE) * size
    return pl.ds(pl.multiple_of(start, size), size)


def message_outs(rows, cols):
    return [jax.ShapeDtypeStruct((rows, cols), kind) for kind in (BF16, BF16, F32)]


def message_scratch(rows, cols):
    return [
        pltpu.VMEM((2, 2, rows // 2, cols), BF16),
        pltpu.VMEM((2, rows // 2, cols), F32),
        pltpu.SemaphoreType.DMA((3, 2)),
    ]


def last_s_kernel(cap, me_ref, place_ref, *refs):
    turned, ss, wd, tails, tail, w = refs[0], refs[1:5], refs[5], refs[6], refs[7], refs[8]
    outs, out, ds = refs[10:13], refs[13], refs[14:16]
    turned_v, q_v, s_v, wd_v, f_v, d_v, w_v, rows_v = refs[16:24]
    sent_v, wait_v, message_sems, in_sems, q_sems, wd_sems, w_sems, out_sems, row_sems = refs[24:]
    rows, width = ss[0].shape
    hidden = wd.shape[0]
    turned_load = begun(turned, turned_v, in_sems.at[0])
    q_loads = []
    for k, ahead in enumerate(AHEAD):
        cols = ahead_of(place_ref, ahead, width // SIDE)
        for j in range(SIDE):
            part = q_v.at[k, pl.ds(j * rows, rows), :]
            q_loads.append(begun(ss[j].at[:, cols], part, q_sems.at[k, j]))
    s_load = begun(ss[3], s_v, in_sems.at[1])
    wd_loads = [begun(wd.at[c, :], wd_v.at[c, :], wd_sems.at[t]) for t, c in enumerate(tiles(hidden, 256))]
    loads = [begun(tails, f_v.at[:, pl.ds(0, 3)], in_sems.at[2])]
    loads.append(begun(tail, f_v.at[:, 3], in_sems.at[3]))
    parts = tiles(w.shape[0], 512)
    w_loads = [begun(w.at[c, :], w_v.at[c, :], w_sems.at[t]) for t, c in enumerate(parts)]
    turned_load.wait()
    copies = []
    for k in range(3):
        for load in q_loads[4 * k : 4 * k + 4]:
            load.wait()
        part = dot(turned_v[...], q_v[k])
        copies += put_halves(k, part, sent_v, wait_v, outs, message_sems)
    s_load.wait()
    for load in loads:
        load.wait()
    for t, cols in enumerate(tiles(hidden, 256)):
        wd_loads[t].wait()
        dh = dot(s_v[...], wd_v[cols, :], 1, 1)
        for k in range(2):
            factors = [f_v[k, i, :, cols].astype(F32)[8:] for i in range(SIDE)]
            d_v[k, :, cols] = (dh * jnp.concatenate(factors, axis=0)).astype(BF16)
    copies += [begun(d_v.at[k], ds[k], out_sems.at[k]) for k in range(2)]
    for t, cols in enumerate(parts):
        w_loads[t].wait()
        part = dot(d_v[0], w_v[cols, :hidden], 1, 1) + dot(d_v[1], w_v[cols, hidden:], 1, 1)
        for i in range(SIDE):
            rows_v[t, i] = part[i * cap : (i + 1) * cap].astype(BF16)
            target = out.at[home_of(me_ref, i, 3), :, cols]
            copies.append(begun(rows_v.at[t, i], target, row_sems.at[t, i]))
    for copy in copies:
        copy.wait()


def last_s(me, place, turned_h, ss, wdown, tails, tail, wgu, slots, cap):
    rows, width = ss[0].shape
    hidden, total = turned_h.shape
    quarter = width // SIDE
    steps = width // 512
    dab = jax.ShapeDtypeStruct((rows, hidden), BF16)
    *down, slots, da, db = pl.pallas_call(
        functools.partial(last_s_kernel, cap),
        in_specs=[SCALARS] * 2 + [FAR] * 10,
        out_specs=[FAR] * 6,
        out_shape=message_outs(hidden, quarter)
        + [jax.ShapeDtypeStruct(slots.shape, BF16), dab, dab],
        input_output_aliases={11: 3},
        scratch_shapes=[
            pltpu.VMEM((hidden, total), BF16),
            pltpu.VMEM((3, total, quarter), BF16),
            pltpu.VMEM((rows, width), BF16),
            pltpu.VMEM((hidden, width), BF16),
            pltpu.VMEM((2, SIDE, cap + 8, hidden), BF16),
            pltpu.VMEM((2, rows, hidden), BF16),
            pltpu.VMEM((width, 2 * hidden), BF16),
            pltpu.VMEM((steps, SIDE, cap, 512), BF16),
        ]
        + message_scratch(hidden, quarter)
        + [
            pltpu.SemaphoreType.DMA((4,)),
            pltpu.SemaphoreType.DMA((3, SIDE)),
            pltpu.SemaphoreType.DMA((hidden // 256,)),
            pltpu.SemaphoreType.DMA((steps,)),
            pltpu.SemaphoreType.DMA((2,)),
            pltpu.SemaphoreType.DMA((steps, SIDE)),
        ],
        compiler_params=params(0),
        cost_estimate=cost(1, 1),
        name="last_s",
    )(me, place, turned_h, *ss, wdown, tails, tail, wgu, slots)
    return down, slots, [da, db]


def down_own_kernel(place_ref, *refs):
    turned_ref, ss, out = refs[0], refs[1:5], refs[5]
    out[...] = dot(turned_ref[...], jnp.concatenate([s[...] for s in ss], axis=0))


def down_own(place, turned_h, ss):
    hidden, total = turned_h.shape
    rows, width = ss[0].shape
    quarter = width // SIDE
    return pl.pallas_call(
        down_own_kernel,
        grid_spec=pltpu.PrefetchScalarGridSpec(
            num_scalar_prefetch=1,
            grid=(2,),
            in_specs=[pl.BlockSpec((hidden // 2, total), lambda i, place: (i, 0))]
            + [held((rows, quarter), lambda i, place: (0, place[0]))] * 4,
            out_specs=pl.BlockSpec((hidden // 2, quarter), lambda i, place: (i, 0)),
        ),
        out_shape=jax.ShapeDtypeStruct((hidden, quarter), F32),
        compiler_params=params(1),
        cost_estimate=cost(1, 1),
        name="down_own",
    )(place, turned_h, *ss)


def gate_up_kernel(cap, place_ref, *refs):
    early, late, xs, outs, ds = refs[:2], refs[2:4], refs[4:8], refs[8:11], refs[11:13]
    d_v, late_v, x_v, sent_v, wait_v, out_sems, d_sems, x_sems = refs[13:]
    rows, width = xs[0].shape
    size = width // SIDE
    loads = []
    for k in range(2):
        loads.append(begun(early[k], d_v.at[k], d_sems.at[0, k]))
        loads.append(begun(late[k], late_v.at[k], d_sems.at[1, k]))
    for k, ahead in enumerate(AHEAD):
        cols = ahead_of(place_ref, ahead, size)
        for i in range(SIDE):
            part = x_v.at[k, pl.ds(i * rows, rows), :]
            loads.append(begun(xs[i].at[:, cols], part, x_sems.at[k, i]))
    for load in loads[:4]:
        load.wait()
    edge = 3 * cap - 8
    copies = []
    for k in range(2):
        fresh = late_v[k].astype(F32)
        for i in range(SIDE):
            at = slice(i * rows + edge, (i + 1) * rows)
            old = d_v[k, at, :].astype(F32)[:8]
            new = fresh[i * cap : (i + 1) * cap]
            d_v[k, at, :] = jnp.concatenate([old, new], axis=0).astype(BF16)
        copies.append(begun(d_v.at[k], ds[k], d_sems.at[2, k]))
    for k in range(3):
        for load in loads[4 * k + 4 : 4 * k + 8]:
            load.wait()
        turned_x = x_v[k].T
        part = jnp.concatenate([dot(turned_x, d_v[0]), dot(turned_x, d_v[1])], axis=1)
        copies += put_halves(k, part, sent_v, wait_v, outs, out_sems)
    for copy in copies:
        copy.wait()


def gate_up_parts(place, early, late, xs, cap):
    rows, width = xs[0].shape
    total, hidden = early[0].shape
    quarter = width // SIDE
    out = jax.ShapeDtypeStruct((total, hidden), BF16)
    *messages, da, db = pl.pallas_call(
        functools.partial(gate_up_kernel, cap),
        in_specs=[SCALARS] + [FAR] * 8,
        out_specs=[FAR] * 5,
        out_shape=message_outs(quarter, 2 * hidden) + [out, out],
        scratch_shapes=[
            pltpu.VMEM((2, total, hidden), BF16),
            pltpu.VMEM((2, *late[0].shape), BF16),
            pltpu.VMEM((3, total, quarter), BF16),
        ]
        + message_scratch(quarter, 2 * hidden)
        + [pltpu.SemaphoreType.DMA((3, 2)), pltpu.SemaphoreType.DMA((3, SIDE))],
        compiler_params=params(0),
        cost_estimate=cost(1, 1),
        name="gate_up_parts",
    )(place, *early, *late, *xs)
    return messages, [da, db]


def gate_up_own_kernel(place_ref, *refs):
    xs, ds, out = refs[:4], refs[4:6], refs[6]
    rows = jnp.concatenate([x[...] for x in xs], axis=0).T
    out[...] = jnp.concatenate([dot(rows, d[...]) for d in ds], axis=1)


def gate_up_own(place, xs, ds):
    rows, width = xs[0].shape
    total, hidden = ds[0].shape
    half = width // SIDE // 2
    return pl.pallas_call(
        gate_up_own_kernel,
        grid_spec=pltpu.PrefetchScalarGridSpec(
            num_scalar_prefetch=1,
            grid=(2,),
            in_specs=[pl.BlockSpec((rows, half), lambda i, place: (0, 2 * place[0] + i))] * 4
            + [held((total, hidden), lambda i, place: (0, 0))] * 2,
            out_specs=pl.BlockSpec((half, 2 * hidden), lambda i, place: (i, 0)),
        ),
        out_shape=jax.ShapeDtypeStruct((2 * half, 2 * hidden), F32),
        compiler_params=params(1),
        cost_estimate=cost(200e9, 10e6),
        name="gate_up_own",
    )(place, *xs, *ds)


def around(first, axis):
    return [first] + [moved_along(first, axis, OFF[b]) for b in range(1, SIDE)]


def spread(outs, axis, work):
    near = [moved_along(outs[j], axis, OFF[j]) for j in (1, 2)]
    done = work(outs[0])
    far, near[0], near[1], *done = lax.optimization_barrier((outs[3], *near, *done))
    return [outs[0], *near, moved_along(far, axis, OFF[3])], done


def ring_first(first_up, first_down, wait):
    return moved_along(first_up, "edata", 1), moved_along(first_down, "edata", -1)


def ring_second(up1, down1, first_up, first_down, wait):
    half = wait.shape[0] // 2
    second_up = (wait[:half] + up1[:half].astype(F32)).astype(BF16)
    second_down = (wait[half:] + down1[half:].astype(F32)).astype(BF16)
    return moved_along(second_up, "edata", 1), moved_along(second_down, "edata", -1)


def ring_own(own, up1, down1):
    half = own.shape[0] // 2
    return own + jnp.concatenate([down1[:half], up1[half:]], axis=0).astype(F32)


def ring_last(total, up2, down2):
    return (total + jnp.concatenate([up2, down2], axis=0).astype(F32)).astype(BF16)


def body(hidden_in, out_grad, routes, gates, w_gate_up, w_down):
    tok = hidden_in.shape[1]
    width = hidden_in.shape[2]
    topk = routes.shape[2]
    experts = lax.axis_size("expert")
    cap = min(tok, tok * topk * 9 // (8 * experts))
    wgu, wdown = w_gate_up[0, 0], w_down[0, 0]
    me = lax.axis_index("expert").astype(jnp.int32).reshape(1)
    place = lax.axis_index("edata").astype(jnp.int32).reshape(1)

    xe, ge, tail = prep(routes[0].T, gates[0].T, hidden_in[0], out_grad[0], experts)
    xblocks = around(xe, "x")
    gblocks = around(ge, "z")
    def packed(blocks, scale, name, which):
        steps_to = tuple((OFF[j], 0) if scale else (0, OFF[j]) for j in which)
        return list(pack(me, blocks, width, experts, cap, steps_to, scale, name))

    xnear = packed(xblocks, False, "pack_rows", (1, 2))
    xnear[0], gblocks[0] = lax.optimization_barrier((xnear[0], gblocks[0]))
    gnear = packed(gblocks, True, "pack_scaled", (1, 2))
    xblocks[0], gnear[0] = lax.optimization_barrier((xblocks[0], gnear[0]))
    x0, xfar = packed(xblocks, False, "pack_rows_rest", (0, 3))
    s0, sfar = packed(gblocks, True, "pack_scaled_rest", (0, 3))
    xs, (h0, *factors) = spread([x0, *xnear, xfar], "z", lambda rows: up([rows], wgu)[0])
    ss, (dh0,) = spread([s0, *gnear, sfar], "x", lambda rows: dh_of([rows], wdown))
    hs, tails, dh_tail, slots, early = middle(
        me, wgu, wdown, xs[1:3], ss[1:3], factors, dh0, cap
    )
    turned_h, last_tail, slots, early = last_x(
        me, wgu, xs[3], [h0, *hs], dh_tail, slots, early, cap
    )
    last, slots, turned_h = lax.optimization_barrier((ss[3], slots, turned_h))
    ss = ss[:3] + [last]
    down, rows, late = last_s(me, place, turned_h, ss, wdown, tails, last_tail, wgu, slots, cap)
    down_first = ring_first(*down)
    returned = lax.all_to_all(rows, "expert", split_axis=0, concat_axis=0, tiled=True)
    rows, *late = lax.optimization_barrier((rows, *late))
    gate_up, ds = gate_up_parts(place, early, late, xs, cap)
    gate_up[0], gate_up[1], *down_first = lax.optimization_barrier((gate_up[0], gate_up[1], *down_first))
    gate_up_first = ring_first(*gate_up)
    wait, da, db, turned_h = lax.optimization_barrier((gate_up[2], *ds, turned_h))
    gate_up = [*gate_up[:2], wait]
    own_down = down_own(place, turned_h, ss)
    own_gate_up = gate_up_own(place, xs, [da, db])
    own_down, own_gate_up, *gate_up_first = lax.optimization_barrier(
        (own_down, own_gate_up, *gate_up_first)
    )
    down_second = ring_second(*down_first, *down)
    gate_up_second = ring_second(*gate_up_first, *gate_up)
    down_grad = ring_last(ring_own(own_down, *down_first), *down_second)
    gate_up_grad = ring_last(ring_own(own_gate_up, *gate_up_first), *gate_up_second)

    layer = home(tail, returned.reshape(experts * cap, width), out_grad[0], experts, cap)
    upstream = moved_along(layer, "section", -1)
    return (upstream[None], gate_up_grad[None, None], down_grad[None, None])


def solution(mesh):
    return jax.shard_map(
        body,
        mesh=mesh,
        in_specs=(
            P("section", ("edata", "expert"), None),
            P("section", ("edata", "expert"), None),
            P("section", ("edata", "expert"), None),
            P("section", ("edata", "expert"), None),
            P("section", "expert", None, None),
            P("section", "expert", None, None),
        ),
        out_specs=(
            P("section", ("edata", "expert"), None),
            P("section", "expert", "edata", None),
            P("section", "expert", None, "edata"),
        ),
        check_vma=False,
    )
```

```python
import functools

import jax
import jax.numpy as jnp
from jax import lax
from jax.experimental import pallas as pl
from jax.experimental.pallas import tpu as pltpu
from jax.sharding import PartitionSpec as P

BF16 = jnp.bfloat16
F32 = jnp.float32
OFF = (0, 1, 3, 2)
SIDE = 4
LANES = 128
MIB = 1024 * 1024


def params(steps):
    return pltpu.CompilerParams(
        vmem_limit_bytes=58 * MIB, dimension_semantics=("arbitrary",) * steps
    )


SCALARS = pl.BlockSpec(memory_space=pltpu.SMEM)
FAR = pl.BlockSpec(memory_space=pl.ANY)


def begun(src, dst, sem):
    copy = pltpu.make_async_copy(src, dst, sem)
    copy.start()
    return copy


def expert_at(me_ref, dx, dz):
    x, z = lax.div(me_ref[0], SIDE), lax.rem(me_ref[0], SIDE)
    return lax.rem(x + dx, SIDE) * SIDE + lax.rem(z + dz, SIDE)


def home_of(me_ref, i, j):
    return expert_at(me_ref, SIDE - OFF[j], SIDE - OFF[i])


def held(shape, index):
    return pl.BlockSpec(shape, index, pipeline_mode=pl.Buffered(1))


def cost(flops, moved):
    return pl.CostEstimate(flops=int(flops), bytes_accessed=int(moved), transcendentals=0)


def moved_along(block, axis, distance):
    if axis == "edata" or axis == "section":
        size = lax.axis_size(axis)
        return lax.ppermute(block, axis, [(i, (i + distance) % size) for i in range(size)])
    pairs = []
    for a in range(SIDE):
        for b in range(SIDE):
            if axis == "x":
                pairs.append((a * SIDE + b, (a + distance) % SIDE * SIDE + b))
            else:
                pairs.append((a * SIDE + b, a * SIDE + (b + distance) % SIDE))
    return lax.ppermute(block, "expert", pairs)


def iota(shape, dim):
    return lax.broadcasted_iota(jnp.int32, shape, dim)


def dot(a, b, da=1, db=0):
    return lax.dot_general(a, b, (((da,), (db,)), ((), ())), preferred_element_type=F32)


def prep_kernel(experts, routes_ref, gates_ref, x_ref, g_ref, xe_ref, ge_ref, tail_ref):
    tok, width = x_ref.shape
    topk = routes_ref.shape[0]
    expert = lax.rem(iota((LANES, tok), 0), experts)
    full = jnp.zeros((LANES, tok), F32)
    for k in range(topk):
        full += jnp.where(routes_ref[k : k + 1, :] == expert, gates_ref[k : k + 1, :], 0.0)
    full = full.T
    lane = iota((tok, LANES), 1)
    high = full.astype(BF16).astype(F32)
    rest = full - high
    middle = rest.astype(BF16).astype(F32)
    low = rest - middle
    piece = jnp.where(lane < 2 * experts, middle, jnp.where(lane < 3 * experts, low, 0.0))
    piece = jnp.where(lane < experts, high, piece).astype(BF16)
    for src, dst in ((x_ref, xe_ref), (g_ref, ge_ref)):
        dst[:, :width] = src[...]
        dst[:, width:] = piece
    tail_ref[...] = piece


def prep(routes, gates, x, g, experts):
    tok, width = x.shape
    shape = jax.ShapeDtypeStruct((tok, width + LANES), BF16)
    return pl.pallas_call(
        functools.partial(prep_kernel, experts),
        out_shape=(shape, shape, jax.ShapeDtypeStruct((tok, LANES), BF16)),
        compiler_params=params(0),
        name="prep",
    )(routes, gates, x, g)


def places(piece, experts, blocks):
    rows = piece.shape[0]
    tok = rows // blocks
    r, c = iota((rows, rows), 0), iota((rows, rows), 1)
    upto = jnp.where((c <= r) & (lax.div(c, tok) == lax.div(r, tok)), 1.0, 0.0).astype(BF16)
    lane = iota((rows, LANES), 1)
    mask = jnp.where((lane < experts) & (piece.astype(F32) > 0.0), 1.0, 0.0)
    return (dot(upto, mask.astype(BF16)) * mask).astype(BF16)


def pack_kernel(scale, experts, cap, steps_to, me_ref, *refs):
    blocks, outs = refs[:4], refs[4:-5]
    rows_v, packed_v, table_v, in_sems, out_sems = refs[-5:]
    count = len(outs)
    eids = [expert_at(me_ref, dx, dz) for dx, dz in steps_to]
    pair = 2 * cap
    tok, width = blocks[0].shape[0], outs[0].shape[1]
    steps, step = packed_v.shape[0], packed_v.shape[3]
    pieces = [slice(width, width + LANES)] + [slice(t * step, (t + 1) * step) for t in range(steps)]
    loads = []
    for n, cols in enumerate(pieces):
        for b in range(4):
            part = rows_v.at[b // 2, pl.ds(b % 2 * tok, tok), cols]
            loads.append(begun(blocks[b].at[:, cols], part, in_sems.at[n, b]))
    for load in loads[:4]:
        load.wait()
    lane = iota((pair, LANES), 1)
    second = jnp.where(iota((pair, 2 * tok), 1) >= tok, cap, 0)
    place = iota((pair, 2 * tok), 0) + 1 - second
    place = jnp.where(place > 0, place, -1).astype(F32)
    factors = []
    for p in range(2):
        piece = rows_v[p, :, width:]
        known = places(piece, experts, 2)
        for j in range(count):
            choose = jnp.where(lane == eids[j], 1.0, 0.0).astype(BF16)
            found = dot(choose, known, 1, 1)
            table = jnp.where(found == place, 1.0, 0.0).astype(BF16)
            table_v[p, j * pair : (j + 1) * pair, :] = table
            if scale:
                mine = (lax.rem(lane, experts) == eids[j]) & (lane < 3 * experts)
                gate = jnp.where(mine, dot(table, piece), 0.0)
                factors.append(jnp.sum(gate, axis=1, keepdims=True))
    stores = []
    for t in range(steps):
        for load in loads[4 * t + 4 : 4 * t + 8]:
            load.wait()
        for p in range(2):
            packed = dot(table_v[p], rows_v[p, :, pieces[t + 1]])
            for j in range(count):
                part = packed[j * pair : (j + 1) * pair]
                if scale:
                    part = part * factors[p * count + j]
                packed_v[t, j, p * pair : (p + 1) * pair, :] = part.astype(BF16)
        for j in range(count):
            target = outs[j].at[:, pieces[t + 1]]
            stores.append(begun(packed_v.at[t, j], target, out_sems.at[t, j]))
    for store in stores:
        store.wait()


def pack(me, blocks, width, experts, cap, steps_to, scale, name):
    count = len(steps_to)
    tok = blocks[0].shape[0]
    step = 512
    steps = width // step
    pair = 2 * cap
    out = jax.ShapeDtypeStruct((2 * pair, width), BF16)
    return pl.pallas_call(
        functools.partial(pack_kernel, scale, experts, cap, steps_to),
        in_specs=[SCALARS] + [FAR] * 4,
        out_specs=[FAR] * count,
        out_shape=[out] * count,
        scratch_shapes=[
            pltpu.VMEM((2, 2 * tok, width + LANES), BF16),
            pltpu.VMEM((steps, count, 2 * pair, step), BF16),
            pltpu.VMEM((2, count * pair, 2 * tok), BF16),
            pltpu.SemaphoreType.DMA((steps + 1, 4)),
            pltpu.SemaphoreType.DMA((steps, count)),
        ],
        compiler_params=params(0),
        cost_estimate=cost(3e9, 10e6),
        name=name,
    )(me, *blocks)


def home_kernel(experts, cap, tail_ref, rows_ref, grad_ref, out_ref, table_ref):
    tok = tail_ref.shape[0]
    total = experts * cap

    @pl.when(pl.program_id(0) == 0)
    def _():
        choose = jnp.where(iota((LANES, total), 0) == lax.div(iota((LANES, total), 1), cap), 1.0, 0.0)
        found = dot(places(tail_ref[...], experts, 1), choose.astype(BF16))
        place = lax.rem(iota((tok, total), 1), cap) + 1
        table_ref[...] = jnp.where(found == place.astype(F32), 1.0, 0.0).astype(BF16)

    total_grad = dot(table_ref[...], rows_ref[...]) + grad_ref[...].astype(F32)
    out_ref[...] = total_grad.astype(BF16)


def home(tail, rows, grad, experts, cap):
    tok, width = grad.shape
    step = 512
    total = experts * cap
    return pl.pallas_call(
        functools.partial(home_kernel, experts, cap),
        grid=(width // step,),
        in_specs=[
            held((tok, LANES), lambda i: (0, 0)),
            pl.BlockSpec((total, step), lambda i: (0, i)),
            pl.BlockSpec((tok, step), lambda i: (0, i)),
        ],
        out_specs=pl.BlockSpec((tok, step), lambda i: (0, i)),
        out_shape=jax.ShapeDtypeStruct((tok, width), BF16),
        scratch_shapes=[pltpu.VMEM((tok, total), BF16)],
        compiler_params=params(1),
        cost_estimate=cost(3e9, 10e6),
        name="home",
    )(tail, rows, grad)


def up_kernel(count, *refs):
    xs, (wa, wb), outs = refs[:count], refs[count : count + 2], refs[count + 2 :]
    for i in range(count):
        rows = xs[i][...]
        a = dot(rows, wa[...])
        b = dot(rows, wb[...])
        sig = jax.nn.sigmoid(a)
        outs[3 * i][...] = a * sig * b
        outs[3 * i + 1][...] = (b * sig * (1.0 + a * (1.0 - sig))).astype(BF16)
        outs[3 * i + 2][...] = (a * sig).astype(BF16)


def up(xs, wgu):
    count = len(xs)
    rows, width = xs[0].shape
    hidden = wgu.shape[1] // 2
    step = 256
    steps = hidden // step
    kinds = (F32, BF16, BF16) * count
    flat = pl.pallas_call(
        functools.partial(up_kernel, count),
        grid=(steps,),
        in_specs=[held((rows, width), lambda i: (0, 0))] * count
        + [
            pl.BlockSpec((width, step), lambda i: (0, i)),
            pl.BlockSpec((width, step), lambda i: (0, i + steps)),
        ],
        out_specs=[pl.BlockSpec((rows, step), lambda i: (0, i))] * (3 * count),
        out_shape=[jax.ShapeDtypeStruct((rows, hidden), kind) for kind in kinds],
        compiler_params=params(1),
        cost_estimate=cost(3e9, 10e6),
        name="up",
    )(*xs, wgu, wgu)
    return [flat[3 * i : 3 * i + 3] for i in range(count)]


def dh_kernel(count, *refs):
    ss, wd, outs = refs[:count], refs[count], refs[count + 1 :]
    for i in range(count):
        outs[i][...] = dot(ss[i][...], wd[...], 1, 1)


def dh_of(ss, wdown):
    count = len(ss)
    rows, width = ss[0].shape
    hidden = wdown.shape[0]
    step = 256
    return pl.pallas_call(
        functools.partial(dh_kernel, count),
        grid=(hidden // step,),
        in_specs=[held((rows, width), lambda i: (0, 0))] * count
        + [pl.BlockSpec((step, width), lambda i: (i, 0))],
        out_specs=[pl.BlockSpec((rows, step), lambda i: (0, i))] * count,
        out_shape=[jax.ShapeDtypeStruct((rows, hidden), F32)] * count,
        compiler_params=params(1),
        cost_estimate=cost(3e9, 10e6),
        name="dh",
    )(*ss, wdown)


def crossed(parts, j, cap):
    return jnp.concatenate([part[j * cap : (j + 1) * cap, :] for part in parts], axis=0)


def activations(rows, w, t, hidden):
    a = dot(rows, w[:, tile(t, 256)])
    b = dot(rows, w[:, tile(t + hidden // 256, 256)])
    sig = jax.nn.sigmoid(a)
    return a * sig * b, (b * sig * (1.0 + a * (1.0 - sig)), a * sig)


def tile(t, step):
    return pl.ds(pl.multiple_of(t * step, step), step)


def gate_up_load(w, w_v, sems, hidden, t, k):
    part = tile(t + k * (hidden // 256), 256)
    return pltpu.make_async_copy(w.at[:, part], w_v.at[:, part], sems.at[t, k])


def gate_up_loads(w, w_v, sems, hidden):
    for t in range(hidden // 256):
        for k in range(2):
            gate_up_load(w, w_v, sems, hidden, t, k).start()


def row_load(w, w_v, sems, t, step):
    return pltpu.make_async_copy(w.at[tile(t, step), :], w_v.at[tile(t, step), :], sems.at[t])


def send_rows(d_v, w_v, blocks, cap, me_ref, rows_v, out, sems, ready=None):
    hidden = w_v.shape[1] // 2

    def copy_of(t, n, i, j):
        target = out.at[home_of(me_ref, i, j), :, tile(t, 512)]
        return pltpu.make_async_copy(rows_v.at[t, n], target, sems.at[t, n])

    @pl.loop(0, w_v.shape[0] // 512)
    def _(t):
        if ready is not None:
            ready(t)
        w = w_v[tile(t, 512), :]
        part = dot(d_v[0], w[:, :hidden], 1, 1) + dot(d_v[1], w[:, hidden:], 1, 1)
        for n, (i, j) in enumerate(blocks):
            rows_v[t, n] = part[n * cap : (n + 1) * cap].astype(BF16)
            copy_of(t, n, i, j).start()

    @pl.loop(0, w_v.shape[0] // 512)
    def _(t):
        for n, (i, j) in enumerate(blocks):
            copy_of(t, n, i, j).wait()


def middle_kernel(cap, me_ref, *refs):
    w, wd, xs, ss, fs, dh0 = refs[0], refs[1], refs[2:4], refs[4:6], refs[6:8], refs[8]
    h_out, tail_out, dh_out, out, ds = refs[9:11], refs[11], refs[12], refs[13], refs[14:16]
    w_v, wd_v, x_v, s_v, h_v, f_v, dh_v, tail_v, dh_tail_v, d_v, e_v, rows_v = refs[16:28]
    w_sems, wd_sems, in_sems, out_sems, row_sems = refs[28:]
    rows = xs[0].shape[0]
    hidden = wd.shape[0]
    edge = 3 * cap - 8
    x_loads = [begun(xs[n], x_v.at[n], in_sems.at[n]) for n in range(2)]
    gate_up_loads(w, w_v, w_sems, hidden)
    s_loads = [begun(ss[n], s_v.at[n], in_sems.at[2 + n]) for n in range(2)]
    for t in range(hidden // 256):
        row_load(wd, wd_v, wd_sems, t, 256).start()
    f_loads = [begun(fs[k], f_v.at[k, 0], in_sems.at[4 + k]) for k in range(2)]
    f_loads.append(begun(dh0, dh_v.at[0], in_sems.at[6]))
    for load in x_loads:
        load.wait()
    @pl.loop(0, hidden // 256)
    def _(t):
        for k in range(2):
            gate_up_load(w, w_v, w_sems, hidden, t, k).wait()
        for n in range(2):
            h, factors = activations(x_v[n], w_v, t, hidden)
            h_v[n, :, tile(t, 256)] = h
            for k in range(2):
                f_v[k, n + 1, :, tile(t, 256)] = factors[k].astype(BF16)

    copies = [begun(h_v.at[n], h_out[n], out_sems.at[n]) for n in range(2)]
    for load in s_loads:
        load.wait()
    @pl.loop(0, hidden // 256)
    def _(t):
        row_load(wd, wd_v, wd_sems, t, 256).wait()
        for n in range(2):
            dh_v[n + 1, :, tile(t, 256)] = dot(s_v[n], wd_v[tile(t, 256), :], 1, 1)

    for load in f_loads:
        load.wait()
    for j in range(3):
        dh_tail_v[j * cap : (j + 1) * cap, :] = dh_v[j, 3 * cap :, :]
        for k in range(2):
            tail_v[k, j] = f_v[k, j, edge:, :]
    copies.append(begun(dh_tail_v, dh_out, out_sems.at[2]))
    copies.append(begun(tail_v, tail_out, out_sems.at[3]))
    for k in range(2):
        @pl.loop(0, hidden // 256)
        def _(t):
            cols = tile(t, 256)
            chunks = [dh_v[j, :, cols] for j in range(3)]
            kept = []
            for i in range(3):
                factor = f_v[k, i, :, cols].astype(F32)[: 3 * cap]
                product = crossed(chunks, i, cap) * factor
                kept.append(product)
                whole = jnp.concatenate([product, jnp.zeros((cap, 256), F32)], axis=0)
                d_v[k, i * rows : (i + 1) * rows, cols] = whole.astype(BF16)
            e_v[k, :, cols] = jnp.concatenate(kept, axis=0).astype(BF16)

        copies.append(begun(d_v.at[k], ds[k].at[pl.ds(0, 3 * rows), :], out_sems.at[4 + k]))
    blocks = [(i, j) for i in range(3) for j in range(3)]
    send_rows(e_v, w_v, blocks, cap, me_ref, rows_v, out, row_sems)
    for copy in copies:
        copy.wait()


def middle(me, wgu, wdown, xs, ss, factors, dh0, cap):
    rows, width = xs[0].shape
    hidden = wdown.shape[0]
    steps = width // 512
    h = jax.ShapeDtypeStruct((rows, hidden), F32)
    tail = jax.ShapeDtypeStruct((2, 3, cap + 8, hidden), BF16)
    dab = jax.ShapeDtypeStruct((SIDE * rows, hidden), BF16)
    slots = jax.ShapeDtypeStruct((SIDE * SIDE, cap, width), BF16)
    h1, h2, tails, dh_tail, slots, da, db = pl.pallas_call(
        functools.partial(middle_kernel, cap),
        in_specs=[SCALARS] + [FAR] * 9,
        out_specs=[FAR] * 7,
        out_shape=[h, h, tail, jax.ShapeDtypeStruct((3 * cap, hidden), F32), slots, dab, dab],
        scratch_shapes=[
            pltpu.VMEM((width, 2 * hidden), BF16),
            pltpu.VMEM((hidden, width), BF16),
            pltpu.VMEM((2, rows, width), BF16),
            pltpu.VMEM((2, rows, width), BF16),
            pltpu.VMEM((2, rows, hidden), F32),
            pltpu.VMEM((2, 3, rows, hidden), BF16),
            pltpu.VMEM((3, rows, hidden), F32),
            pltpu.VMEM((2, 3, cap + 8, hidden), BF16),
            pltpu.VMEM((3 * cap, hidden), F32),
            pltpu.VMEM((2, 3 * rows, hidden), BF16),
            pltpu.VMEM((2, 9 * cap, hidden), BF16),
            pltpu.VMEM((steps, 9, cap, 512), BF16),
            pltpu.SemaphoreType.DMA((hidden // 256, 2)),
            pltpu.SemaphoreType.DMA((hidden // 256,)),
            pltpu.SemaphoreType.DMA((7,)),
            pltpu.SemaphoreType.DMA((6,)),
            pltpu.SemaphoreType.DMA((steps, 9)),
        ],
        compiler_params=params(0),
        cost_estimate=cost(3e9, 10e6),
        name="middle",
    )(me, wgu, wdown, *xs, *ss, *factors, dh0)
    return [h1, h2], tails, dh_tail, slots, [da, db]


def last_x_kernel(cap, me_ref, *refs):
    w, x, hs, dh_tail = refs[0], refs[1], refs[2:5], refs[5]
    turned_out, tail_out, out, ds = refs[9], refs[10], refs[11], refs[12:14]
    w_v, x_v, h_v, f_v, dh_v, turned_v, d_v, e_v, rows_v = refs[14:23]
    w_sems, in_sems, out_sems, row_sems = refs[23:]
    rows = x.shape[0]
    hidden = w.shape[1] // 2
    edge = 3 * cap - 8
    x_load = begun(x, x_v, in_sems.at[0])
    gate_up_loads(w, w_v, w_sems, hidden)
    loads = [begun(hs[n], h_v.at[n], in_sems.at[1 + n]) for n in range(3)]
    loads.append(begun(dh_tail, dh_v, in_sems.at[4]))
    x_load.wait()
    @pl.loop(0, hidden // 256)
    def _(t):
        for k in range(2):
            gate_up_load(w, w_v, w_sems, hidden, t, k).wait()
        h, factors = activations(x_v[...], w_v, t, hidden)
        h_v[3, :, tile(t, 256)] = h
        for k in range(2):
            f_v[k, :, tile(t, 256)] = factors[k].astype(BF16)

    for load in loads:
        load.wait()
    copies = [begun(f_v.at[:, pl.ds(edge, cap + 8), :], tail_out, out_sems.at[0])]
    @pl.loop(0, hidden // 256)
    def _(t):
        cols = tile(t, 256)
        parts = [h_v[n, :, cols] for n in range(SIDE)]
        whole = jnp.concatenate([crossed(parts, j, cap) for j in range(SIDE)], axis=0)
        turned_v[cols, :] = whole.T.astype(BF16)
        for k in range(2):
            product = dh_v[:, cols] * f_v[k, :, cols].astype(F32)[: 3 * cap]
            e_v[k, :, cols] = product.astype(BF16)
            whole = jnp.concatenate([product, jnp.zeros((cap, 256), F32)], axis=0)
            d_v[k, :, cols] = whole.astype(BF16)

    copies.append(begun(turned_v, turned_out, out_sems.at[1]))
    for k in range(2):
        copies.append(begun(d_v.at[k], ds[k].at[pl.ds(3 * rows, rows), :], out_sems.at[2 + k]))
    blocks = [(3, j) for j in range(3)]
    send_rows(e_v, w_v, blocks, cap, me_ref, rows_v, out, row_sems)
    for copy in copies:
        copy.wait()


def last_x(me, wgu, x, hs, dh_tail, slots, ds, cap):
    rows, width = x.shape
    hidden = wgu.shape[1] // 2
    steps = width // 512
    turned_h, tail, slots, da, db = pl.pallas_call(
        functools.partial(last_x_kernel, cap),
        in_specs=[SCALARS] + [FAR] * 9,
        out_specs=[FAR] * 5,
        out_shape=[
            jax.ShapeDtypeStruct((hidden, SIDE * rows), BF16),
            jax.ShapeDtypeStruct((2, cap + 8, hidden), BF16),
        ]
        + [jax.ShapeDtypeStruct(a.shape, BF16) for a in (slots, *ds)],
        input_output_aliases={7: 2, 8: 3, 9: 4},
        scratch_shapes=[
            pltpu.VMEM((width, 2 * hidden), BF16),
            pltpu.VMEM((rows, width), BF16),
            pltpu.VMEM((SIDE, rows, hidden), F32),
            pltpu.VMEM((2, rows, hidden), BF16),
            pltpu.VMEM((3 * cap, hidden), F32),
            pltpu.VMEM((hidden, SIDE * rows), BF16),
            pltpu.VMEM((2, rows, hidden), BF16),
            pltpu.VMEM((2, 3 * cap, hidden), BF16),
            pltpu.VMEM((steps, 3, cap, 512), BF16),
            pltpu.SemaphoreType.DMA((hidden // 256, 2)),
            pltpu.SemaphoreType.DMA((5,)),
            pltpu.SemaphoreType.DMA((4,)),
            pltpu.SemaphoreType.DMA((steps, 3)),
        ],
        compiler_params=params(0),
        cost_estimate=cost(3e9, 10e6),
        name="last_x",
    )(me, wgu, x, *hs, dh_tail, slots, *ds)
    return turned_h, tail, slots, [da, db]


AHEAD = (2, 1, 3)
SPOTS = (((0, 0), (1, 1)), ((2, 0), (0, 1)), ((1, 0), (2, 1)))


def put_halves(k, part, sent_v, wait_v, outs, sems):
    half = part.shape[0] // 2
    copies = []
    for side in range(2):
        out, row = SPOTS[k][side]
        piece = part[side * half : (side + 1) * half]
        if out == 2:
            staged = wait_v.at[row]
            staged[...] = piece
        else:
            staged = sent_v.at[out, row]
            staged[...] = piece.astype(BF16)
        target = outs[out].at[row * half : (row + 1) * half, :]
        copies.append(begun(staged, target, sems.at[k, side]))
    return copies


def ahead_of(place_ref, ahead, size):
    start = lax.rem(place_ref[0] + ahead, SIDE) * size
    return pl.ds(pl.multiple_of(start, size), size)


def message_outs(rows, cols):
    return [jax.ShapeDtypeStruct((rows, cols), kind) for kind in (BF16, BF16, F32)]


def message_scratch(rows, cols):
    return [
        pltpu.VMEM((2, 2, rows // 2, cols), BF16),
        pltpu.VMEM((2, rows // 2, cols), F32),
        pltpu.SemaphoreType.DMA((3, 2)),
    ]


def last_s_kernel(cap, me_ref, place_ref, *refs):
    turned, ss, wd, tails, tail, w = refs[0], refs[1:5], refs[5], refs[6], refs[7], refs[8]
    outs, out, ds = refs[10:13], refs[13], refs[14:16]
    turned_v, q_v, s_v, wd_v, f_v, d_v, w_v, rows_v = refs[16:24]
    sent_v, wait_v, message_sems, in_sems, q_sems, wd_sems, w_sems, out_sems, row_sems = refs[24:]
    rows, width = ss[0].shape
    hidden = wd.shape[0]
    turned_load = begun(turned, turned_v, in_sems.at[0])
    q_loads = []
    for k, ahead in enumerate(AHEAD):
        cols = ahead_of(place_ref, ahead, width // SIDE)
        for j in range(SIDE):
            part = q_v.at[k, pl.ds(j * rows, rows), :]
            q_loads.append(begun(ss[j].at[:, cols], part, q_sems.at[k, j]))
    s_load = begun(ss[3], s_v, in_sems.at[1])
    for t in range(hidden // 256):
        row_load(wd, wd_v, wd_sems, t, 256).start()
    loads = [begun(tails, f_v.at[:, pl.ds(0, 3)], in_sems.at[2])]
    loads.append(begun(tail, f_v.at[:, 3], in_sems.at[3]))
    for t in range(w.shape[0] // 512):
        row_load(w, w_v, w_sems, t, 512).start()
    turned_load.wait()
    copies = []
    for k in range(3):
        for load in q_loads[4 * k : 4 * k + 4]:
            load.wait()
        part = dot(turned_v[...], q_v[k])
        copies += put_halves(k, part, sent_v, wait_v, outs, message_sems)
    s_load.wait()
    for load in loads:
        load.wait()
    @pl.loop(0, hidden // 256)
    def _(t):
        row_load(wd, wd_v, wd_sems, t, 256).wait()
        cols = tile(t, 256)
        dh = dot(s_v[...], wd_v[cols, :], 1, 1)
        for k in range(2):
            factors = [f_v[k, i, :, cols].astype(F32)[8:] for i in range(SIDE)]
            d_v[k, :, cols] = (dh * jnp.concatenate(factors, axis=0)).astype(BF16)

    copies += [begun(d_v.at[k], ds[k], out_sems.at[k]) for k in range(2)]
    blocks = [(i, 3) for i in range(SIDE)]
    ready = lambda t: row_load(w, w_v, w_sems, t, 512).wait()
    send_rows(d_v, w_v, blocks, cap, me_ref, rows_v, out, row_sems, ready)
    for copy in copies:
        copy.wait()


def last_s(me, place, turned_h, ss, wdown, tails, tail, wgu, slots, cap):
    rows, width = ss[0].shape
    hidden, total = turned_h.shape
    quarter = width // SIDE
    steps = width // 512
    dab = jax.ShapeDtypeStruct((rows, hidden), BF16)
    *down, slots, da, db = pl.pallas_call(
        functools.partial(last_s_kernel, cap),
        in_specs=[SCALARS] * 2 + [FAR] * 10,
        out_specs=[FAR] * 6,
        out_shape=message_outs(hidden, quarter)
        + [jax.ShapeDtypeStruct(slots.shape, BF16), dab, dab],
        input_output_aliases={11: 3},
        scratch_shapes=[
            pltpu.VMEM((hidden, total), BF16),
            pltpu.VMEM((3, total, quarter), BF16),
            pltpu.VMEM((rows, width), BF16),
            pltpu.VMEM((hidden, width), BF16),
            pltpu.VMEM((2, SIDE, cap + 8, hidden), BF16),
            pltpu.VMEM((2, rows, hidden), BF16),
            pltpu.VMEM((width, 2 * hidden), BF16),
            pltpu.VMEM((steps, SIDE, cap, 512), BF16),
        ]
        + message_scratch(hidden, quarter)
        + [
            pltpu.SemaphoreType.DMA((4,)),
            pltpu.SemaphoreType.DMA((3, SIDE)),
            pltpu.SemaphoreType.DMA((hidden // 256,)),
            pltpu.SemaphoreType.DMA((steps,)),
            pltpu.SemaphoreType.DMA((2,)),
            pltpu.SemaphoreType.DMA((steps, SIDE)),
        ],
        compiler_params=params(0),
        cost_estimate=cost(1, 1),
        name="last_s",
    )(me, place, turned_h, *ss, wdown, tails, tail, wgu, slots)
    return down, slots, [da, db]


def down_own_kernel(place_ref, *refs):
    turned_ref, ss, out = refs[0], refs[1:5], refs[5]
    out[...] = dot(turned_ref[...], jnp.concatenate([s[...] for s in ss], axis=0))


def down_own(place, turned_h, ss):
    hidden, total = turned_h.shape
    rows, width = ss[0].shape
    quarter = width // SIDE
    return pl.pallas_call(
        down_own_kernel,
        grid_spec=pltpu.PrefetchScalarGridSpec(
            num_scalar_prefetch=1,
            grid=(2,),
            in_specs=[pl.BlockSpec((hidden // 2, total), lambda i, place: (i, 0))]
            + [held((rows, quarter), lambda i, place: (0, place[0]))] * 4,
            out_specs=pl.BlockSpec((hidden // 2, quarter), lambda i, place: (i, 0)),
        ),
        out_shape=jax.ShapeDtypeStruct((hidden, quarter), F32),
        compiler_params=params(1),
        cost_estimate=cost(1, 1),
        name="down_own",
    )(place, turned_h, *ss)


def gate_up_kernel(cap, place_ref, *refs):
    early, late, xs, outs, ds = refs[:2], refs[2:4], refs[4:8], refs[8:11], refs[11:13]
    d_v, late_v, x_v, sent_v, wait_v, out_sems, d_sems, x_sems = refs[13:]
    rows, width = xs[0].shape
    size = width // SIDE
    loads = []
    for k in range(2):
        loads.append(begun(early[k], d_v.at[k], d_sems.at[0, k]))
        loads.append(begun(late[k], late_v.at[k], d_sems.at[1, k]))
    for k, ahead in enumerate(AHEAD):
        cols = ahead_of(place_ref, ahead, size)
        for i in range(SIDE):
            part = x_v.at[k, pl.ds(i * rows, rows), :]
            loads.append(begun(xs[i].at[:, cols], part, x_sems.at[k, i]))
    for load in loads[:4]:
        load.wait()
    edge = 3 * cap - 8
    copies = []
    for k in range(2):
        fresh = late_v[k].astype(F32)
        for i in range(SIDE):
            at = slice(i * rows + edge, (i + 1) * rows)
            old = d_v[k, at, :].astype(F32)[:8]
            new = fresh[i * cap : (i + 1) * cap]
            d_v[k, at, :] = jnp.concatenate([old, new], axis=0).astype(BF16)
        copies.append(begun(d_v.at[k], ds[k], d_sems.at[2, k]))
    for k in range(3):
        for load in loads[4 * k + 4 : 4 * k + 8]:
            load.wait()
        turned_x = x_v[k].T
        part = jnp.concatenate([dot(turned_x, d_v[0]), dot(turned_x, d_v[1])], axis=1)
        copies += put_halves(k, part, sent_v, wait_v, outs, out_sems)
    for copy in copies:
        copy.wait()


def gate_up_parts(place, early, late, xs, cap):
    rows, width = xs[0].shape
    total, hidden = early[0].shape
    quarter = width // SIDE
    out = jax.ShapeDtypeStruct((total, hidden), BF16)
    *messages, da, db = pl.pallas_call(
        functools.partial(gate_up_kernel, cap),
        in_specs=[SCALARS] + [FAR] * 8,
        out_specs=[FAR] * 5,
        out_shape=message_outs(quarter, 2 * hidden) + [out, out],
        scratch_shapes=[
            pltpu.VMEM((2, total, hidden), BF16),
            pltpu.VMEM((2, *late[0].shape), BF16),
            pltpu.VMEM((3, total, quarter), BF16),
        ]
        + message_scratch(quarter, 2 * hidden)
        + [pltpu.SemaphoreType.DMA((3, 2)), pltpu.SemaphoreType.DMA((3, SIDE))],
        compiler_params=params(0),
        cost_estimate=cost(1, 1),
        name="gate_up_parts",
    )(place, *early, *late, *xs)
    return messages, [da, db]


def gate_up_own_kernel(place_ref, *refs):
    xs, ds, out = refs[:4], refs[4:6], refs[6]
    rows = jnp.concatenate([x[...] for x in xs], axis=0).T
    out[...] = jnp.concatenate([dot(rows, d[...]) for d in ds], axis=1)


def gate_up_own(place, xs, ds):
    rows, width = xs[0].shape
    total, hidden = ds[0].shape
    half = width // SIDE // 2
    return pl.pallas_call(
        gate_up_own_kernel,
        grid_spec=pltpu.PrefetchScalarGridSpec(
            num_scalar_prefetch=1,
            grid=(2,),
            in_specs=[pl.BlockSpec((rows, half), lambda i, place: (0, 2 * place[0] + i))] * 4
            + [held((total, hidden), lambda i, place: (0, 0))] * 2,
            out_specs=pl.BlockSpec((half, 2 * hidden), lambda i, place: (i, 0)),
        ),
        out_shape=jax.ShapeDtypeStruct((2 * half, 2 * hidden), F32),
        compiler_params=params(1),
        cost_estimate=cost(200e9, 10e6),
        name="gate_up_own",
    )(place, *xs, *ds)


def around(first, axis):
    return [first] + [moved_along(first, axis, OFF[b]) for b in range(1, SIDE)]


def spread(outs, axis, work):
    near = [moved_along(outs[j], axis, OFF[j]) for j in (1, 2)]
    done = work(outs[0])
    far, near[0], near[1], *done = lax.optimization_barrier((outs[3], *near, *done))
    return [outs[0], *near, moved_along(far, axis, OFF[3])], done


def ring_first(first_up, first_down, wait):
    return moved_along(first_up, "edata", 1), moved_along(first_down, "edata", -1)


def ring_second(up1, down1, first_up, first_down, wait):
    half = wait.shape[0] // 2
    second_up = (wait[:half] + up1[:half].astype(F32)).astype(BF16)
    second_down = (wait[half:] + down1[half:].astype(F32)).astype(BF16)
    return moved_along(second_up, "edata", 1), moved_along(second_down, "edata", -1)


def ring_own(own, up1, down1):
    half = own.shape[0] // 2
    return own + jnp.concatenate([down1[:half], up1[half:]], axis=0).astype(F32)


def ring_last(total, up2, down2):
    return (total + jnp.concatenate([up2, down2], axis=0).astype(F32)).astype(BF16)


def body(hidden_in, out_grad, routes, gates, w_gate_up, w_down):
    tok = hidden_in.shape[1]
    width = hidden_in.shape[2]
    topk = routes.shape[2]
    experts = lax.axis_size("expert")
    cap = min(tok, tok * topk * 9 // (8 * experts))
    wgu, wdown = w_gate_up[0, 0], w_down[0, 0]
    me = lax.axis_index("expert").astype(jnp.int32).reshape(1)
    place = lax.axis_index("edata").astype(jnp.int32).reshape(1)

    xe, ge, tail = prep(routes[0].T, gates[0].T, hidden_in[0], out_grad[0], experts)
    xblocks = around(xe, "x")
    gblocks = around(ge, "z")
    def packed(blocks, scale, name, which):
        steps_to = tuple((OFF[j], 0) if scale else (0, OFF[j]) for j in which)
        return list(pack(me, blocks, width, experts, cap, steps_to, scale, name))

    xnear = packed(xblocks, False, "pack_rows", (1, 2))
    xnear[0], gblocks[0] = lax.optimization_barrier((xnear[0], gblocks[0]))
    gnear = packed(gblocks, True, "pack_scaled", (1, 2))
    xblocks[0], gnear[0] = lax.optimization_barrier((xblocks[0], gnear[0]))
    x0, xfar = packed(xblocks, False, "pack_rows_rest", (0, 3))
    s0, sfar = packed(gblocks, True, "pack_scaled_rest", (0, 3))
    xs, (h0, *factors) = spread([x0, *xnear, xfar], "z", lambda rows: up([rows], wgu)[0])
    ss, (dh0,) = spread([s0, *gnear, sfar], "x", lambda rows: dh_of([rows], wdown))
    hs, tails, dh_tail, slots, early = middle(
        me, wgu, wdown, xs[1:3], ss[1:3], factors, dh0, cap
    )
    turned_h, last_tail, slots, early = last_x(
        me, wgu, xs[3], [h0, *hs], dh_tail, slots, early, cap
    )
    last, slots, turned_h = lax.optimization_barrier((ss[3], slots, turned_h))
    ss = ss[:3] + [last]
    down, rows, late = last_s(me, place, turned_h, ss, wdown, tails, last_tail, wgu, slots, cap)
    down_first = ring_first(*down)
    returned = lax.all_to_all(rows, "expert", split_axis=0, concat_axis=0, tiled=True)
    rows, *late = lax.optimization_barrier((rows, *late))
    gate_up, ds = gate_up_parts(place, early, late, xs, cap)
    gate_up[0], gate_up[1], *down_first = lax.optimization_barrier((gate_up[0], gate_up[1], *down_first))
    gate_up_first = ring_first(*gate_up)
    wait, da, db, turned_h = lax.optimization_barrier((gate_up[2], *ds, turned_h))
    gate_up = [*gate_up[:2], wait]
    own_down = down_own(place, turned_h, ss)
    own_gate_up = gate_up_own(place, xs, [da, db])
    own_down, own_gate_up, *gate_up_first = lax.optimization_barrier(
        (own_down, own_gate_up, *gate_up_first)
    )
    down_second = ring_second(*down_first, *down)
    gate_up_second = ring_second(*gate_up_first, *gate_up)
    down_grad = ring_last(ring_own(own_down, *down_first), *down_second)
    gate_up_grad = ring_last(ring_own(own_gate_up, *gate_up_first), *gate_up_second)

    layer = home(tail, returned.reshape(experts * cap, width), out_grad[0], experts, cap)
    upstream = moved_along(layer, "section", -1)
    return (upstream[None], gate_up_grad[None, None], down_grad[None, None])


def solution(mesh):
    return jax.shard_map(
        body,
        mesh=mesh,
        in_specs=(
            P("section", ("edata", "expert"), None),
            P("section", ("edata", "expert"), None),
            P("section", ("edata", "expert"), None),
            P("section", ("edata", "expert"), None),
            P("section", "expert", None, None),
            P("section", "expert", None, None),
        ),
        out_specs=(
            P("section", ("edata", "expert"), None),
            P("section", "expert", "edata", None),
            P("section", "expert", None, "edata"),
        ),
        check_vma=False,
    )
```

```python
import functools

import jax
import jax.numpy as jnp
from jax import lax
from jax.experimental import pallas as pl
from jax.experimental.pallas import tpu as pltpu
from jax.sharding import PartitionSpec as P

BF16 = jnp.bfloat16
F32 = jnp.float32
OFF = (0, 1, 3, 2)
SIDE = 4
LANES = 128
MIB = 1024 * 1024


def params(steps):
    return pltpu.CompilerParams(
        vmem_limit_bytes=58 * MIB, dimension_semantics=("arbitrary",) * steps
    )


SCALARS = pl.BlockSpec(memory_space=pltpu.SMEM)
FAR = pl.BlockSpec(memory_space=pl.ANY)


def begun(src, dst, sem):
    copy = pltpu.make_async_copy(src, dst, sem)
    copy.start()
    return copy


def expert_at(me_ref, dx, dz):
    x, z = lax.div(me_ref[0], SIDE), lax.rem(me_ref[0], SIDE)
    return lax.rem(x + dx, SIDE) * SIDE + lax.rem(z + dz, SIDE)


def home_of(me_ref, i, j):
    return expert_at(me_ref, SIDE - OFF[j], SIDE - OFF[i])


def held(shape, index):
    return pl.BlockSpec(shape, index, pipeline_mode=pl.Buffered(1))


def cost(flops, moved):
    return pl.CostEstimate(flops=int(flops), bytes_accessed=int(moved), transcendentals=0)


def moved_along(block, axis, distance):
    if axis == "edata" or axis == "section":
        size = lax.axis_size(axis)
        return lax.ppermute(block, axis, [(i, (i + distance) % size) for i in range(size)])
    pairs = []
    for a in range(SIDE):
        for b in range(SIDE):
            if axis == "x":
                pairs.append((a * SIDE + b, (a + distance) % SIDE * SIDE + b))
            else:
                pairs.append((a * SIDE + b, a * SIDE + (b + distance) % SIDE))
    return lax.ppermute(block, "expert", pairs)


def iota(shape, dim):
    return lax.broadcasted_iota(jnp.int32, shape, dim)


def dot(a, b, da=1, db=0):
    return lax.dot_general(a, b, (((da,), (db,)), ((), ())), preferred_element_type=F32)


def prep_kernel(experts, routes_ref, gates_ref, x_ref, g_ref, xe_ref, ge_ref, tail_ref):
    tok, width = x_ref.shape
    topk = routes_ref.shape[0]
    expert = lax.rem(iota((LANES, tok), 0), experts)
    full = jnp.zeros((LANES, tok), F32)
    for k in range(topk):
        full += jnp.where(routes_ref[k : k + 1, :] == expert, gates_ref[k : k + 1, :], 0.0)
    full = full.T
    lane = iota((tok, LANES), 1)
    high = full.astype(BF16).astype(F32)
    rest = full - high
    middle = rest.astype(BF16).astype(F32)
    low = rest - middle
    piece = jnp.where(lane < 2 * experts, middle, jnp.where(lane < 3 * experts, low, 0.0))
    piece = jnp.where(lane < experts, high, piece).astype(BF16)
    for src, dst in ((x_ref, xe_ref), (g_ref, ge_ref)):
        dst[:, :width] = src[...]
        dst[:, width:] = piece
    tail_ref[...] = piece


def prep(routes, gates, x, g, experts):
    tok, width = x.shape
    shape = jax.ShapeDtypeStruct((tok, width + LANES), BF16)
    return pl.pallas_call(
        functools.partial(prep_kernel, experts),
        out_shape=(shape, shape, jax.ShapeDtypeStruct((tok, LANES), BF16)),
        compiler_params=params(0),
        name="prep",
    )(routes, gates, x, g)


def places(piece, experts, blocks):
    rows = piece.shape[0]
    tok = rows // blocks
    r, c = iota((rows, rows), 0), iota((rows, rows), 1)
    upto = jnp.where((c <= r) & (lax.div(c, tok) == lax.div(r, tok)), 1.0, 0.0).astype(BF16)
    lane = iota((rows, LANES), 1)
    mask = jnp.where((lane < experts) & (piece.astype(F32) > 0.0), 1.0, 0.0)
    return (dot(upto, mask.astype(BF16)) * mask).astype(BF16)


def pack_kernel(scale, experts, cap, steps_to, me_ref, *refs):
    blocks, outs = refs[:4], refs[4:-5]
    rows_v, packed_v, table_v, in_sems, out_sems = refs[-5:]
    count = len(outs)
    eids = [expert_at(me_ref, dx, dz) for dx, dz in steps_to]
    pair = 2 * cap
    tok, width = blocks[0].shape[0], outs[0].shape[1]
    steps, step = packed_v.shape[0], packed_v.shape[3]
    pieces = [slice(width, width + LANES)] + [slice(t * step, (t + 1) * step) for t in range(steps)]
    loads = []
    for n, cols in enumerate(pieces):
        for b in range(4):
            part = rows_v.at[b // 2, pl.ds(b % 2 * tok, tok), cols]
            loads.append(begun(blocks[b].at[:, cols], part, in_sems.at[n, b]))
    for load in loads[:4]:
        load.wait()
    lane = iota((pair, LANES), 1)
    second = jnp.where(iota((pair, 2 * tok), 1) >= tok, cap, 0)
    place = iota((pair, 2 * tok), 0) + 1 - second
    place = jnp.where(place > 0, place, -1).astype(F32)
    factors = []
    for p in range(2):
        piece = rows_v[p, :, width:]
        known = places(piece, experts, 2)
        for j in range(count):
            choose = jnp.where(lane == eids[j], 1.0, 0.0).astype(BF16)
            found = dot(choose, known, 1, 1)
            table = jnp.where(found == place, 1.0, 0.0).astype(BF16)
            table_v[p, j * pair : (j + 1) * pair, :] = table
            if scale:
                mine = (lax.rem(lane, experts) == eids[j]) & (lane < 3 * experts)
                gate = jnp.where(mine, dot(table, piece), 0.0)
                factors.append(jnp.sum(gate, axis=1, keepdims=True))
    stores = []
    for t in range(steps):
        for load in loads[4 * t + 4 : 4 * t + 8]:
            load.wait()
        for p in range(2):
            packed = dot(table_v[p], rows_v[p, :, pieces[t + 1]])
            for j in range(count):
                part = packed[j * pair : (j + 1) * pair]
                if scale:
                    part = part * factors[p * count + j]
                packed_v[t, j, p * pair : (p + 1) * pair, :] = part.astype(BF16)
        for j in range(count):
            target = outs[j].at[:, pieces[t + 1]]
            stores.append(begun(packed_v.at[t, j], target, out_sems.at[t, j]))
    for store in stores:
        store.wait()


def pack(me, blocks, width, experts, cap, steps_to, scale, name):
    count = len(steps_to)
    tok = blocks[0].shape[0]
    step = 512
    steps = width // step
    pair = 2 * cap
    out = jax.ShapeDtypeStruct((2 * pair, width), BF16)
    return pl.pallas_call(
        functools.partial(pack_kernel, scale, experts, cap, steps_to),
        in_specs=[SCALARS] + [FAR] * 4,
        out_specs=[FAR] * count,
        out_shape=[out] * count,
        scratch_shapes=[
            pltpu.VMEM((2, 2 * tok, width + LANES), BF16),
            pltpu.VMEM((steps, count, 2 * pair, step), BF16),
            pltpu.VMEM((2, count * pair, 2 * tok), BF16),
            pltpu.SemaphoreType.DMA((steps + 1, 4)),
            pltpu.SemaphoreType.DMA((steps, count)),
        ],
        compiler_params=params(0),
        cost_estimate=cost(3e9, 10e6),
        name=name,
    )(me, *blocks)


def home_kernel(experts, cap, tail_ref, rows_ref, grad_ref, out_ref, table_ref):
    tok = tail_ref.shape[0]
    total = experts * cap

    @pl.when(pl.program_id(0) == 0)
    def _():
        choose = jnp.where(iota((LANES, total), 0) == lax.div(iota((LANES, total), 1), cap), 1.0, 0.0)
        found = dot(places(tail_ref[...], experts, 1), choose.astype(BF16))
        place = lax.rem(iota((tok, total), 1), cap) + 1
        table_ref[...] = jnp.where(found == place.astype(F32), 1.0, 0.0).astype(BF16)

    total_grad = dot(table_ref[...], rows_ref[...]) + grad_ref[...].astype(F32)
    out_ref[...] = total_grad.astype(BF16)


def home(tail, rows, grad, experts, cap):
    tok, width = grad.shape
    step = 512
    total = experts * cap
    return pl.pallas_call(
        functools.partial(home_kernel, experts, cap),
        grid=(width // step,),
        in_specs=[
            held((tok, LANES), lambda i: (0, 0)),
            pl.BlockSpec((total, step), lambda i: (0, i)),
            pl.BlockSpec((tok, step), lambda i: (0, i)),
        ],
        out_specs=pl.BlockSpec((tok, step), lambda i: (0, i)),
        out_shape=jax.ShapeDtypeStruct((tok, width), BF16),
        scratch_shapes=[pltpu.VMEM((tok, total), BF16)],
        compiler_params=params(1),
        cost_estimate=cost(3e9, 10e6),
        name="home",
    )(tail, rows, grad)


def up_kernel(count, *refs):
    xs, (wa, wb), outs = refs[:count], refs[count : count + 2], refs[count + 2 :]
    for i in range(count):
        rows = xs[i][...]
        a = dot(rows, wa[...])
        b = dot(rows, wb[...])
        sig = jax.nn.sigmoid(a)
        outs[3 * i][...] = a * sig * b
        outs[3 * i + 1][...] = (b * sig * (1.0 + a * (1.0 - sig))).astype(BF16)
        outs[3 * i + 2][...] = (a * sig).astype(BF16)


def up(xs, wgu):
    count = len(xs)
    rows, width = xs[0].shape
    hidden = wgu.shape[1] // 2
    step = 256
    steps = hidden // step
    kinds = (F32, BF16, BF16) * count
    flat = pl.pallas_call(
        functools.partial(up_kernel, count),
        grid=(steps,),
        in_specs=[held((rows, width), lambda i: (0, 0))] * count
        + [
            pl.BlockSpec((width, step), lambda i: (0, i)),
            pl.BlockSpec((width, step), lambda i: (0, i + steps)),
        ],
        out_specs=[pl.BlockSpec((rows, step), lambda i: (0, i))] * (3 * count),
        out_shape=[jax.ShapeDtypeStruct((rows, hidden), kind) for kind in kinds],
        compiler_params=params(1),
        cost_estimate=cost(3e9, 10e6),
        name="up",
    )(*xs, wgu, wgu)
    return [flat[3 * i : 3 * i + 3] for i in range(count)]


def dh_kernel(count, *refs):
    ss, wd, outs = refs[:count], refs[count], refs[count + 1 :]
    for i in range(count):
        outs[i][...] = dot(ss[i][...], wd[...], 1, 1)


def dh_of(ss, wdown):
    count = len(ss)
    rows, width = ss[0].shape
    hidden = wdown.shape[0]
    step = 256
    return pl.pallas_call(
        functools.partial(dh_kernel, count),
        grid=(hidden // step,),
        in_specs=[held((rows, width), lambda i: (0, 0))] * count
        + [pl.BlockSpec((step, width), lambda i: (i, 0))],
        out_specs=[pl.BlockSpec((rows, step), lambda i: (0, i))] * count,
        out_shape=[jax.ShapeDtypeStruct((rows, hidden), F32)] * count,
        compiler_params=params(1),
        cost_estimate=cost(3e9, 10e6),
        name="dh",
    )(*ss, wdown)


def crossed(parts, j, cap):
    return jnp.concatenate([part[j * cap : (j + 1) * cap, :] for part in parts], axis=0)


def activations(rows, w, t, hidden):
    a = dot(rows, w[:, tile(t, 256)])
    b = dot(rows, w[:, tile(t + hidden // 256, 256)])
    sig = jax.nn.sigmoid(a)
    return a * sig * b, (b * sig * (1.0 + a * (1.0 - sig)), a * sig)


def tile(t, step):
    return pl.ds(pl.multiple_of(t * step, step), step)


def gate_up_load(w, w_v, sems, hidden, t, k):
    part = tile(t + k * (hidden // 256), 256)
    return pltpu.make_async_copy(w.at[:, part], w_v.at[:, part], sems.at[t, k])


def gate_up_loads(w, w_v, sems, hidden):
    for t in range(hidden // 256):
        for k in range(2):
            gate_up_load(w, w_v, sems, hidden, t, k).start()


def row_load(w, w_v, sems, t, step):
    return pltpu.make_async_copy(w.at[tile(t, step), :], w_v.at[tile(t, step), :], sems.at[t])


def send_rows(d_v, w_v, blocks, cap, me_ref, rows_v, out, sems, ready=None):
    hidden = w_v.shape[1] // 2

    def copy_of(t, n, i, j):
        target = out.at[home_of(me_ref, i, j), :, tile(t, 512)]
        return pltpu.make_async_copy(rows_v.at[t, n], target, sems.at[t, n])

    @pl.loop(0, w_v.shape[0] // 512)
    def _(t):
        if ready is not None:
            ready(t)
        w = w_v[tile(t, 512), :]
        part = dot(d_v[0], w[:, :hidden], 1, 1) + dot(d_v[1], w[:, hidden:], 1, 1)
        for n, (i, j) in enumerate(blocks):
            rows_v[t, n] = part[n * cap : (n + 1) * cap].astype(BF16)
            copy_of(t, n, i, j).start()

    @pl.loop(0, w_v.shape[0] // 512)
    def _(t):
        for n, (i, j) in enumerate(blocks):
            copy_of(t, n, i, j).wait()


def middle_kernel(cap, me_ref, *refs):
    w, wd, xs, ss, fs, dh0 = refs[0], refs[1], refs[2:4], refs[4:6], refs[6:8], refs[8]
    h_out, tail_out, dh_out, out, ds = refs[9:11], refs[11], refs[12], refs[13], refs[14:16]
    w_v, wd_v, x_v, s_v, h_v, f_v, dh_v, tail_v, dh_tail_v, d_v, e_v, rows_v = refs[16:28]
    w_sems, wd_sems, in_sems, out_sems, row_sems = refs[28:]
    rows = xs[0].shape[0]
    hidden = wd.shape[0]
    edge = 3 * cap - 8
    x_loads = [begun(xs[n], x_v.at[n], in_sems.at[n]) for n in range(2)]
    gate_up_loads(w, w_v, w_sems, hidden)
    s_loads = [begun(ss[n], s_v.at[n], in_sems.at[2 + n]) for n in range(2)]
    for t in range(hidden // 256):
        row_load(wd, wd_v, wd_sems, t, 256).start()
    f_loads = [begun(fs[k], f_v.at[k, 0], in_sems.at[4 + k]) for k in range(2)]
    f_loads.append(begun(dh0, dh_v.at[0], in_sems.at[6]))
    for load in x_loads:
        load.wait()
    @pl.loop(0, hidden // 256)
    def _(t):
        for k in range(2):
            gate_up_load(w, w_v, w_sems, hidden, t, k).wait()
        for n in range(2):
            h, factors = activations(x_v[n], w_v, t, hidden)
            h_v[n, :, tile(t, 256)] = h
            for k in range(2):
                f_v[k, n + 1, :, tile(t, 256)] = factors[k].astype(BF16)

    copies = [begun(h_v.at[n], h_out[n], out_sems.at[n]) for n in range(2)]
    for load in s_loads:
        load.wait()
    @pl.loop(0, hidden // 256)
    def _(t):
        row_load(wd, wd_v, wd_sems, t, 256).wait()
        for n in range(2):
            dh_v[n + 1, :, tile(t, 256)] = dot(s_v[n], wd_v[tile(t, 256), :], 1, 1)

    for load in f_loads:
        load.wait()
    for j in range(3):
        dh_tail_v[j * cap : (j + 1) * cap, :] = dh_v[j, 3 * cap :, :]
        for k in range(2):
            tail_v[k, j] = f_v[k, j, edge:, :]
    copies.append(begun(dh_tail_v, dh_out, out_sems.at[2]))
    copies.append(begun(tail_v, tail_out, out_sems.at[3]))
    for k in range(2):
        @pl.loop(0, hidden // 256)
        def _(t):
            cols = tile(t, 256)
            chunks = [dh_v[j, :, cols] for j in range(3)]
            kept = []
            for i in range(3):
                factor = f_v[k, i, :, cols].astype(F32)[: 3 * cap]
                product = crossed(chunks, i, cap) * factor
                kept.append(product)
                whole = jnp.concatenate([product, jnp.zeros((cap, 256), F32)], axis=0)
                d_v[k, i * rows : (i + 1) * rows, cols] = whole.astype(BF16)
            e_v[k, :, cols] = jnp.concatenate(kept, axis=0).astype(BF16)

        copies.append(begun(d_v.at[k], ds[k].at[pl.ds(0, 3 * rows), :], out_sems.at[4 + k]))
    blocks = [(i, j) for i in range(3) for j in range(3)]
    send_rows(e_v, w_v, blocks, cap, me_ref, rows_v, out, row_sems)
    for copy in copies:
        copy.wait()


def middle(me, wgu, wdown, xs, ss, factors, dh0, cap):
    rows, width = xs[0].shape
    hidden = wdown.shape[0]
    steps = width // 512
    h = jax.ShapeDtypeStruct((rows, hidden), F32)
    tail = jax.ShapeDtypeStruct((2, 3, cap + 8, hidden), BF16)
    dab = jax.ShapeDtypeStruct((SIDE * rows, hidden), BF16)
    slots = jax.ShapeDtypeStruct((SIDE * SIDE, cap, width), BF16)
    h1, h2, tails, dh_tail, slots, da, db = pl.pallas_call(
        functools.partial(middle_kernel, cap),
        in_specs=[SCALARS] + [FAR] * 9,
        out_specs=[FAR] * 7,
        out_shape=[h, h, tail, jax.ShapeDtypeStruct((3 * cap, hidden), F32), slots, dab, dab],
        scratch_shapes=[
            pltpu.VMEM((width, 2 * hidden), BF16),
            pltpu.VMEM((hidden, width), BF16),
            pltpu.VMEM((2, rows, width), BF16),
            pltpu.VMEM((2, rows, width), BF16),
            pltpu.VMEM((2, rows, hidden), F32),
            pltpu.VMEM((2, 3, rows, hidden), BF16),
            pltpu.VMEM((3, rows, hidden), F32),
            pltpu.VMEM((2, 3, cap + 8, hidden), BF16),
            pltpu.VMEM((3 * cap, hidden), F32),
            pltpu.VMEM((2, 3 * rows, hidden), BF16),
            pltpu.VMEM((2, 9 * cap, hidden), BF16),
            pltpu.VMEM((steps, 9, cap, 512), BF16),
            pltpu.SemaphoreType.DMA((hidden // 256, 2)),
            pltpu.SemaphoreType.DMA((hidden // 256,)),
            pltpu.SemaphoreType.DMA((7,)),
            pltpu.SemaphoreType.DMA((6,)),
            pltpu.SemaphoreType.DMA((steps, 9)),
        ],
        compiler_params=params(0),
        cost_estimate=cost(3e9, 10e6),
        name="middle",
    )(me, wgu, wdown, *xs, *ss, *factors, dh0)
    return [h1, h2], tails, dh_tail, slots, [da, db]


def last_x_kernel(cap, me_ref, *refs):
    w, x, hs, dh_tail = refs[0], refs[1], refs[2:5], refs[5]
    turned_out, tail_out, out, ds = refs[9], refs[10], refs[11], refs[12:14]
    w_v, x_v, h_v, f_v, dh_v, turned_v, d_v, e_v, rows_v = refs[14:23]
    w_sems, in_sems, out_sems, row_sems = refs[23:]
    rows = x.shape[0]
    hidden = w.shape[1] // 2
    edge = 3 * cap - 8
    x_load = begun(x, x_v, in_sems.at[0])
    gate_up_loads(w, w_v, w_sems, hidden)
    loads = [begun(hs[n], h_v.at[n], in_sems.at[1 + n]) for n in range(3)]
    loads.append(begun(dh_tail, dh_v, in_sems.at[4]))
    x_load.wait()
    @pl.loop(0, hidden // 256)
    def _(t):
        for k in range(2):
            gate_up_load(w, w_v, w_sems, hidden, t, k).wait()
        h, factors = activations(x_v[...], w_v, t, hidden)
        h_v[3, :, tile(t, 256)] = h
        for k in range(2):
            f_v[k, :, tile(t, 256)] = factors[k].astype(BF16)

    for load in loads:
        load.wait()
    copies = [begun(f_v.at[:, pl.ds(edge, cap + 8), :], tail_out, out_sems.at[0])]
    @pl.loop(0, hidden // 256)
    def _(t):
        cols = tile(t, 256)
        parts = [h_v[n, :, cols] for n in range(SIDE)]
        whole = jnp.concatenate([crossed(parts, j, cap) for j in range(SIDE)], axis=0)
        turned_v[cols, :] = whole.T.astype(BF16)
        for k in range(2):
            product = dh_v[:, cols] * f_v[k, :, cols].astype(F32)[: 3 * cap]
            e_v[k, :, cols] = product.astype(BF16)
            whole = jnp.concatenate([product, jnp.zeros((cap, 256), F32)], axis=0)
            d_v[k, :, cols] = whole.astype(BF16)

    copies.append(begun(turned_v, turned_out, out_sems.at[1]))
    for k in range(2):
        copies.append(begun(d_v.at[k], ds[k].at[pl.ds(3 * rows, rows), :], out_sems.at[2 + k]))
    blocks = [(3, j) for j in range(3)]
    send_rows(e_v, w_v, blocks, cap, me_ref, rows_v, out, row_sems)
    for copy in copies:
        copy.wait()


def last_x(me, wgu, x, hs, dh_tail, slots, ds, cap):
    rows, width = x.shape
    hidden = wgu.shape[1] // 2
    steps = width // 512
    turned_h, tail, slots, da, db = pl.pallas_call(
        functools.partial(last_x_kernel, cap),
        in_specs=[SCALARS] + [FAR] * 9,
        out_specs=[FAR] * 5,
        out_shape=[
            jax.ShapeDtypeStruct((hidden, SIDE * rows), BF16),
            jax.ShapeDtypeStruct((2, cap + 8, hidden), BF16),
        ]
        + [jax.ShapeDtypeStruct(a.shape, BF16) for a in (slots, *ds)],
        input_output_aliases={7: 2, 8: 3, 9: 4},
        scratch_shapes=[
            pltpu.VMEM((width, 2 * hidden), BF16),
            pltpu.VMEM((rows, width), BF16),
            pltpu.VMEM((SIDE, rows, hidden), F32),
            pltpu.VMEM((2, rows, hidden), BF16),
            pltpu.VMEM((3 * cap, hidden), F32),
            pltpu.VMEM((hidden, SIDE * rows), BF16),
            pltpu.VMEM((2, rows, hidden), BF16),
            pltpu.VMEM((2, 3 * cap, hidden), BF16),
            pltpu.VMEM((steps, 3, cap, 512), BF16),
            pltpu.SemaphoreType.DMA((hidden // 256, 2)),
            pltpu.SemaphoreType.DMA((5,)),
            pltpu.SemaphoreType.DMA((4,)),
            pltpu.SemaphoreType.DMA((steps, 3)),
        ],
        compiler_params=params(0),
        cost_estimate=cost(3e9, 10e6),
        name="last_x",
    )(me, wgu, x, *hs, dh_tail, slots, *ds)
    return turned_h, tail, slots, [da, db]


AHEAD = (2, 1, 3)
SPOTS = (((0, 0), (1, 1)), ((2, 0), (0, 1)), ((1, 0), (2, 1)))


def put_halves(k, part, sent_v, wait_v, outs, sems):
    half = part.shape[0] // 2
    copies = []
    for side in range(2):
        out, row = SPOTS[k][side]
        piece = part[side * half : (side + 1) * half]
        staged = wait_v.at[row] if out == 2 else sent_v.at[out, row]
        staged[...] = piece.astype(BF16)
        target = outs[out].at[row * half : (row + 1) * half, :]
        copies.append(begun(staged, target, sems.at[k, side]))
    return copies


def ahead_of(place_ref, ahead, size):
    start = lax.rem(place_ref[0] + ahead, SIDE) * size
    return pl.ds(pl.multiple_of(start, size), size)


def message_outs(rows, cols):
    return [jax.ShapeDtypeStruct((rows, cols), kind) for kind in (BF16, BF16, BF16)]


def message_scratch(rows, cols):
    return [
        pltpu.VMEM((2, 2, rows // 2, cols), BF16),
        pltpu.VMEM((2, rows // 2, cols), BF16),
        pltpu.SemaphoreType.DMA((3, 2)),
    ]


def last_s_kernel(cap, me_ref, place_ref, *refs):
    turned, ss, wd, tails, tail, w = refs[0], refs[1:5], refs[5], refs[6], refs[7], refs[8]
    outs, out, ds = refs[10:13], refs[13], refs[14:16]
    turned_v, q_v, s_v, wd_v, f_v, d_v, w_v, rows_v = refs[16:24]
    sent_v, wait_v, message_sems, in_sems, q_sems, wd_sems, w_sems, out_sems, row_sems = refs[24:]
    rows, width = ss[0].shape
    hidden = wd.shape[0]
    turned_load = begun(turned, turned_v, in_sems.at[0])
    q_loads = []
    for k, ahead in enumerate(AHEAD):
        cols = ahead_of(place_ref, ahead, width // SIDE)
        for j in range(SIDE):
            part = q_v.at[k, pl.ds(j * rows, rows), :]
            q_loads.append(begun(ss[j].at[:, cols], part, q_sems.at[k, j]))
    s_load = begun(ss[3], s_v, in_sems.at[1])
    for t in range(hidden // 256):
        row_load(wd, wd_v, wd_sems, t, 256).start()
    loads = [begun(tails, f_v.at[:, pl.ds(0, 3)], in_sems.at[2])]
    loads.append(begun(tail, f_v.at[:, 3], in_sems.at[3]))
    for t in range(w.shape[0] // 512):
        row_load(w, w_v, w_sems, t, 512).start()
    turned_load.wait()
    copies = []
    for k in range(3):
        for load in q_loads[4 * k : 4 * k + 4]:
            load.wait()
        part = dot(turned_v[...], q_v[k])
        copies += put_halves(k, part, sent_v, wait_v, outs, message_sems)
    s_load.wait()
    for load in loads:
        load.wait()
    @pl.loop(0, hidden // 256)
    def _(t):
        row_load(wd, wd_v, wd_sems, t, 256).wait()
        cols = tile(t, 256)
        dh = dot(s_v[...], wd_v[cols, :], 1, 1)
        for k in range(2):
            factors = [f_v[k, i, :, cols].astype(F32)[8:] for i in range(SIDE)]
            d_v[k, :, cols] = (dh * jnp.concatenate(factors, axis=0)).astype(BF16)

    copies += [begun(d_v.at[k], ds[k], out_sems.at[k]) for k in range(2)]
    blocks = [(i, 3) for i in range(SIDE)]
    ready = lambda t: row_load(w, w_v, w_sems, t, 512).wait()
    send_rows(d_v, w_v, blocks, cap, me_ref, rows_v, out, row_sems, ready)
    for copy in copies:
        copy.wait()


def last_s(me, place, turned_h, ss, wdown, tails, tail, wgu, slots, cap):
    rows, width = ss[0].shape
    hidden, total = turned_h.shape
    quarter = width // SIDE
    steps = width // 512
    dab = jax.ShapeDtypeStruct((rows, hidden), BF16)
    *down, slots, da, db = pl.pallas_call(
        functools.partial(last_s_kernel, cap),
        in_specs=[SCALARS] * 2 + [FAR] * 10,
        out_specs=[FAR] * 6,
        out_shape=message_outs(hidden, quarter)
        + [jax.ShapeDtypeStruct(slots.shape, BF16), dab, dab],
        input_output_aliases={11: 3},
        scratch_shapes=[
            pltpu.VMEM((hidden, total), BF16),
            pltpu.VMEM((3, total, quarter), BF16),
            pltpu.VMEM((rows, width), BF16),
            pltpu.VMEM((hidden, width), BF16),
            pltpu.VMEM((2, SIDE, cap + 8, hidden), BF16),
            pltpu.VMEM((2, rows, hidden), BF16),
            pltpu.VMEM((width, 2 * hidden), BF16),
            pltpu.VMEM((steps, SIDE, cap, 512), BF16),
        ]
        + message_scratch(hidden, quarter)
        + [
            pltpu.SemaphoreType.DMA((4,)),
            pltpu.SemaphoreType.DMA((3, SIDE)),
            pltpu.SemaphoreType.DMA((hidden // 256,)),
            pltpu.SemaphoreType.DMA((steps,)),
            pltpu.SemaphoreType.DMA((2,)),
            pltpu.SemaphoreType.DMA((steps, SIDE)),
        ],
        compiler_params=params(0),
        cost_estimate=cost(1, 1),
        name="last_s",
    )(me, place, turned_h, *ss, wdown, tails, tail, wgu, slots)
    return down, slots, [da, db]


def down_own_kernel(place_ref, *refs):
    turned_ref, ss, out = refs[0], refs[1:5], refs[5]
    out[...] = dot(turned_ref[...], jnp.concatenate([s[...] for s in ss], axis=0))


def down_own(place, turned_h, ss):
    hidden, total = turned_h.shape
    rows, width = ss[0].shape
    quarter = width // SIDE
    return pl.pallas_call(
        down_own_kernel,
        grid_spec=pltpu.PrefetchScalarGridSpec(
            num_scalar_prefetch=1,
            grid=(2,),
            in_specs=[pl.BlockSpec((hidden // 2, total), lambda i, place: (i, 0))]
            + [held((rows, quarter), lambda i, place: (0, place[0]))] * 4,
            out_specs=pl.BlockSpec((hidden // 2, quarter), lambda i, place: (i, 0)),
        ),
        out_shape=jax.ShapeDtypeStruct((hidden, quarter), F32),
        compiler_params=params(1),
        cost_estimate=cost(1, 1),
        name="down_own",
    )(place, turned_h, *ss)


def gate_up_kernel(cap, place_ref, *refs):
    early, late, xs, outs, ds = refs[:2], refs[2:4], refs[4:8], refs[8:11], refs[11:13]
    d_v, late_v, x_v, sent_v, wait_v, out_sems, d_sems, x_sems = refs[13:]
    rows, width = xs[0].shape
    size = width // SIDE
    edge = 3 * cap - 8

    def dab_loads(k):
        first = begun(early[k], d_v.at[k], d_sems.at[0, k])
        return [first, begun(late[k], late_v.at[k], d_sems.at[1, k])]

    def x_loads(k):
        cols = ahead_of(place_ref, AHEAD[k], size)
        at = [pl.ds(i * rows, rows) for i in range(SIDE)]
        return [begun(xs[i].at[:, cols], x_v.at[k, at[i], :], x_sems.at[k, i]) for i in range(SIDE)]

    def filled(k, loads):
        for load in loads:
            load.wait()
        fresh = late_v[k].astype(F32)
        for i in range(SIDE):
            at = slice(i * rows + edge, (i + 1) * rows)
            old = d_v[k, at, :].astype(F32)[:8]
            new = fresh[i * cap : (i + 1) * cap]
            d_v[k, at, :] = jnp.concatenate([old, new], axis=0).astype(BF16)
        return begun(d_v.at[k], ds[k], d_sems.at[2, k])

    first, quarters = dab_loads(0), [x_loads(0)]
    second = dab_loads(1)
    quarters += [x_loads(1), x_loads(2)]
    copies = [filled(0, first)]
    for k in range(3):
        for load in quarters[k]:
            load.wait()
        turned_x = x_v[k].T
        part = dot(turned_x, d_v[0])
        if k == 0:
            copies.append(filled(1, second))
        part = jnp.concatenate([part, dot(turned_x, d_v[1])], axis=1)
        copies += put_halves(k, part, sent_v, wait_v, outs, out_sems)
    for copy in copies:
        copy.wait()


def gate_up_parts(place, early, late, xs, cap):
    rows, width = xs[0].shape
    total, hidden = early[0].shape
    quarter = width // SIDE
    out = jax.ShapeDtypeStruct((total, hidden), BF16)
    *messages, da, db = pl.pallas_call(
        functools.partial(gate_up_kernel, cap),
        in_specs=[SCALARS] + [FAR] * 8,
        out_specs=[FAR] * 5,
        out_shape=message_outs(quarter, 2 * hidden) + [out, out],
        scratch_shapes=[
            pltpu.VMEM((2, total, hidden), BF16),
            pltpu.VMEM((2, *late[0].shape), BF16),
            pltpu.VMEM((3, total, quarter), BF16),
        ]
        + message_scratch(quarter, 2 * hidden)
        + [pltpu.SemaphoreType.DMA((3, 2)), pltpu.SemaphoreType.DMA((3, SIDE))],
        compiler_params=params(0),
        cost_estimate=cost(1, 1),
        name="gate_up_parts",
    )(place, *early, *late, *xs)
    return messages, [da, db]


def gate_up_own_kernel(place_ref, *refs):
    xs, ds, out = refs[:4], refs[4:6], refs[6]
    rows = jnp.concatenate([x[...] for x in xs], axis=0).T
    out[...] = jnp.concatenate([dot(rows, d[...]) for d in ds], axis=1)


def gate_up_own(place, xs, ds):
    rows, width = xs[0].shape
    total, hidden = ds[0].shape
    half = width // SIDE // 2
    return pl.pallas_call(
        gate_up_own_kernel,
        grid_spec=pltpu.PrefetchScalarGridSpec(
            num_scalar_prefetch=1,
            grid=(2,),
            in_specs=[pl.BlockSpec((rows, half), lambda i, place: (0, 2 * place[0] + i))] * 4
            + [held((total, hidden), lambda i, place: (0, 0))] * 2,
            out_specs=pl.BlockSpec((half, 2 * hidden), lambda i, place: (i, 0)),
        ),
        out_shape=jax.ShapeDtypeStruct((2 * half, 2 * hidden), F32),
        compiler_params=params(1),
        cost_estimate=cost(200e9, 10e6),
        name="gate_up_own",
    )(place, *xs, *ds)


def around(first, axis):
    return [first] + [moved_along(first, axis, OFF[b]) for b in range(1, SIDE)]


def spread(outs, axis, work):
    near = [moved_along(outs[j], axis, OFF[j]) for j in (1, 2)]
    done = work(outs[0])
    far, near[0], near[1], *done = lax.optimization_barrier((outs[3], *near, *done))
    return [outs[0], *near, moved_along(far, axis, OFF[3])], done


def ring_first(first_up, first_down, wait):
    return moved_along(first_up, "edata", 1), moved_along(first_down, "edata", -1)


def ring_second(up1, down1, first_up, first_down, wait):
    half = wait.shape[0] // 2
    second_up = (wait[:half].astype(F32) + up1[:half].astype(F32)).astype(BF16)
    second_down = (wait[half:].astype(F32) + down1[half:].astype(F32)).astype(BF16)
    return moved_along(second_up, "edata", 1), moved_along(second_down, "edata", -1)


def ring_own(own, up1, down1):
    half = own.shape[0] // 2
    return own[:half] + down1[:half].astype(F32), own[half:] + up1[half:].astype(F32)


def ring_last(total, up2, down2):
    messages = jnp.concatenate([up2, down2], axis=0).astype(F32)
    return (jnp.concatenate(total, axis=0) + messages).astype(BF16)


def body(hidden_in, out_grad, routes, gates, w_gate_up, w_down):
    tok = hidden_in.shape[1]
    width = hidden_in.shape[2]
    topk = routes.shape[2]
    experts = lax.axis_size("expert")
    cap = min(tok, tok * topk * 9 // (8 * experts))
    wgu, wdown = w_gate_up[0, 0], w_down[0, 0]
    me = lax.axis_index("expert").astype(jnp.int32).reshape(1)
    place = lax.axis_index("edata").astype(jnp.int32).reshape(1)

    xe, ge, tail = prep(routes[0].T, gates[0].T, hidden_in[0], out_grad[0], experts)
    xblocks = around(xe, "x")
    gblocks = around(ge, "z")
    def packed(blocks, scale, name, which):
        steps_to = tuple((OFF[j], 0) if scale else (0, OFF[j]) for j in which)
        return list(pack(me, blocks, width, experts, cap, steps_to, scale, name))

    xnear = packed(xblocks, False, "pack_rows", (1, 2))
    xnear[0], gblocks[0] = lax.optimization_barrier((xnear[0], gblocks[0]))
    gnear = packed(gblocks, True, "pack_scaled", (1, 2))
    xblocks[0], gnear[0] = lax.optimization_barrier((xblocks[0], gnear[0]))
    x0, xfar = packed(xblocks, False, "pack_rows_rest", (0, 3))
    s0, sfar = packed(gblocks, True, "pack_scaled_rest", (0, 3))
    xs, (h0, *factors) = spread([x0, *xnear, xfar], "z", lambda rows: up([rows], wgu)[0])
    ss, (dh0,) = spread([s0, *gnear, sfar], "x", lambda rows: dh_of([rows], wdown))
    hs, tails, dh_tail, slots, early = middle(
        me, wgu, wdown, xs[1:3], ss[1:3], factors, dh0, cap
    )
    turned_h, last_tail, slots, early = last_x(
        me, wgu, xs[3], [h0, *hs], dh_tail, slots, early, cap
    )
    last, slots, turned_h = lax.optimization_barrier((ss[3], slots, turned_h))
    ss = ss[:3] + [last]
    down, rows, late = last_s(me, place, turned_h, ss, wdown, tails, last_tail, wgu, slots, cap)
    down_first = ring_first(*down)
    returned = lax.all_to_all(rows, "expert", split_axis=0, concat_axis=0, tiled=True)
    rows, *late = lax.optimization_barrier((rows, *late))
    gate_up, ds = gate_up_parts(place, early, late, xs, cap)
    gate_up[0], gate_up[1], *down_first = lax.optimization_barrier((gate_up[0], gate_up[1], *down_first))
    gate_up_first = ring_first(*gate_up)
    wait, da, db, turned_h = lax.optimization_barrier((gate_up[2], *ds, turned_h))
    gate_up = [*gate_up[:2], wait]
    own_down = down_own(place, turned_h, ss)
    own_gate_up = gate_up_own(place, xs, [da, db])
    own_down, own_gate_up, *gate_up_first = lax.optimization_barrier(
        (own_down, own_gate_up, *gate_up_first)
    )
    down_second = ring_second(*down_first, *down)
    gate_up_second = ring_second(*gate_up_first, *gate_up)
    returned, own_down, own_gate_up, *firsts = lax.optimization_barrier(
        (returned, own_down, own_gate_up, *down_first, *gate_up_first)
    )
    totals = (*ring_own(own_down, *firsts[:2]), *ring_own(own_gate_up, *firsts[2:]))
    totals = lax.optimization_barrier(totals)
    layer = home(tail, returned.reshape(experts * cap, width), out_grad[0], experts, cap)
    upstream = moved_along(layer, "section", -1)
    down_grad = ring_last(totals[:2], *down_second)
    gate_up_grad = ring_last(totals[2:], *gate_up_second)
    return (upstream[None], gate_up_grad[None, None], down_grad[None, None])


def solution(mesh):
    return jax.shard_map(
        body,
        mesh=mesh,
        in_specs=(
            P("section", ("edata", "expert"), None),
            P("section", ("edata", "expert"), None),
            P("section", ("edata", "expert"), None),
            P("section", ("edata", "expert"), None),
            P("section", "expert", None, None),
            P("section", "expert", None, None),
        ),
        out_specs=(
            P("section", ("edata", "expert"), None),
            P("section", "expert", "edata", None),
            P("section", "expert", None, "edata"),
        ),
        check_vma=False,
    )
```

```python
import functools

import jax
import jax.numpy as jnp
from jax import lax
from jax.experimental import pallas as pl
from jax.experimental.pallas import tpu as pltpu
from jax.sharding import PartitionSpec as P

BF16 = jnp.bfloat16
F32 = jnp.float32
OFF = (0, 1, 3, 2)
SIDE = 4
LANES = 128
MIB = 1024 * 1024


def params(steps):
    return pltpu.CompilerParams(
        vmem_limit_bytes=58 * MIB, dimension_semantics=("arbitrary",) * steps
    )


SCALARS = pl.BlockSpec(memory_space=pltpu.SMEM)
FAR = pl.BlockSpec(memory_space=pl.ANY)


def begun(src, dst, sem):
    copy = pltpu.make_async_copy(src, dst, sem)
    copy.start()
    return copy


def expert_at(me_ref, dx, dz):
    x, z = lax.div(me_ref[0], SIDE), lax.rem(me_ref[0], SIDE)
    return lax.rem(x + dx, SIDE) * SIDE + lax.rem(z + dz, SIDE)


def home_of(me_ref, i, j):
    return expert_at(me_ref, SIDE - OFF[j], SIDE - OFF[i])


def held(shape, index):
    return pl.BlockSpec(shape, index, pipeline_mode=pl.Buffered(1))


def cost(flops, moved):
    return pl.CostEstimate(flops=int(flops), bytes_accessed=int(moved), transcendentals=0)


def moved_along(block, axis, distance):
    if axis == "edata" or axis == "section":
        size = lax.axis_size(axis)
        return lax.ppermute(block, axis, [(i, (i + distance) % size) for i in range(size)])
    pairs = []
    for a in range(SIDE):
        for b in range(SIDE):
            if axis == "x":
                pairs.append((a * SIDE + b, (a + distance) % SIDE * SIDE + b))
            else:
                pairs.append((a * SIDE + b, a * SIDE + (b + distance) % SIDE))
    return lax.ppermute(block, "expert", pairs)


def iota(shape, dim):
    return lax.broadcasted_iota(jnp.int32, shape, dim)


def dot(a, b, da=1, db=0):
    return lax.dot_general(a, b, (((da,), (db,)), ((), ())), preferred_element_type=F32)


def prep_kernel(experts, routes_ref, gates_ref, x_ref, g_ref, xe_ref, ge_ref, tail_ref):
    tok, width = x_ref.shape
    topk = routes_ref.shape[0]
    expert = lax.rem(iota((LANES, tok), 0), experts)
    full = jnp.zeros((LANES, tok), F32)
    for k in range(topk):
        full += jnp.where(routes_ref[k : k + 1, :] == expert, gates_ref[k : k + 1, :], 0.0)
    full = full.T
    lane = iota((tok, LANES), 1)
    high = full.astype(BF16).astype(F32)
    rest = full - high
    middle = rest.astype(BF16).astype(F32)
    low = rest - middle
    piece = jnp.where(lane < 2 * experts, middle, jnp.where(lane < 3 * experts, low, 0.0))
    piece = jnp.where(lane < experts, high, piece).astype(BF16)
    for src, dst in ((x_ref, xe_ref), (g_ref, ge_ref)):
        dst[:, :width] = src[...]
        dst[:, width:] = piece
    tail_ref[...] = piece


def prep(routes, gates, x, g, experts):
    tok, width = x.shape
    shape = jax.ShapeDtypeStruct((tok, width + LANES), BF16)
    return pl.pallas_call(
        functools.partial(prep_kernel, experts),
        out_shape=(shape, shape, jax.ShapeDtypeStruct((tok, LANES), BF16)),
        compiler_params=params(0),
        name="prep",
    )(routes, gates, x, g)


def places(piece, experts, blocks):
    rows = piece.shape[0]
    tok = rows // blocks
    r, c = iota((rows, rows), 0), iota((rows, rows), 1)
    upto = jnp.where((c <= r) & (lax.div(c, tok) == lax.div(r, tok)), 1.0, 0.0).astype(BF16)
    lane = iota((rows, LANES), 1)
    mask = jnp.where((lane < experts) & (piece.astype(F32) > 0.0), 1.0, 0.0)
    return (dot(upto, mask.astype(BF16)) * mask).astype(BF16)


def pack_kernel(scale, experts, cap, steps_to, me_ref, *refs):
    blocks, outs = refs[:4], refs[4:-5]
    rows_v, packed_v, table_v, in_sems, out_sems = refs[-5:]
    count = len(outs)
    eids = [expert_at(me_ref, dx, dz) for dx, dz in steps_to]
    pair = 2 * cap
    tok, width = blocks[0].shape[0], outs[0].shape[1]
    steps, step = packed_v.shape[0], packed_v.shape[3]
    pieces = [slice(width, width + LANES)] + [slice(t * step, (t + 1) * step) for t in range(steps)]
    loads = []
    for n, cols in enumerate(pieces):
        for b in range(4):
            part = rows_v.at[b // 2, pl.ds(b % 2 * tok, tok), cols]
            loads.append(begun(blocks[b].at[:, cols], part, in_sems.at[n, b]))
    for load in loads[:4]:
        load.wait()
    lane = iota((pair, LANES), 1)
    second = jnp.where(iota((pair, 2 * tok), 1) >= tok, cap, 0)
    place = iota((pair, 2 * tok), 0) + 1 - second
    place = jnp.where(place > 0, place, -1).astype(F32)
    factors = []
    for p in range(2):
        piece = rows_v[p, :, width:]
        known = places(piece, experts, 2)
        for j in range(count):
            choose = jnp.where(lane == eids[j], 1.0, 0.0).astype(BF16)
            found = dot(choose, known, 1, 1)
            table = jnp.where(found == place, 1.0, 0.0).astype(BF16)
            table_v[p, j * pair : (j + 1) * pair, :] = table
            if scale:
                mine = (lax.rem(lane, experts) == eids[j]) & (lane < 3 * experts)
                gate = jnp.where(mine, dot(table, piece), 0.0)
                factors.append(jnp.sum(gate, axis=1, keepdims=True))
    stores = []
    for t in range(steps):
        for load in loads[4 * t + 4 : 4 * t + 8]:
            load.wait()
        for p in range(2):
            packed = dot(table_v[p], rows_v[p, :, pieces[t + 1]])
            for j in range(count):
                part = packed[j * pair : (j + 1) * pair]
                if scale:
                    part = part * factors[p * count + j]
                packed_v[t, j, p * pair : (p + 1) * pair, :] = part.astype(BF16)
        for j in range(count):
            target = outs[j].at[:, pieces[t + 1]]
            stores.append(begun(packed_v.at[t, j], target, out_sems.at[t, j]))
    for store in stores:
        store.wait()


def pack(me, blocks, width, experts, cap, steps_to, scale, name):
    count = len(steps_to)
    tok = blocks[0].shape[0]
    step = 512
    steps = width // step
    pair = 2 * cap
    out = jax.ShapeDtypeStruct((2 * pair, width), BF16)
    return pl.pallas_call(
        functools.partial(pack_kernel, scale, experts, cap, steps_to),
        in_specs=[SCALARS] + [FAR] * 4,
        out_specs=[FAR] * count,
        out_shape=[out] * count,
        scratch_shapes=[
            pltpu.VMEM((2, 2 * tok, width + LANES), BF16),
            pltpu.VMEM((steps, count, 2 * pair, step), BF16),
            pltpu.VMEM((2, count * pair, 2 * tok), BF16),
            pltpu.SemaphoreType.DMA((steps + 1, 4)),
            pltpu.SemaphoreType.DMA((steps, count)),
        ],
        compiler_params=params(0),
        cost_estimate=cost(3e9, 10e6),
        name=name,
    )(me, *blocks)


def home_kernel(experts, cap, tail_ref, rows_ref, grad_ref, out_ref, table_ref):
    tok = tail_ref.shape[0]
    total = experts * cap

    @pl.when(pl.program_id(0) == 0)
    def _():
        choose = jnp.where(iota((LANES, total), 0) == lax.div(iota((LANES, total), 1), cap), 1.0, 0.0)
        found = dot(places(tail_ref[...], experts, 1), choose.astype(BF16))
        place = lax.rem(iota((tok, total), 1), cap) + 1
        table_ref[...] = jnp.where(found == place.astype(F32), 1.0, 0.0).astype(BF16)

    total_grad = dot(table_ref[...], rows_ref[...]) + grad_ref[...].astype(F32)
    out_ref[...] = total_grad.astype(BF16)


def home(tail, rows, grad, experts, cap):
    tok, width = grad.shape
    step = 512
    total = experts * cap
    return pl.pallas_call(
        functools.partial(home_kernel, experts, cap),
        grid=(width // step,),
        in_specs=[
            held((tok, LANES), lambda i: (0, 0)),
            pl.BlockSpec((total, step), lambda i: (0, i)),
            pl.BlockSpec((tok, step), lambda i: (0, i)),
        ],
        out_specs=pl.BlockSpec((tok, step), lambda i: (0, i)),
        out_shape=jax.ShapeDtypeStruct((tok, width), BF16),
        scratch_shapes=[pltpu.VMEM((tok, total), BF16)],
        compiler_params=params(1),
        cost_estimate=cost(3e9, 10e6),
        name="home",
    )(tail, rows, grad)


def up_kernel(count, *refs):
    xs, (wa, wb), outs = refs[:count], refs[count : count + 2], refs[count + 2 :]
    for i in range(count):
        rows = xs[i][...]
        a = dot(rows, wa[...])
        b = dot(rows, wb[...])
        sig = jax.nn.sigmoid(a)
        outs[3 * i][...] = a * sig * b
        outs[3 * i + 1][...] = b * sig * (1.0 + a * (1.0 - sig))
        outs[3 * i + 2][...] = a * sig


def up(xs, wgu):
    count = len(xs)
    rows, width = xs[0].shape
    hidden = wgu.shape[1] // 2
    step = 256
    steps = hidden // step
    flat = pl.pallas_call(
        functools.partial(up_kernel, count),
        grid=(steps,),
        in_specs=[held((rows, width), lambda i: (0, 0))] * count
        + [
            pl.BlockSpec((width, step), lambda i: (0, i)),
            pl.BlockSpec((width, step), lambda i: (0, i + steps)),
        ],
        out_specs=[pl.BlockSpec((rows, step), lambda i: (0, i))] * (3 * count),
        out_shape=[jax.ShapeDtypeStruct((rows, hidden), F32)] * (3 * count),
        compiler_params=params(1),
        cost_estimate=cost(3e9, 10e6),
        name="up",
    )(*xs, wgu, wgu)
    return [flat[3 * i : 3 * i + 3] for i in range(count)]


def dh_kernel(count, *refs):
    ss, wd, outs = refs[:count], refs[count], refs[count + 1 :]
    for i in range(count):
        outs[i][...] = dot(ss[i][...], wd[...], 1, 1)


def dh_of(ss, wdown):
    count = len(ss)
    rows, width = ss[0].shape
    hidden = wdown.shape[0]
    step = 256
    return pl.pallas_call(
        functools.partial(dh_kernel, count),
        grid=(hidden // step,),
        in_specs=[held((rows, width), lambda i: (0, 0))] * count
        + [pl.BlockSpec((step, width), lambda i: (i, 0))],
        out_specs=[pl.BlockSpec((rows, step), lambda i: (0, i))] * count,
        out_shape=[jax.ShapeDtypeStruct((rows, hidden), F32)] * count,
        compiler_params=params(1),
        cost_estimate=cost(3e9, 10e6),
        name="dh",
    )(*ss, wdown)


def crossed(parts, j, cap):
    return jnp.concatenate([part[j * cap : (j + 1) * cap, :] for part in parts], axis=0)


def activations(rows, w, t, hidden):
    a = dot(rows, w[:, tile(t, 256)])
    b = dot(rows, w[:, tile(t + hidden // 256, 256)])
    sig = jax.nn.sigmoid(a)
    return a * sig * b, (b * sig * (1.0 + a * (1.0 - sig)), a * sig)


def tile(t, step):
    return pl.ds(pl.multiple_of(t * step, step), step)


def gate_up_load(w, w_v, sems, hidden, t, k):
    part = tile(t + k * (hidden // 256), 256)
    return pltpu.make_async_copy(w.at[:, part], w_v.at[:, part], sems.at[t, k])


def gate_up_loads(w, w_v, sems, hidden):
    for t in range(hidden // 256):
        for k in range(2):
            gate_up_load(w, w_v, sems, hidden, t, k).start()


def row_load(w, w_v, sems, t, step):
    return pltpu.make_async_copy(w.at[tile(t, step), :], w_v.at[tile(t, step), :], sems.at[t])


def send_rows(d_v, w_v, blocks, cap, me_ref, rows_v, out, sems, ready=None):
    hidden = w_v.shape[1] // 2

    def copy_of(t, n, i, j):
        target = out.at[home_of(me_ref, i, j), :, tile(t, 512)]
        return pltpu.make_async_copy(rows_v.at[t, n], target, sems.at[t, n])

    @pl.loop(0, w_v.shape[0] // 512)
    def _(t):
        if ready is not None:
            ready(t)
        w = w_v[tile(t, 512), :]
        part = dot(d_v[0], w[:, :hidden], 1, 1) + dot(d_v[1], w[:, hidden:], 1, 1)
        for n, (i, j) in enumerate(blocks):
            rows_v[t, n] = part[n * cap : (n + 1) * cap].astype(BF16)
            copy_of(t, n, i, j).start()

    @pl.loop(0, w_v.shape[0] // 512)
    def _(t):
        for n, (i, j) in enumerate(blocks):
            copy_of(t, n, i, j).wait()


def middle_kernel(cap, me_ref, *refs):
    w, wd, xs, ss, fs, dh0 = refs[0], refs[1], refs[2:4], refs[4:6], refs[6:8], refs[8]
    h_out, tail_out, dh_out, out, ds = refs[9:11], refs[11], refs[12], refs[13], refs[14:16]
    w_v, wd_v, x_v, s_v, h_v, f_v, dh_v, tail_v, dh_tail_v, d_v, e_v, rows_v = refs[16:28]
    w_sems, wd_sems, in_sems, out_sems, row_sems = refs[28:]
    rows = xs[0].shape[0]
    hidden = wd.shape[0]
    edge = 3 * cap - 8
    x_loads = [begun(xs[n], x_v.at[n], in_sems.at[n]) for n in range(2)]
    gate_up_loads(w, w_v, w_sems, hidden)
    s_loads = [begun(ss[n], s_v.at[n], in_sems.at[2 + n]) for n in range(2)]
    for t in range(hidden // 256):
        row_load(wd, wd_v, wd_sems, t, 256).start()
    f_loads = [begun(fs[k], f_v.at[k, 0], in_sems.at[4 + k]) for k in range(2)]
    f_loads.append(begun(dh0, dh_v.at[0], in_sems.at[6]))
    for load in x_loads:
        load.wait()
    @pl.loop(0, hidden // 256)
    def _(t):
        for k in range(2):
            gate_up_load(w, w_v, w_sems, hidden, t, k).wait()
        for n in range(2):
            h, factors = activations(x_v[n], w_v, t, hidden)
            h_v[n, :, tile(t, 256)] = h
            for k in range(2):
                f_v[k, n + 1, :, tile(t, 256)] = factors[k]

    copies = [begun(h_v.at[n], h_out[n], out_sems.at[n]) for n in range(2)]
    for load in s_loads:
        load.wait()
    @pl.loop(0, hidden // 256)
    def _(t):
        row_load(wd, wd_v, wd_sems, t, 256).wait()
        for n in range(2):
            dh_v[n + 1, :, tile(t, 256)] = dot(s_v[n], wd_v[tile(t, 256), :], 1, 1)

    for load in f_loads:
        load.wait()
    for j in range(3):
        dh_tail_v[j * cap : (j + 1) * cap, :] = dh_v[j, 3 * cap :, :]
        for k in range(2):
            tail_v[k, j] = f_v[k, j, edge:, :]
    copies.append(begun(dh_tail_v, dh_out, out_sems.at[2]))
    copies.append(begun(tail_v, tail_out, out_sems.at[3]))
    for k in range(2):
        @pl.loop(0, hidden // 256)
        def _(t):
            cols = tile(t, 256)
            chunks = [dh_v[j, :, cols] for j in range(3)]
            kept = []
            for i in range(3):
                factor = f_v[k, i, :, cols][: 3 * cap]
                product = crossed(chunks, i, cap) * factor
                kept.append(product)
                whole = jnp.concatenate([product, jnp.zeros((cap, 256), F32)], axis=0)
                d_v[k, i * rows : (i + 1) * rows, cols] = whole.astype(BF16)
            e_v[k, :, cols] = jnp.concatenate(kept, axis=0).astype(BF16)

        copies.append(begun(d_v.at[k], ds[k].at[pl.ds(0, 3 * rows), :], out_sems.at[4 + k]))
    blocks = [(i, j) for i in range(3) for j in range(3)]
    send_rows(e_v, w_v, blocks, cap, me_ref, rows_v, out, row_sems)
    for copy in copies:
        copy.wait()


def middle(me, wgu, wdown, xs, ss, factors, dh0, cap):
    rows, width = xs[0].shape
    hidden = wdown.shape[0]
    steps = width // 512
    h = jax.ShapeDtypeStruct((rows, hidden), F32)
    tail = jax.ShapeDtypeStruct((2, 3, cap + 8, hidden), F32)
    dab = jax.ShapeDtypeStruct((SIDE * rows, hidden), BF16)
    slots = jax.ShapeDtypeStruct((SIDE * SIDE, cap, width), BF16)
    h1, h2, tails, dh_tail, slots, da, db = pl.pallas_call(
        functools.partial(middle_kernel, cap),
        in_specs=[SCALARS] + [FAR] * 9,
        out_specs=[FAR] * 7,
        out_shape=[h, h, tail, jax.ShapeDtypeStruct((3 * cap, hidden), F32), slots, dab, dab],
        scratch_shapes=[
            pltpu.VMEM((width, 2 * hidden), BF16),
            pltpu.VMEM((hidden, width), BF16),
            pltpu.VMEM((2, rows, width), BF16),
            pltpu.VMEM((2, rows, width), BF16),
            pltpu.VMEM((2, rows, hidden), F32),
            pltpu.VMEM((2, 3, rows, hidden), F32),
            pltpu.VMEM((3, rows, hidden), F32),
            pltpu.VMEM((2, 3, cap + 8, hidden), F32),
            pltpu.VMEM((3 * cap, hidden), F32),
            pltpu.VMEM((2, 3 * rows, hidden), BF16),
            pltpu.VMEM((2, 9 * cap, hidden), BF16),
            pltpu.VMEM((steps, 9, cap, 512), BF16),
            pltpu.SemaphoreType.DMA((hidden // 256, 2)),
            pltpu.SemaphoreType.DMA((hidden // 256,)),
            pltpu.SemaphoreType.DMA((7,)),
            pltpu.SemaphoreType.DMA((6,)),
            pltpu.SemaphoreType.DMA((steps, 9)),
        ],
        compiler_params=params(0),
        cost_estimate=cost(3e9, 10e6),
        name="middle",
    )(me, wgu, wdown, *xs, *ss, *factors, dh0)
    return [h1, h2], tails, dh_tail, slots, [da, db]


def last_x_kernel(cap, me_ref, *refs):
    w, x, hs, dh_tail = refs[0], refs[1], refs[2:5], refs[5]
    turned_out, tail_out, out, ds = refs[9], refs[10], refs[11], refs[12:14]
    w_v, x_v, h_v, f_v, dh_v, turned_v, d_v, e_v, rows_v = refs[14:23]
    w_sems, in_sems, out_sems, row_sems = refs[23:]
    rows = x.shape[0]
    hidden = w.shape[1] // 2
    edge = 3 * cap - 8
    x_load = begun(x, x_v, in_sems.at[0])
    gate_up_loads(w, w_v, w_sems, hidden)
    loads = [begun(hs[n], h_v.at[n], in_sems.at[1 + n]) for n in range(3)]
    loads.append(begun(dh_tail, dh_v, in_sems.at[4]))
    x_load.wait()
    @pl.loop(0, hidden // 256)
    def _(t):
        for k in range(2):
            gate_up_load(w, w_v, w_sems, hidden, t, k).wait()
        h, factors = activations(x_v[...], w_v, t, hidden)
        h_v[3, :, tile(t, 256)] = h
        for k in range(2):
            f_v[k, :, tile(t, 256)] = factors[k]

    for load in loads:
        load.wait()
    copies = [begun(f_v.at[:, pl.ds(edge, cap + 8), :], tail_out, out_sems.at[0])]
    @pl.loop(0, hidden // 256)
    def _(t):
        cols = tile(t, 256)
        parts = [h_v[n, :, cols] for n in range(SIDE)]
        whole = jnp.concatenate([crossed(parts, j, cap) for j in range(SIDE)], axis=0)
        turned_v[cols, :] = whole.T.astype(BF16)
        for k in range(2):
            product = dh_v[:, cols] * f_v[k, :, cols][: 3 * cap]
            e_v[k, :, cols] = product.astype(BF16)
            whole = jnp.concatenate([product, jnp.zeros((cap, 256), F32)], axis=0)
            d_v[k, :, cols] = whole.astype(BF16)

    copies.append(begun(turned_v, turned_out, out_sems.at[1]))
    for k in range(2):
        copies.append(begun(d_v.at[k], ds[k].at[pl.ds(3 * rows, rows), :], out_sems.at[2 + k]))
    blocks = [(3, j) for j in range(3)]
    send_rows(e_v, w_v, blocks, cap, me_ref, rows_v, out, row_sems)
    for copy in copies:
        copy.wait()


def last_x(me, wgu, x, hs, dh_tail, slots, ds, cap):
    rows, width = x.shape
    hidden = wgu.shape[1] // 2
    steps = width // 512
    turned_h, tail, slots, da, db = pl.pallas_call(
        functools.partial(last_x_kernel, cap),
        in_specs=[SCALARS] + [FAR] * 9,
        out_specs=[FAR] * 5,
        out_shape=[
            jax.ShapeDtypeStruct((hidden, SIDE * rows), BF16),
            jax.ShapeDtypeStruct((2, cap + 8, hidden), F32),
        ]
        + [jax.ShapeDtypeStruct(a.shape, BF16) for a in (slots, *ds)],
        input_output_aliases={7: 2, 8: 3, 9: 4},
        scratch_shapes=[
            pltpu.VMEM((width, 2 * hidden), BF16),
            pltpu.VMEM((rows, width), BF16),
            pltpu.VMEM((SIDE, rows, hidden), F32),
            pltpu.VMEM((2, rows, hidden), F32),
            pltpu.VMEM((3 * cap, hidden), F32),
            pltpu.VMEM((hidden, SIDE * rows), BF16),
            pltpu.VMEM((2, rows, hidden), BF16),
            pltpu.VMEM((2, 3 * cap, hidden), BF16),
            pltpu.VMEM((steps, 3, cap, 512), BF16),
            pltpu.SemaphoreType.DMA((hidden // 256, 2)),
            pltpu.SemaphoreType.DMA((5,)),
            pltpu.SemaphoreType.DMA((4,)),
            pltpu.SemaphoreType.DMA((steps, 3)),
        ],
        compiler_params=params(0),
        cost_estimate=cost(3e9, 10e6),
        name="last_x",
    )(me, wgu, x, *hs, dh_tail, slots, *ds)
    return turned_h, tail, slots, [da, db]


AHEAD = (2, 1, 3)
SPOTS = (((0, 0), (1, 1)), ((2, 0), (0, 1)), ((1, 0), (2, 1)))


def put_halves(k, part, sent_v, wait_v, outs, sems):
    half = part.shape[0] // 2
    copies = []
    for side in range(2):
        out, row = SPOTS[k][side]
        piece = part[side * half : (side + 1) * half]
        staged = wait_v.at[row] if out == 2 else sent_v.at[out, row]
        staged[...] = piece.astype(BF16)
        target = outs[out].at[row * half : (row + 1) * half, :]
        copies.append(begun(staged, target, sems.at[k, side]))
    return copies


def ahead_of(place_ref, ahead, size):
    start = lax.rem(place_ref[0] + ahead, SIDE) * size
    return pl.ds(pl.multiple_of(start, size), size)


def message_outs(rows, cols):
    return [jax.ShapeDtypeStruct((rows, cols), kind) for kind in (BF16, BF16, BF16)]


def message_scratch(rows, cols):
    return [
        pltpu.VMEM((2, 2, rows // 2, cols), BF16),
        pltpu.VMEM((2, rows // 2, cols), BF16),
        pltpu.SemaphoreType.DMA((3, 2)),
    ]


def last_s_kernel(cap, me_ref, place_ref, *refs):
    turned, ss, wd, tails, tail, w = refs[0], refs[1:5], refs[5], refs[6], refs[7], refs[8]
    outs, out, ds = refs[10:13], refs[13], refs[14:16]
    turned_v, q_v, s_v, wd_v, f_v, d_v, w_v, rows_v = refs[16:24]
    sent_v, wait_v, message_sems, in_sems, q_sems, wd_sems, w_sems, out_sems, row_sems = refs[24:]
    rows, width = ss[0].shape
    hidden = wd.shape[0]
    turned_load = begun(turned, turned_v, in_sems.at[0])
    q_loads = []
    for k, ahead in enumerate(AHEAD):
        cols = ahead_of(place_ref, ahead, width // SIDE)
        for j in range(SIDE):
            part = q_v.at[k, pl.ds(j * rows, rows), :]
            q_loads.append(begun(ss[j].at[:, cols], part, q_sems.at[k, j]))
    s_load = begun(ss[3], s_v, in_sems.at[1])
    for t in range(hidden // 256):
        row_load(wd, wd_v, wd_sems, t, 256).start()
    loads = [begun(tails, f_v.at[:, pl.ds(0, 3)], in_sems.at[2])]
    loads.append(begun(tail, f_v.at[:, 3], in_sems.at[3]))
    for t in range(w.shape[0] // 512):
        row_load(w, w_v, w_sems, t, 512).start()
    turned_load.wait()
    copies = []
    for k in range(3):
        for load in q_loads[4 * k : 4 * k + 4]:
            load.wait()
        part = dot(turned_v[...], q_v[k])
        copies += put_halves(k, part, sent_v, wait_v, outs, message_sems)
    s_load.wait()
    for load in loads:
        load.wait()
    @pl.loop(0, hidden // 256)
    def _(t):
        row_load(wd, wd_v, wd_sems, t, 256).wait()
        cols = tile(t, 256)
        dh = dot(s_v[...], wd_v[cols, :], 1, 1)
        for k in range(2):
            factors = [f_v[k, i, :, cols][8:] for i in range(SIDE)]
            d_v[k, :, cols] = (dh * jnp.concatenate(factors, axis=0)).astype(BF16)

    copies += [begun(d_v.at[k], ds[k], out_sems.at[k]) for k in range(2)]
    blocks = [(i, 3) for i in range(SIDE)]
    ready = lambda t: row_load(w, w_v, w_sems, t, 512).wait()
    send_rows(d_v, w_v, blocks, cap, me_ref, rows_v, out, row_sems, ready)
    for copy in copies:
        copy.wait()


def last_s(me, place, turned_h, ss, wdown, tails, tail, wgu, slots, cap):
    rows, width = ss[0].shape
    hidden, total = turned_h.shape
    quarter = width // SIDE
    steps = width // 512
    dab = jax.ShapeDtypeStruct((rows, hidden), BF16)
    *down, slots, da, db = pl.pallas_call(
        functools.partial(last_s_kernel, cap),
        in_specs=[SCALARS] * 2 + [FAR] * 10,
        out_specs=[FAR] * 6,
        out_shape=message_outs(hidden, quarter)
        + [jax.ShapeDtypeStruct(slots.shape, BF16), dab, dab],
        input_output_aliases={11: 3},
        scratch_shapes=[
            pltpu.VMEM((hidden, total), BF16),
            pltpu.VMEM((3, total, quarter), BF16),
            pltpu.VMEM((rows, width), BF16),
            pltpu.VMEM((hidden, width), BF16),
            pltpu.VMEM((2, SIDE, cap + 8, hidden), F32),
            pltpu.VMEM((2, rows, hidden), BF16),
            pltpu.VMEM((width, 2 * hidden), BF16),
            pltpu.VMEM((steps, SIDE, cap, 512), BF16),
        ]
        + message_scratch(hidden, quarter)
        + [
            pltpu.SemaphoreType.DMA((4,)),
            pltpu.SemaphoreType.DMA((3, SIDE)),
            pltpu.SemaphoreType.DMA((hidden // 256,)),
            pltpu.SemaphoreType.DMA((steps,)),
            pltpu.SemaphoreType.DMA((2,)),
            pltpu.SemaphoreType.DMA((steps, SIDE)),
        ],
        compiler_params=params(0),
        cost_estimate=cost(1, 1),
        name="last_s",
    )(me, place, turned_h, *ss, wdown, tails, tail, wgu, slots)
    return down, slots, [da, db]


def down_own_kernel(place_ref, *refs):
    turned_ref, ss, out = refs[0], refs[1:5], refs[5]
    out[...] = dot(turned_ref[...], jnp.concatenate([s[...] for s in ss], axis=0))


def down_own(place, turned_h, ss):
    hidden, total = turned_h.shape
    rows, width = ss[0].shape
    quarter = width // SIDE
    return pl.pallas_call(
        down_own_kernel,
        grid_spec=pltpu.PrefetchScalarGridSpec(
            num_scalar_prefetch=1,
            grid=(2,),
            in_specs=[pl.BlockSpec((hidden // 2, total), lambda i, place: (i, 0))]
            + [held((rows, quarter), lambda i, place: (0, place[0]))] * 4,
            out_specs=pl.BlockSpec((hidden // 2, quarter), lambda i, place: (i, 0)),
        ),
        out_shape=jax.ShapeDtypeStruct((hidden, quarter), F32),
        compiler_params=params(1),
        cost_estimate=cost(1, 1),
        name="down_own",
    )(place, turned_h, *ss)


def gate_up_kernel(cap, place_ref, *refs):
    early, late, xs, outs, ds = refs[:2], refs[2:4], refs[4:8], refs[8:11], refs[11:13]
    d_v, late_v, x_v, sent_v, wait_v, out_sems, d_sems, x_sems = refs[13:]
    rows, width = xs[0].shape
    size = width // SIDE
    edge = 3 * cap - 8

    def dab_loads(k):
        first = begun(early[k], d_v.at[k], d_sems.at[0, k])
        return [first, begun(late[k], late_v.at[k], d_sems.at[1, k])]

    def x_loads(k):
        cols = ahead_of(place_ref, AHEAD[k], size)
        at = [pl.ds(i * rows, rows) for i in range(SIDE)]
        return [begun(xs[i].at[:, cols], x_v.at[k, at[i], :], x_sems.at[k, i]) for i in range(SIDE)]

    def filled(k, loads):
        for load in loads:
            load.wait()
        fresh = late_v[k].astype(F32)
        for i in range(SIDE):
            at = slice(i * rows + edge, (i + 1) * rows)
            old = d_v[k, at, :].astype(F32)[:8]
            new = fresh[i * cap : (i + 1) * cap]
            d_v[k, at, :] = jnp.concatenate([old, new], axis=0).astype(BF16)
        return begun(d_v.at[k], ds[k], d_sems.at[2, k])

    first, quarters = dab_loads(0), [x_loads(0)]
    second = dab_loads(1)
    quarters += [x_loads(1), x_loads(2)]
    copies = [filled(0, first)]
    for k in range(3):
        for load in quarters[k]:
            load.wait()
        turned_x = x_v[k].T
        part = dot(turned_x, d_v[0])
        if k == 0:
            copies.append(filled(1, second))
        part = jnp.concatenate([part, dot(turned_x, d_v[1])], axis=1)
        copies += put_halves(k, part, sent_v, wait_v, outs, out_sems)
    for copy in copies:
        copy.wait()


def gate_up_parts(place, early, late, xs, cap):
    rows, width = xs[0].shape
    total, hidden = early[0].shape
    quarter = width // SIDE
    out = jax.ShapeDtypeStruct((total, hidden), BF16)
    *messages, da, db = pl.pallas_call(
        functools.partial(gate_up_kernel, cap),
        in_specs=[SCALARS] + [FAR] * 8,
        out_specs=[FAR] * 5,
        out_shape=message_outs(quarter, 2 * hidden) + [out, out],
        scratch_shapes=[
            pltpu.VMEM((2, total, hidden), BF16),
            pltpu.VMEM((2, *late[0].shape), BF16),
            pltpu.VMEM((3, total, quarter), BF16),
        ]
        + message_scratch(quarter, 2 * hidden)
        + [pltpu.SemaphoreType.DMA((3, 2)), pltpu.SemaphoreType.DMA((3, SIDE))],
        compiler_params=params(0),
        cost_estimate=cost(1, 1),
        name="gate_up_parts",
    )(place, *early, *late, *xs)
    return messages, [da, db]


def gate_up_own_kernel(place_ref, *refs):
    xs, ds, out = refs[:4], refs[4:6], refs[6]
    rows = jnp.concatenate([x[...] for x in xs], axis=0).T
    out[...] = jnp.concatenate([dot(rows, d[...]) for d in ds], axis=1)


def gate_up_own(place, xs, ds):
    rows, width = xs[0].shape
    total, hidden = ds[0].shape
    half = width // SIDE // 2
    return pl.pallas_call(
        gate_up_own_kernel,
        grid_spec=pltpu.PrefetchScalarGridSpec(
            num_scalar_prefetch=1,
            grid=(2,),
            in_specs=[pl.BlockSpec((rows, half), lambda i, place: (0, 2 * place[0] + i))] * 4
            + [held((total, hidden), lambda i, place: (0, 0))] * 2,
            out_specs=pl.BlockSpec((half, 2 * hidden), lambda i, place: (i, 0)),
        ),
        out_shape=jax.ShapeDtypeStruct((2 * half, 2 * hidden), F32),
        compiler_params=params(1),
        cost_estimate=cost(200e9, 10e6),
        name="gate_up_own",
    )(place, *xs, *ds)


def around(first, axis):
    return [first] + [moved_along(first, axis, OFF[b]) for b in range(1, SIDE)]


def spread(outs, axis, work):
    near = [moved_along(outs[j], axis, OFF[j]) for j in (1, 2)]
    done = work(outs[0])
    far, near[0], near[1], *done = lax.optimization_barrier((outs[3], *near, *done))
    return [outs[0], *near, moved_along(far, axis, OFF[3])], done


def ring_first(first_up, first_down, wait):
    return moved_along(first_up, "edata", 1), moved_along(first_down, "edata", -1)


def ring_second(up1, down1, first_up, first_down, wait):
    half = wait.shape[0] // 2
    second_up = (wait[:half].astype(F32) + up1[:half].astype(F32)).astype(BF16)
    second_down = (wait[half:].astype(F32) + down1[half:].astype(F32)).astype(BF16)
    return moved_along(second_up, "edata", 1), moved_along(second_down, "edata", -1)


def ring_own(own, up1, down1):
    half = own.shape[0] // 2
    return own[:half] + down1[:half].astype(F32), own[half:] + up1[half:].astype(F32)


def ring_last(total, up2, down2):
    messages = jnp.concatenate([up2, down2], axis=0).astype(F32)
    return (jnp.concatenate(total, axis=0) + messages).astype(BF16)


def body(hidden_in, out_grad, routes, gates, w_gate_up, w_down):
    tok = hidden_in.shape[1]
    width = hidden_in.shape[2]
    topk = routes.shape[2]
    experts = lax.axis_size("expert")
    cap = min(tok, tok * topk * 9 // (8 * experts))
    wgu, wdown = w_gate_up[0, 0], w_down[0, 0]
    me = lax.axis_index("expert").astype(jnp.int32).reshape(1)
    place = lax.axis_index("edata").astype(jnp.int32).reshape(1)

    xe, ge, tail = prep(routes[0].T, gates[0].T, hidden_in[0], out_grad[0], experts)
    xblocks = around(xe, "x")
    gblocks = around(ge, "z")
    def packed(blocks, scale, name, which):
        steps_to = tuple((OFF[j], 0) if scale else (0, OFF[j]) for j in which)
        return list(pack(me, blocks, width, experts, cap, steps_to, scale, name))

    xnear = packed(xblocks, False, "pack_rows", (1, 2))
    xnear[0], gblocks[0] = lax.optimization_barrier((xnear[0], gblocks[0]))
    gnear = packed(gblocks, True, "pack_scaled", (1, 2))
    xblocks[0], gnear[0] = lax.optimization_barrier((xblocks[0], gnear[0]))
    x0, xfar = packed(xblocks, False, "pack_rows_rest", (0, 3))
    s0, sfar = packed(gblocks, True, "pack_scaled_rest", (0, 3))
    xs, (h0, *factors) = spread([x0, *xnear, xfar], "z", lambda rows: up([rows], wgu)[0])
    ss, (dh0,) = spread([s0, *gnear, sfar], "x", lambda rows: dh_of([rows], wdown))
    hs, tails, dh_tail, slots, early = middle(
        me, wgu, wdown, xs[1:3], ss[1:3], factors, dh0, cap
    )
    turned_h, last_tail, slots, early = last_x(
        me, wgu, xs[3], [h0, *hs], dh_tail, slots, early, cap
    )
    last, slots, turned_h = lax.optimization_barrier((ss[3], slots, turned_h))
    ss = ss[:3] + [last]
    down, rows, late = last_s(me, place, turned_h, ss, wdown, tails, last_tail, wgu, slots, cap)
    down_first = ring_first(*down)
    returned = lax.all_to_all(rows, "expert", split_axis=0, concat_axis=0, tiled=True)
    rows, *late = lax.optimization_barrier((rows, *late))
    gate_up, ds = gate_up_parts(place, early, late, xs, cap)
    gate_up[0], gate_up[1], *down_first = lax.optimization_barrier((gate_up[0], gate_up[1], *down_first))
    gate_up_first = ring_first(*gate_up)
    wait, da, db, turned_h = lax.optimization_barrier((gate_up[2], *ds, turned_h))
    gate_up = [*gate_up[:2], wait]
    own_down = down_own(place, turned_h, ss)
    own_gate_up = gate_up_own(place, xs, [da, db])
    own_down, own_gate_up, *gate_up_first = lax.optimization_barrier(
        (own_down, own_gate_up, *gate_up_first)
    )
    down_second = ring_second(*down_first, *down)
    gate_up_second = ring_second(*gate_up_first, *gate_up)
    returned, own_down, own_gate_up, *firsts = lax.optimization_barrier(
        (returned, own_down, own_gate_up, *down_first, *gate_up_first)
    )
    totals = (*ring_own(own_down, *firsts[:2]), *ring_own(own_gate_up, *firsts[2:]))
    totals = lax.optimization_barrier(totals)
    layer = home(tail, returned.reshape(experts * cap, width), out_grad[0], experts, cap)
    upstream = moved_along(layer, "section", -1)
    down_grad = ring_last(totals[:2], *down_second)
    gate_up_grad = ring_last(totals[2:], *gate_up_second)
    return (upstream[None], gate_up_grad[None, None], down_grad[None, None])


def solution(mesh):
    return jax.shard_map(
        body,
        mesh=mesh,
        in_specs=(
            P("section", ("edata", "expert"), None),
            P("section", ("edata", "expert"), None),
            P("section", ("edata", "expert"), None),
            P("section", ("edata", "expert"), None),
            P("section", "expert", None, None),
            P("section", "expert", None, None),
        ),
        out_specs=(
            P("section", ("edata", "expert"), None),
            P("section", "expert", "edata", None),
            P("section", "expert", None, "edata"),
        ),
        check_vma=False,
    )
```
